512 devices in a mesh: dp: 32 (over z_hi, x, core), tensor: 16 (over z_lo, y).
Axes of the slice: x: 4, y: 8, z: 8 (z_hi: 4, z_lo: 2; z = z_hi * 2 + z_lo), core: 2. Of those that a mesh axis runs over, the one named last changes fastest.
Arguments:
- inputs: bfloat16 [4096, 8192], P(('dp', 'tensor')), may hold values from -24 to 24
- cotangent: bfloat16 [4096, 8192], P('dp', 'tensor'), may hold values from -6 to 6
- weight: bfloat16 [8192, 8192], P('dp', 'tensor'), may hold values from -0.0625 to 0.0625
- left_factor: bfloat16 [8192, 16], replicated, may hold values from -0.0625 to 0.0625
- right_factor: bfloat16 [16, 8192], P(None, 'tensor'), may hold values from -0.0625 to 0.0625
- singular: float32 [16], replicated, may hold values from -6 to 6
- keep_mask: int32 [16], replicated, may hold values 0 or 1
Outputs:
- grad_inputs: bfloat16 [4096, 8192], P(('dp', 'tensor'))
- grad_left: float32 [8192, 16], P(('dp', 'tensor'))
- grad_right: float32 [16, 8192], P(None, 'tensor')
- grad_singular: float32 [16], replicated
The draws below stay inside these ranges and needn't reach their ends.
Inputs may be any that keep to these rules, and one draw needn't show every extreme that they name: `keep_mask`: 1 keeps a singular value, 0 prunes it.
All inputs are finite; a program needn't handle non-finite values.
Results may differ from the reference program's by a relative error of at most 0.0034.
Values may be sent and summed in bfloat16 or wider, within the bound.
No kernel may reach another device: no remote copies, remote signals or barrier semaphores. Data moves between devices by JAX's collectives and lax.ppermute only.
A program may use at most 64 MiB of HBM per device.

```python
import jax
import jax.numpy as jnp

D = 8192
DQ = 8192
R = 16
TOKENS = 4096
N_DP = 32


def with_ends(entries, own_key, low, top_value):
    shape = entries.shape
    place = [jax.random.randint(jax.random.fold_in(own_key, axis), (), 0, shape[axis]) for axis in range(len(shape))]
    entries = entries.at[tuple(place)].set(low)
    longest = shape.index(max(shape))
    place[longest] = (place[longest] + 1) % shape[longest]
    return entries.at[tuple(place)].set(top_value)


def spiked(values, key, source, target, shards_of, factor):
    owner, partner = [(jnp.arange(values.shape[dim]) // (values.shape[dim] // shards_of)).reshape([-1 if axis == dim else 1 for axis in range(values.ndim)]) for dim in (source, target)]
    chosen = jax.random.permutation(key, shards_of)[partner]
    strong = (owner == chosen) | (owner == (partner + shards_of // 2) % shards_of)
    return jnp.where(strong, factor * values, values)


def levels(stream_key, extent, split, smallest, high):
    factor_of, own = 1.0, jax.random.fold_in(stream_key, 6)
    for axis_at, shards_of in split:
        draws = jnp.exp(jax.random.uniform(jax.random.fold_in(own, axis_at), (shards_of,), jnp.float32, smallest / len(split), high / len(split)))
        factor_of = factor_of * jnp.repeat(draws, extent[axis_at] // shards_of).reshape([-1 if axis == axis_at else 1 for axis in range(len(extent))])
    return factor_of


def centred(stream_key, shape, deviation, most, shards=(), held_as=jnp.bfloat16):
    drawn = jax.random.normal(stream_key, shape, jnp.float32) * deviation
    if len(shards) > 0:
        drawn = levels(stream_key, shape, shards, -0.22, 0.18) * drawn
    return jnp.clip(drawn, min=-most, max=most).astype(held_as)


def noise_with(own_key, shape, deviation, limit, cuts, heavy, kind=jnp.bfloat16):
    values = deviation * jax.random.normal(own_key, shape, jnp.float32)
    if cuts:
        values = values * levels(own_key, shape, cuts, -0.22, 0.18)
    return jnp.clip(spiked(values, jax.random.fold_in(own_key, 3), *heavy), -limit, limit).astype(kind)


def setup_inputs(seed: int = 0) -> dict:
    keys = jax.random.split(jax.random.key(seed), 8)
    inputs = noise_with(keys[0], (TOKENS, D), 1.0, 24.0, ((0, 512),), (0, 1, 512, 6.0))
    cotangent = centred(keys[1], (TOKENS, DQ), 1.0, 6.0, ((0, 32), (1, 16)))
    weight = centred(keys[2], (D, DQ), DQ ** -0.5, 0.0625, ((0, 32), (1, 16)))
    left_factor = centred(keys[3], (D, R), D ** -0.5, 0.0625)
    right_factor = centred(keys[4], (R, DQ), DQ ** -0.5, 0.0625, ((1, 16),))
    singular = centred(keys[5], (R,), 1.5, 6.0, (), jnp.float32)
    keep_mask = with_ends((jax.random.randint(keys[6], (R,), 0, 4) < 3).astype(jnp.int32), jax.random.fold_in(keys[6], 1), 0, 1)
    return dict(inputs=inputs, cotangent=cotangent, weight=weight, left_factor=left_factor, right_factor=right_factor, singular=singular, keep_mask=keep_mask)


adapter_scale = 2.0


def reference(inputs, cotangent, weight, left_factor, right_factor, singular, keep_mask):
    coeff = adapter_scale * singular * keep_mask.astype(jnp.float32)
    projected = jnp.dot(inputs, left_factor, preferred_element_type=jnp.float32)
    back_rank = jnp.dot(cotangent, right_factor.T, preferred_element_type=jnp.float32)
    scaled_back = (back_rank * coeff).astype(jnp.bfloat16)
    scaled_fwd = (projected * coeff).astype(jnp.bfloat16)
    base_grad = jnp.dot(cotangent, weight.T, preferred_element_type=jnp.float32)
    grad_inputs = (base_grad + jnp.dot(scaled_back, left_factor.T, preferred_element_type=jnp.float32)).astype(jnp.bfloat16)
    grad_left = jnp.dot(inputs.T, scaled_back, preferred_element_type=jnp.float32) / N_DP
    grad_right = jnp.dot(scaled_fwd.T, cotangent, preferred_element_type=jnp.float32) / N_DP
    grad_singular = adapter_scale * keep_mask.astype(jnp.float32) * jnp.sum(projected * back_rank, axis=0) / N_DP
    return grad_inputs, grad_left, grad_right, grad_singular
```

```python
import jax
import jax.numpy as jnp
from jax import lax
from jax.experimental import pallas as pl
from jax.experimental.pallas import tpu as pltpu
from jax.sharding import Mesh
from jax.sharding import PartitionSpec as P

adapter_scale = 2.0
n_dp = 32
f32 = jnp.float32
bf16 = jnp.bfloat16
in_vmem = pl.BlockSpec(memory_space=pltpu.VMEM)
in_smem = pl.BlockSpec(memory_space=pltpu.SMEM)
unread = pl.BlockSpec(memory_space=pl.ANY)


def dot_t(a, b):
    return lax.dot_general(a, b, (((1,), (1,)), ((), ())), preferred_element_type=f32)


def t_dot(a, b):
    return lax.dot_general(a, b, (((0,), (0,)), ((), ())), preferred_element_type=f32)


def swap(a, axis, count, mask):
    return lax.ppermute(a, axis, [(i, i ^ mask) for i in range(count)])


def call(kernel, out_shape, in_specs, flops, moved):
    return pl.pallas_call(
        kernel,
        out_shape=out_shape,
        in_specs=in_specs,
        out_specs=jax.tree.map(lambda _: in_vmem, out_shape),
        compiler_params=pltpu.CompilerParams(vmem_limit_bytes=32 << 20),
        cost_estimate=pl.CostEstimate(flops=flops, bytes_accessed=moved, transcendentals=0),
    )


def rank_kernel(cot_ref, right_ref, inputs_ref, left_ref, after_ref, out_ref):
    back = dot_t(cot_ref[...], right_ref[...])
    projected = jnp.dot(inputs_ref[...], left_ref[...], preferred_element_type=f32)
    out_ref[...] = jnp.zeros((16, 8, 128), f32)
    out_ref[:, :, 0:16] = back.reshape(16, 8, 16)
    out_ref[:, :, 16:32] = jnp.broadcast_to(projected[None], (16, 8, 16))


def pack_kernel(
    place_ref, sent_ref, rank_ref, coeff_ref, cot_ref, weight_ref, got_ref, inputs_ref, after1, after3,
    x_ref, back_ref, right_ref,
):
    lane = lax.broadcasted_iota(jnp.int32, (1, 128), 1)
    rank = rank_ref[...]
    coeff = coeff_ref[...]
    own = jnp.where(lane < 16, jnp.sum(rank, axis=0), 0.0)
    back = (own * coeff).astype(bf16)
    back_ref[...] = back
    fwd = (jnp.where((lane >= 16) & (lane < 32), rank, 0.0) * coeff).astype(bf16)
    right_ref[...] = t_dot(fwd.reshape(128, 128), cot_ref[...])[16:32]
    projected = pltpu.roll(sent_ref[0], 112, 1)
    singular = jnp.sum(projected * own, axis=0, keepdims=True)
    high = singular.astype(bf16).astype(f32)
    low = singular - high
    wide = lambda a: jnp.broadcast_to(a, (32, 128))
    back32 = back.astype(f32)
    small = jnp.concatenate(
        [
            jnp.concatenate([back32] * 4, axis=0),
            jnp.concatenate([pltpu.roll(back32, 16, 1)] * 4, axis=0),
            wide(pltpu.roll(jnp.broadcast_to(high, (8, 128)), 32, 1)[0:1]),
            wide(pltpu.roll(jnp.broadcast_to(low, (8, 128)), 32, 1)[0:1]),
        ],
        axis=1,
    ).astype(bf16)
    inputs = inputs_ref[...].astype(f32)
    kept = weight_ref[pl.ds(pl.multiple_of(place_ref[1] * 128, 128), 128), :]
    got = got_ref[...]
    for x in range(4):
        x_ref[x, 0:128, :] = kept
        x_ref[x, 128:256, :] = got
        rows = [inputs[:, (h * 4 + x) * 512 : (h * 4 + x + 1) * 512] for h in range(4)]
        x_ref[x, 256:288, :] = jnp.concatenate(rows, axis=0).astype(bf16)
        x_ref[x, 288:320, :] = small


def terms_kernel(place_ref, own_ref, other_ref, c0_ref, c1_ref, c2_ref, c3_ref, right_ref, out_ref, right_out_ref):
    core, z_high = place_ref[0], place_ref[2]
    right_out_ref[...] = right_ref[...]
    cots = (c0_ref, c1_ref, c2_ref, c3_ref)
    parts = [jnp.concatenate([c[half] for c in cots], axis=0) for half in (0, 1)]
    for s, ref in enumerate((own_ref, other_ref)):
        total = dot_t(parts[0], ref[:, 0:128, :].reshape(512, 512))
        total += dot_t(parts[1], ref[:, 128:256, :].reshape(512, 512))
        total = total.astype(bf16).reshape(4, 128, 512)
        for k in range(4):
            out_ref[z_high ^ k, :, s * 512 : (s + 1) * 512] = total[k]
    tok, back, singular = [], [], jnp.zeros((1, 128), f32)
    for ref in (own_ref, other_ref):
        for x in range(4):
            rows = ref[x, 256:288, :]
            tok.append(jnp.where(core == 0, rows[:, :256], rows[:, 256:]))
            back.append(ref[x, 288:320, 0:256])
            line = ref[x, 288:320, 256:512].astype(f32)[0:1]
            singular += line[:, :128] + line[:, 128:]
    tok = jnp.concatenate(tok, axis=0)
    back = jnp.concatenate(back, axis=0)
    group = lax.rem(lax.broadcasted_iota(jnp.int32, (256, 1), 0), 32) // 8
    for h in range(4):
        both = t_dot(tok, jnp.where(group == h, back, jnp.zeros_like(back)))
        a = both[:, :128].reshape(16, 2, 8, 128)[:, 0]
        b = both[:, 128:].reshape(16, 2, 8, 128)[:, 1]
        z = (a + b + singular).reshape(128, 128)
        high = z.astype(bf16).astype(f32)
        out_ref[h, :, 1024:1152] = (high + pltpu.roll(z - high, 64, 1)).astype(bf16)


def body(inputs, cotangent, weight, left_factor, right_factor, singular, keep_mask):
    core = lax.axis_index("c")
    z_low = lax.axis_index("zl")
    z_high = lax.axis_index("zh")
    place = jnp.stack([core, z_low, z_high]).astype(jnp.int32)
    shape = jax.ShapeDtypeStruct
    keep_float = keep_mask.astype(f32)
    coeff = adapter_scale * singular * keep_float

    given = lax.dynamic_index_in_dim(weight.reshape(2, 128, 512), 1 - z_low, 0, keepdims=False)
    got = swap(given, "zl", 2, 1)

    cot_other = swap(cotangent, "zl", 2, 1)
    cot_pair = jnp.stack([cotangent, cot_other])
    cots = [cot_pair] + [swap(cot_pair, "zh", 4, k) for k in (1, 2, 3)]

    rank_out = call(
        rank_kernel, shape((16, 8, 128), f32), [in_vmem] * 4 + [unread], 6 << 20, 1 << 20
    )(cotangent, right_factor, inputs, left_factor, cot_other)
    rank_in = lax.all_to_all(rank_out, ("zl", "y"), 0, 0)

    coeff_lanes = jnp.pad(jnp.concatenate([coeff, coeff]), (0, 96)).reshape(1, 128)
    x_out, scaled_back, right_part = call(
        pack_kernel,
        (shape((4, 320, 512), bf16), shape((8, 128), bf16), shape((16, 512), f32)),
        [in_smem] + [in_vmem] * 7 + [unread] * 2,
        16 << 20,
        3 << 20,
    )(place, rank_out, rank_in, coeff_lanes, cotangent, weight, got, inputs, cots[1], cots[3])
    x_in = lax.all_to_all(x_out, "x", 0, 0)
    right_part = right_part + swap(right_part, "zh", 4, 1)
    right_part = right_part + swap(right_part, "zh", 4, 2)

    out, right_part = call(
        terms_kernel,
        (shape((4, 128, 1152), bf16), shape((16, 512), f32)),
        [in_smem] + [in_vmem] * 7,
        1 << 30,
        5 << 20,
    )(place, x_in, swap(x_in, "c", 2, 1), *cots, right_part)
    back = lax.all_to_all(out.reshape(64, 8, 1152), ("zh", "zl", "y"), 0, 0)
    right_part = right_part + swap(right_part, "c", 2, 1)
    right_part = right_part + swap(right_part, "x", 4, 1)
    right_sum = right_part + swap(right_part, "x", 4, 2)

    summed = jnp.sum(back[:, :, :1024].reshape(4, 2, 8, 8, 1024).astype(f32), axis=2)
    summed = summed.reshape(4, 2, 8, 2, 4, 128)
    summed = jnp.where(core == 0, summed, summed[:, :, :, ::-1])
    base_grad = summed.transpose(2, 0, 4, 3, 1, 5).reshape(8, 8192)
    grad_inputs = (base_grad + dot_t(scaled_back[:, :16], left_factor)).astype(bf16)
    tail = jnp.sum(back[:, :, 1024:].astype(f32), axis=0)
    tail = tail[:, :64] + tail[:, 64:]
    grad_left = jnp.concatenate([tail[:, :16], tail[:, 16:32]], axis=0) / n_dp
    grad_right = right_sum / n_dp
    grad_singular = adapter_scale * keep_float * tail[0, 32:48] / n_dp
    return (grad_inputs, grad_left, grad_right, grad_singular)


def solution(mesh):
    fine = Mesh(mesh.devices.reshape(4, 4, 2, 2, 8), ("zh", "x", "c", "zl", "y"))
    dp = ("zh", "x", "c")
    tensor = ("zl", "y")
    in_specs = (
        P(dp + tensor, None),
        P(dp, tensor),
        P(dp, tensor),
        P(),
        P(None, tensor),
        P(),
        P(),
    )
    out_specs = (P(dp + tensor, None), P(dp + tensor, None), P(None, tensor), P())
    return jax.shard_map(body, mesh=fine, in_specs=in_specs, out_specs=out_specs, check_vma=False)
```

```python
import jax
import jax.numpy as jnp
from jax import lax
from jax.experimental import pallas as pl
from jax.experimental.pallas import tpu as pltpu
from jax.sharding import Mesh
from jax.sharding import PartitionSpec as P

adapter_scale = 2.0
n_dp = 32
f32 = jnp.float32
bf16 = jnp.bfloat16
in_vmem = pl.BlockSpec(memory_space=pltpu.VMEM)
in_smem = pl.BlockSpec(memory_space=pltpu.SMEM)
unread = pl.BlockSpec(memory_space=pl.ANY)


def dot_t(a, b):
    return lax.dot_general(a, b, (((1,), (1,)), ((), ())), preferred_element_type=f32)


def t_dot(a, b):
    return lax.dot_general(a, b, (((0,), (0,)), ((), ())), preferred_element_type=f32)


def swap(a, axis, count, mask):
    return lax.ppermute(a, axis, [(i, i ^ mask) for i in range(count)])


def call(kernel, out_shape, in_specs, flops, moved):
    return pl.pallas_call(
        kernel,
        out_shape=out_shape,
        in_specs=in_specs,
        out_specs=jax.tree.map(lambda _: in_vmem, out_shape),
        compiler_params=pltpu.CompilerParams(vmem_limit_bytes=32 << 20),
        cost_estimate=pl.CostEstimate(flops=flops, bytes_accessed=moved, transcendentals=0),
    )


def after(a, *others):
    return pl.pallas_call(
        lambda *refs: None,
        out_shape=jax.ShapeDtypeStruct(a.shape, a.dtype),
        in_specs=[unread] * (1 + len(others)),
        out_specs=unread,
        input_output_aliases={0: 0},
    )(a, *others)


def rank_kernel(cot_ref, right_ref, projected_ref, after_ref, out_ref):
    back = dot_t(cot_ref[...], right_ref[...])
    projected = projected_ref[...]
    out_ref[...] = jnp.zeros((16, 8, 128), f32)
    out_ref[:, :, 0:16] = back.reshape(16, 8, 16)
    out_ref[:, :, 16:32] = jnp.broadcast_to(projected[None], (16, 8, 16))


def pack_kernel(
    place_ref, sent_ref, rank_ref, coeff_ref, cot_ref, weight_ref, got_ref, inputs_ref, after1, after3,
    x_ref, back_ref, right_ref,
):
    lane = lax.broadcasted_iota(jnp.int32, (1, 128), 1)
    rank = rank_ref[...]
    coeff = coeff_ref[...]
    own = jnp.where(lane < 16, jnp.sum(rank, axis=0), 0.0)
    back = (own * coeff).astype(bf16)
    back_ref[...] = back
    fwd = (jnp.where((lane >= 16) & (lane < 32), rank, 0.0) * coeff).astype(bf16)
    right_ref[...] = t_dot(fwd.reshape(128, 128), cot_ref[...])[16:32]
    projected = pltpu.roll(sent_ref[0], 112, 1)
    singular = jnp.sum(projected * own, axis=0, keepdims=True)
    high = singular.astype(bf16).astype(f32)
    low = singular - high
    wide = lambda a: jnp.broadcast_to(a, (32, 128))
    back32 = back.astype(f32)
    small = jnp.concatenate(
        [
            jnp.concatenate([back32] * 4, axis=0),
            jnp.concatenate([pltpu.roll(back32, 16, 1)] * 4, axis=0),
            wide(pltpu.roll(jnp.broadcast_to(high, (8, 128)), 32, 1)[0:1]),
            wide(pltpu.roll(jnp.broadcast_to(low, (8, 128)), 32, 1)[0:1]),
        ],
        axis=1,
    ).astype(bf16)
    inputs = inputs_ref[...].astype(f32)
    kept = weight_ref[pl.ds(pl.multiple_of(place_ref[1] * 128, 128), 128), :]
    got = got_ref[...]
    for x in range(4):
        x_ref[x, 0:128, :] = kept
        x_ref[x, 128:256, :] = got
        rows = [inputs[:, (h * 4 + x) * 512 : (h * 4 + x + 1) * 512] for h in range(4)]
        x_ref[x, 256:288, :] = jnp.concatenate(rows, axis=0).astype(bf16)
        x_ref[x, 288:320, :] = small


def terms_kernel(place_ref, own_ref, other_ref, c0_ref, c1_ref, c2_ref, c3_ref, right_ref, out_ref, right_out_ref):
    core, z_high = place_ref[0], place_ref[2]
    right_out_ref[...] = right_ref[...]
    cots = (c0_ref, c1_ref, c2_ref, c3_ref)
    parts = [jnp.concatenate([c[half] for c in cots], axis=0) for half in (0, 1)]
    for s, ref in enumerate((own_ref, other_ref)):
        total = dot_t(parts[0], ref[:, 0:128, :].reshape(512, 512))
        total += dot_t(parts[1], ref[:, 128:256, :].reshape(512, 512))
        total = total.astype(bf16).reshape(4, 128, 512)
        for k in range(4):
            out_ref[z_high ^ k, :, s * 512 : (s + 1) * 512] = total[k]
    tok, back, singular = [], [], jnp.zeros((1, 128), f32)
    for ref in (own_ref, other_ref):
        for x in range(4):
            rows = ref[x, 256:288, :]
            tok.append(jnp.where(core == 0, rows[:, :256], rows[:, 256:]))
            back.append(ref[x, 288:320, 0:256])
            line = ref[x, 288:320, 256:512].astype(f32)[0:1]
            singular += line[:, :128] + line[:, 128:]
    tok = jnp.concatenate(tok, axis=0)
    back = jnp.concatenate(back, axis=0)
    group = lax.rem(lax.broadcasted_iota(jnp.int32, (256, 1), 0), 32) // 8
    for h in range(4):
        both = t_dot(tok, jnp.where(group == h, back, jnp.zeros_like(back)))
        a = both[:, :128].reshape(16, 2, 8, 128)[:, 0]
        b = both[:, 128:].reshape(16, 2, 8, 128)[:, 1]
        z = (a + b + singular).reshape(128, 128)
        high = z.astype(bf16).astype(f32)
        out_ref[h, :, 1024:1152] = (high + pltpu.roll(z - high, 64, 1)).astype(bf16)


def body(inputs, cotangent, weight, left_factor, right_factor, singular, keep_mask):
    core = lax.axis_index("c")
    z_low = lax.axis_index("zl")
    z_high = lax.axis_index("zh")
    place = jnp.stack([core, z_low, z_high]).astype(jnp.int32)
    shape = jax.ShapeDtypeStruct
    keep_float = keep_mask.astype(f32)
    coeff = adapter_scale * singular * keep_float

    given = lax.dynamic_index_in_dim(weight.reshape(2, 128, 512), 1 - z_low, 0, keepdims=False)
    got = swap(given, "zl", 2, 1)

    cot_other = swap(cotangent, "zl", 2, 1)
    cot_pair = jnp.stack([cotangent, cot_other])
    cots = [cot_pair] + [swap(cot_pair, "zh", 4, k) for k in (1, 2, 3)]

    own_projected = jnp.dot(inputs, left_factor, preferred_element_type=f32)
    rank_out = call(
        rank_kernel, shape((16, 8, 128), f32), [in_vmem] * 3 + [unread], 6 << 20, 1 << 20
    )(cotangent, right_factor, own_projected, cot_other)
    rank_in = lax.all_to_all(rank_out, ("zl", "y"), 0, 0)

    coeff_lanes = jnp.pad(jnp.concatenate([coeff, coeff]), (0, 96)).reshape(1, 128)
    x_out, scaled_back, right_part = call(
        pack_kernel,
        (shape((4, 320, 512), bf16), shape((8, 128), bf16), shape((16, 512), f32)),
        [in_smem] + [in_vmem] * 7 + [unread] * 2,
        16 << 20,
        3 << 20,
    )(place, rank_out, rank_in, coeff_lanes, cotangent, weight, got, inputs, cots[1], cots[3])
    x_in = lax.all_to_all(x_out, "x", 0, 0)
    right_part = right_part + swap(right_part, "zh", 4, 1)
    right_part = right_part + swap(right_part, "zh", 4, 2)
    x_in = after(x_in, cots[2], right_part)

    out, right_part = call(
        terms_kernel,
        (shape((4, 128, 1152), bf16), shape((16, 512), f32)),
        [in_smem] + [in_vmem] * 7,
        1 << 30,
        5 << 20,
    )(place, x_in, swap(x_in, "c", 2, 1), *cots, right_part)
    back = lax.all_to_all(out.reshape(64, 8, 1152), ("zh", "zl", "y"), 0, 0)
    right_part = right_part + swap(right_part, "c", 2, 1)
    right_part = right_part + swap(right_part, "x", 4, 1)
    right_sum = right_part + swap(right_part, "x", 4, 2)

    summed = jnp.sum(back[:, :, :1024].reshape(4, 2, 8, 8, 1024).astype(f32), axis=2)
    summed = summed.reshape(4, 2, 8, 2, 4, 128)
    summed = jnp.where(core == 0, summed, summed[:, :, :, ::-1])
    base_grad = summed.transpose(2, 0, 4, 3, 1, 5).reshape(8, 8192)
    grad_inputs = (base_grad + dot_t(scaled_back[:, :16], left_factor)).astype(bf16)
    tail = jnp.sum(back[:, :, 1024:].astype(f32), axis=0)
    tail = tail[:, :64] + tail[:, 64:]
    grad_left = jnp.concatenate([tail[:, :16], tail[:, 16:32]], axis=0) / n_dp
    grad_right = right_sum / n_dp
    grad_singular = adapter_scale * keep_float * tail[0, 32:48] / n_dp
    return (grad_inputs, grad_left, grad_right, grad_singular)


def solution(mesh):
    fine = Mesh(mesh.devices.reshape(4, 4, 2, 2, 8), ("zh", "x", "c", "zl", "y"))
    dp = ("zh", "x", "c")
    tensor = ("zl", "y")
    in_specs = (
        P(dp + tensor, None),
        P(dp, tensor),
        P(dp, tensor),
        P(),
        P(None, tensor),
        P(),
        P(),
    )
    out_specs = (P(dp + tensor, None), P(dp + tensor, None), P(None, tensor), P())
    return jax.shard_map(body, mesh=fine, in_specs=in_specs, out_specs=out_specs, check_vma=False)
```

```python
import jax
import jax.numpy as jnp
from jax import lax
from jax.experimental import pallas as pl
from jax.experimental.pallas import tpu as pltpu
from jax.sharding import Mesh
from jax.sharding import PartitionSpec as P

adapter_scale = 2.0
n_dp = 32
f32 = jnp.float32
bf16 = jnp.bfloat16
in_vmem = pl.BlockSpec(memory_space=pltpu.VMEM)
in_smem = pl.BlockSpec(memory_space=pltpu.SMEM)
unread = pl.BlockSpec(memory_space=pl.ANY)


def dot_t(a, b):
    return lax.dot_general(a, b, (((1,), (1,)), ((), ())), preferred_element_type=f32)


def t_dot(a, b):
    return lax.dot_general(a, b, (((0,), (0,)), ((), ())), preferred_element_type=f32)


def swap(a, axis, count, mask):
    return lax.ppermute(a, axis, [(i, i ^ mask) for i in range(count)])


def call(kernel, out_shape, in_specs, flops, moved):
    return pl.pallas_call(
        kernel,
        out_shape=out_shape,
        in_specs=in_specs,
        out_specs=jax.tree.map(lambda _: in_vmem, out_shape),
        compiler_params=pltpu.CompilerParams(vmem_limit_bytes=32 << 20),
        cost_estimate=pl.CostEstimate(flops=flops, bytes_accessed=moved, transcendentals=0),
    )


def after(a, *others):
    return pl.pallas_call(
        lambda *refs: None,
        out_shape=jax.ShapeDtypeStruct(a.shape, a.dtype),
        in_specs=[unread] * (1 + len(others)),
        out_specs=unread,
        input_output_aliases={0: 0},
    )(a, *others)


def rank_kernel(cot_ref, right_ref, projected_ref, out_ref):
    back = dot_t(cot_ref[...], right_ref[...])
    projected = projected_ref[...]
    out_ref[...] = jnp.zeros((16, 8, 128), f32)
    out_ref[:, :, 0:16] = back.reshape(16, 8, 16)
    out_ref[:, :, 16:32] = jnp.broadcast_to(projected[None], (16, 8, 16))


def pack_kernel(
    place_ref, sent_ref, rank_ref, coeff_ref, cot_ref, weight_ref, got_ref, inputs_ref, after1, after3,
    x_ref, back_ref,
):
    lane = lax.broadcasted_iota(jnp.int32, (1, 128), 1)
    rank = rank_ref[...]
    coeff = coeff_ref[...]
    own = jnp.where(lane < 16, jnp.sum(rank, axis=0), 0.0)
    back = (own * coeff).astype(bf16)
    back_ref[...] = back
    fwd = (jnp.where((lane >= 16) & (lane < 32), rank, 0.0) * coeff).astype(bf16)
    right = t_dot(fwd.reshape(128, 128), cot_ref[...])[16:32]
    right_high = right.astype(bf16)
    right_low = (right - right_high.astype(f32)).astype(bf16)
    projected = pltpu.roll(sent_ref[0], 112, 1)
    singular = jnp.sum(projected * own, axis=0, keepdims=True)
    high = singular.astype(bf16).astype(f32)
    low = singular - high
    wide = lambda a: jnp.broadcast_to(a, (32, 128))
    back32 = back.astype(f32)
    small = jnp.concatenate(
        [
            jnp.concatenate([back32] * 4, axis=0),
            jnp.concatenate([pltpu.roll(back32, 16, 1)] * 4, axis=0),
            wide(pltpu.roll(jnp.broadcast_to(high, (8, 128)), 32, 1)[0:1]),
            wide(pltpu.roll(jnp.broadcast_to(low, (8, 128)), 32, 1)[0:1]),
        ],
        axis=1,
    ).astype(bf16)
    inputs = inputs_ref[...].astype(f32)
    kept = weight_ref[pl.ds(pl.multiple_of(place_ref[1] * 128, 128), 128), :]
    got = got_ref[...]
    for x in range(4):
        x_ref[x, 0:128, :] = kept
        x_ref[x, 128:256, :] = got
        rows = [inputs[:, (h * 4 + x) * 512 : (h * 4 + x + 1) * 512] for h in range(4)]
        x_ref[x, 256:288, :] = jnp.concatenate(rows, axis=0).astype(bf16)
        x_ref[x, 288:320, :] = small
        x_ref[x, 320:336, :] = right_high
        x_ref[x, 336:352, :] = right_low


def products(parts, ref):
    total = dot_t(parts[0], ref[:, 0:128, :].reshape(512, 512))
    total += dot_t(parts[1], ref[:, 128:256, :].reshape(512, 512))
    return total.astype(bf16).reshape(4, 128, 512)


def stacked(cots):
    return [jnp.concatenate([c[half] for c in cots], axis=0) for half in (0, 1)]


def own_kernel(own_ref, c0_ref, c1_ref, c2_ref, c3_ref, out_ref):
    out_ref[...] = products(stacked((c0_ref, c1_ref, c2_ref, c3_ref)), own_ref)


def other_kernel(
    place_ref, done_ref, own_ref, other_ref, c0_ref, c1_ref, c2_ref, c3_ref, out_ref, right_ref
):
    core, z_high = place_ref[0], place_ref[2]
    total = products(stacked((c0_ref, c1_ref, c2_ref, c3_ref)), other_ref)
    for k in range(4):
        out_ref[z_high ^ k, :, 0:512] = done_ref[k]
        out_ref[z_high ^ k, :, 512:1024] = total[k]
    right = jnp.zeros((16, 512), f32)
    for ref in (own_ref, other_ref):
        for x in range(4):
            right += ref[x, 320:336, :].astype(f32) + ref[x, 336:352, :].astype(f32)
    right_ref[...] = right
    tok, back, singular = [], [], jnp.zeros((1, 128), f32)
    for ref in (own_ref, other_ref):
        for x in range(4):
            rows = ref[x, 256:288, :]
            tok.append(jnp.where(core == 0, rows[:, :256], rows[:, 256:]))
            back.append(ref[x, 288:320, 0:256])
            line = ref[x, 288:320, 256:512].astype(f32)[0:1]
            singular += line[:, :128] + line[:, 128:]
    tok = jnp.concatenate(tok, axis=0)
    back = jnp.concatenate(back, axis=0)
    group = lax.rem(lax.broadcasted_iota(jnp.int32, (256, 1), 0), 32) // 8
    for h in range(4):
        both = t_dot(tok, jnp.where(group == h, back, jnp.zeros_like(back)))
        a = both[:, :128].reshape(16, 2, 8, 128)[:, 0]
        b = both[:, 128:].reshape(16, 2, 8, 128)[:, 1]
        z = (a + b + singular).reshape(128, 128)
        high = z.astype(bf16).astype(f32)
        out_ref[h, :, 1024:1152] = (high + pltpu.roll(z - high, 64, 1)).astype(bf16)


def body(inputs, cotangent, weight, left_factor, right_factor, singular, keep_mask):
    core = lax.axis_index("c")
    z_low = lax.axis_index("zl")
    z_high = lax.axis_index("zh")
    place = jnp.stack([core, z_low, z_high]).astype(jnp.int32)
    shape = jax.ShapeDtypeStruct
    keep_float = keep_mask.astype(f32)
    coeff = adapter_scale * singular * keep_float

    given = lax.dynamic_index_in_dim(weight.reshape(2, 128, 512), 1 - z_low, 0, keepdims=False)
    got = swap(given, "zl", 2, 1)

    cot_other = swap(cotangent, "zl", 2, 1)
    cot_pair = jnp.stack([cotangent, cot_other])
    cots = [cot_pair] + [swap(cot_pair, "zh", 4, k) for k in (1, 2, 3)]

    own_projected = jnp.dot(inputs, left_factor, preferred_element_type=f32)
    rank_out = call(
        rank_kernel, shape((16, 8, 128), f32), [in_vmem] * 3, 6 << 20, 1 << 20
    )(cotangent, right_factor, own_projected)
    rank_in = lax.all_to_all(rank_out, ("zl", "y"), 0, 0)

    coeff_lanes = jnp.pad(jnp.concatenate([coeff, coeff]), (0, 96)).reshape(1, 128)
    x_out, scaled_back = call(
        pack_kernel,
        (shape((4, 352, 512), bf16), shape((8, 128), bf16)),
        [in_smem] + [in_vmem] * 7 + [unread] * 2,
        16 << 20,
        3 << 20,
    )(place, rank_out, rank_in, coeff_lanes, cotangent, weight, got, inputs, cots[1], cots[3])
    x_in = lax.all_to_all(x_out, "x", 0, 0)
    x_in = after(x_in, cots[2])
    x_other = swap(x_in, "c", 2, 1)

    done = call(own_kernel, shape((4, 128, 512), bf16), [in_vmem] * 5, 1 << 29, 3 << 20)(x_in, *cots)
    out, right_part = call(
        other_kernel,
        (shape((4, 128, 1152), bf16), shape((16, 512), f32)),
        [in_smem] + [in_vmem] * 7,
        1 << 29,
        5 << 20,
    )(place, done, x_in, x_other, *cots)
    back = lax.all_to_all(out.reshape(64, 8, 1152), ("zh", "zl", "y"), 0, 0)
    right_sum = right_part + sum(swap(right_part, "zh", 4, k) for k in (1, 2, 3))

    summed = jnp.sum(back[:, :, :1024].reshape(4, 2, 8, 8, 1024).astype(f32), axis=2)
    summed = summed.reshape(4, 2, 8, 2, 4, 128)
    summed = jnp.where(core == 0, summed, summed[:, :, :, ::-1])
    base_grad = summed.transpose(2, 0, 4, 3, 1, 5).reshape(8, 8192)
    grad_inputs = (base_grad + dot_t(scaled_back[:, :16], left_factor)).astype(bf16)
    tail = jnp.sum(back[:, :, 1024:].astype(f32), axis=0)
    tail = tail[:, :64] + tail[:, 64:]
    grad_left = jnp.concatenate([tail[:, :16], tail[:, 16:32]], axis=0) / n_dp
    grad_right = right_sum / n_dp
    grad_singular = adapter_scale * keep_float * tail[0, 32:48] / n_dp
    return (grad_inputs, grad_left, grad_right, grad_singular)


def solution(mesh):
    fine = Mesh(mesh.devices.reshape(4, 4, 2, 2, 8), ("zh", "x", "c", "zl", "y"))
    dp = ("zh", "x", "c")
    tensor = ("zl", "y")
    in_specs = (
        P(dp + tensor, None),
        P(dp, tensor),
        P(dp, tensor),
        P(),
        P(None, tensor),
        P(),
        P(),
    )
    out_specs = (P(dp + tensor, None), P(dp + tensor, None), P(None, tensor), P())
    return jax.shard_map(body, mesh=fine, in_specs=in_specs, out_specs=out_specs, check_vma=False)
```

```python
import jax
import jax.numpy as jnp
from jax import lax
from jax.experimental import pallas as pl
from jax.experimental.pallas import tpu as pltpu
from jax.sharding import Mesh
from jax.sharding import PartitionSpec as P

adapter_scale = 2.0
n_dp = 32
f32 = jnp.float32
bf16 = jnp.bfloat16
in_vmem = pl.BlockSpec(memory_space=pltpu.VMEM)
in_smem = pl.BlockSpec(memory_space=pltpu.SMEM)
anywhere = pl.BlockSpec(memory_space=pl.ANY)


def dot_t(a, b):
    return lax.dot_general(a, b, (((1,), (1,)), ((), ())), preferred_element_type=f32)


def t_dot(a, b):
    return lax.dot_general(a, b, (((0,), (0,)), ((), ())), preferred_element_type=f32)


def swap(a, axis, count, mask):
    return lax.ppermute(a, axis, [(i, i ^ mask) for i in range(count)])


def call(kernel, out_shape, in_specs, flops, moved, out_specs=None, scratch=()):
    return pl.pallas_call(
        kernel,
        out_shape=out_shape,
        in_specs=in_specs,
        out_specs=out_specs or jax.tree.map(lambda _: in_vmem, out_shape),
        scratch_shapes=scratch,
        compiler_params=pltpu.CompilerParams(vmem_limit_bytes=32 << 20),
        cost_estimate=pl.CostEstimate(flops=flops, bytes_accessed=moved, transcendentals=0),
    )


def after(a, *others):
    return pl.pallas_call(
        lambda *refs: None,
        out_shape=jax.ShapeDtypeStruct(a.shape, a.dtype),
        in_specs=[in_vmem] * (1 + len(others)),
        out_specs=in_vmem,
        input_output_aliases={0: 0},
        compiler_params=pltpu.CompilerParams(vmem_limit_bytes=32 << 20),
    )(a, *others)


def rank_kernel(cot_any, right_any, projected_ref, out_ref, cot_ref, right_ref, sems):
    first = pltpu.make_async_copy(cot_any, cot_ref, sems.at[0])
    second = pltpu.make_async_copy(right_any, right_ref, sems.at[1])
    first.start()
    second.start()
    first.wait()
    second.wait()
    back = dot_t(cot_ref[...], right_ref[...])
    projected = projected_ref[...]
    out_ref[...] = jnp.zeros((16, 8, 128), f32)
    out_ref[:, :, 0:16] = back.reshape(16, 8, 16)
    out_ref[:, :, 16:32] = jnp.broadcast_to(projected[None], (16, 8, 16))


def pack_kernel(
    place_ref, sent_ref, rank_ref, coeff_ref, cot_ref, weight_ref, got_ref, inputs_ref, after1, after2, after3,
    x_any, back_ref, x_ref, sems,
):
    lane = lax.broadcasted_iota(jnp.int32, (1, 128), 1)
    rank = rank_ref[...]
    coeff = coeff_ref[...]
    own = jnp.where(lane < 16, jnp.sum(rank, axis=0), 0.0)
    back = (own * coeff).astype(bf16)
    back_ref[...] = back
    fwd = (jnp.where((lane >= 16) & (lane < 32), rank, 0.0) * coeff).astype(bf16)
    right = t_dot(fwd.reshape(128, 128), cot_ref[...])[16:32]
    right_high = right.astype(bf16)
    right_low = (right - right_high.astype(f32)).astype(bf16)
    projected = pltpu.roll(sent_ref[0], 112, 1)
    singular = jnp.sum(projected * own, axis=0, keepdims=True)
    high = singular.astype(bf16).astype(f32)
    low = singular - high
    wide = lambda a: jnp.broadcast_to(a, (32, 128))
    back32 = back.astype(f32)
    small = jnp.concatenate(
        [
            jnp.concatenate([back32] * 4, axis=0),
            jnp.concatenate([pltpu.roll(back32, 16, 1)] * 4, axis=0),
            wide(pltpu.roll(jnp.broadcast_to(high, (8, 128)), 32, 1)[0:1]),
            wide(pltpu.roll(jnp.broadcast_to(low, (8, 128)), 32, 1)[0:1]),
        ],
        axis=1,
    ).astype(bf16)
    inputs = inputs_ref[...].astype(f32)
    kept = weight_ref[pl.ds(pl.multiple_of(place_ref[1] * 128, 128), 128), :]
    got = got_ref[...]
    for x in range(4):
        x_ref[x, 0:128, :] = kept
        x_ref[x, 128:256, :] = got
        rows = [inputs[:, (h * 4 + x) * 512 : (h * 4 + x + 1) * 512] for h in range(4)]
        x_ref[x, 256:288, :] = jnp.concatenate(rows, axis=0).astype(bf16)
        x_ref[x, 288:320, :] = small
        x_ref[x, 320:336, :] = right_high
        x_ref[x, 336:352, :] = right_low
        pltpu.make_async_copy(x_ref.at[x], x_any.at[x], sems.at[x]).start()
    for x in range(4):
        pltpu.make_async_copy(x_ref.at[x], x_any.at[x], sems.at[x]).wait()


def products(parts, ref):
    total = dot_t(parts[0], ref[:, 0:128, :].reshape(512, 512))
    total += dot_t(parts[1], ref[:, 128:256, :].reshape(512, 512))
    return total.astype(bf16).reshape(4, 128, 512)


def own_kernel(own_ref, near_ref, far_ref, out_ref):
    out_ref[...] = products((near_ref[...].reshape(512, 512), far_ref[...].reshape(512, 512)), own_ref)


def other_kernel(place_ref, done_ref, own_ref, other_ref, near_ref, far_ref, out_ref, right_ref):
    core, z_high = place_ref[0], place_ref[2]
    total = products((near_ref[...].reshape(512, 512), far_ref[...].reshape(512, 512)), other_ref)
    for k in range(4):
        out_ref[z_high ^ k, :, 0:512] = done_ref[k]
        out_ref[z_high ^ k, :, 512:1024] = total[k]
    right = jnp.zeros((16, 512), f32)
    for ref in (own_ref, other_ref):
        for x in range(4):
            right += ref[x, 320:336, :].astype(f32) + ref[x, 336:352, :].astype(f32)
    right_ref[...] = right
    tok, back, singular = [], [], jnp.zeros((1, 128), f32)
    for ref in (own_ref, other_ref):
        for x in range(4):
            rows = ref[x, 256:288, :]
            tok.append(jnp.where(core == 0, rows[:, :256], rows[:, 256:]))
            back.append(ref[x, 288:320, 0:256])
            line = ref[x, 288:320, 256:512].astype(f32)[0:1]
            singular += line[:, :128] + line[:, 128:]
    tok = jnp.concatenate(tok, axis=0)
    back = jnp.concatenate(back, axis=0)
    group = lax.rem(lax.broadcasted_iota(jnp.int32, (256, 1), 0), 32) // 8
    for h in range(4):
        both = t_dot(tok, jnp.where(group == h, back, jnp.zeros_like(back)))
        a = both[:, :128].reshape(16, 2, 8, 128)[:, 0]
        b = both[:, 128:].reshape(16, 2, 8, 128)[:, 1]
        z = (a + b + singular).reshape(128, 128)
        high = z.astype(bf16).astype(f32)
        out_ref[h, :, 1024:1152] = (high + pltpu.roll(z - high, 64, 1)).astype(bf16)


def body(inputs, cotangent, weight, left_factor, right_factor, singular, keep_mask):
    core = lax.axis_index("c")
    z_low = lax.axis_index("zl")
    z_high = lax.axis_index("zh")
    place = jnp.stack([core, z_low, z_high]).astype(jnp.int32)
    shape = jax.ShapeDtypeStruct
    keep_float = keep_mask.astype(f32)
    coeff = adapter_scale * singular * keep_float

    given = lax.dynamic_index_in_dim(weight.reshape(2, 128, 512), 1 - z_low, 0, keepdims=False)
    got = swap(given, "zl", 2, 1)

    cots = [cotangent] + [swap(cotangent, "zh", 4, k) for k in (1, 2, 3)]
    near = jnp.stack(cots)
    far = swap(near, "zl", 2, 1)

    own_projected = jnp.dot(inputs, left_factor, preferred_element_type=f32)
    rank_out = call(
        rank_kernel, shape((16, 8, 128), f32), [anywhere] * 2 + [in_vmem], 6 << 20, 1 << 20,
        scratch=[pltpu.VMEM((128, 512), bf16), pltpu.VMEM((16, 512), bf16), pltpu.SemaphoreType.DMA((2,))],
    )(cotangent, right_factor, own_projected)
    rank_in = lax.all_to_all(rank_out, ("zl", "y"), 0, 0)

    coeff_lanes = jnp.pad(jnp.concatenate([coeff, coeff]), (0, 96)).reshape(1, 128)
    x_out, scaled_back = call(
        pack_kernel,
        (shape((4, 352, 512), bf16), shape((8, 128), bf16)),
        [in_smem] + [in_vmem] * 7 + [anywhere] * 3,
        16 << 20,
        3 << 20,
        out_specs=(anywhere, in_vmem),
        scratch=[pltpu.VMEM((4, 352, 512), bf16), pltpu.SemaphoreType.DMA((4,))],
    )(place, rank_out, rank_in, coeff_lanes, cotangent, weight, got, inputs, *cots[1:])
    x_in = lax.all_to_all(x_out, "x", 0, 0)
    x_in = after(x_in, far)
    x_other = swap(x_in, "c", 2, 1)

    done = call(own_kernel, shape((4, 128, 512), bf16), [in_vmem] * 3, 1 << 29, 3 << 20)(x_in, near, far)
    out, right_part = call(
        other_kernel,
        (shape((4, 128, 1152), bf16), shape((16, 512), f32)),
        [in_smem] + [in_vmem] * 5,
        1 << 29,
        5 << 20,
    )(place, done, x_in, x_other, near, far)
    back = lax.all_to_all(out.reshape(64, 8, 1152), ("zh", "zl", "y"), 0, 0)
    right_sum = right_part + sum(swap(right_part, "zh", 4, k) for k in (1, 2, 3))

    summed = jnp.sum(back[:, :, :1024].reshape(4, 2, 8, 8, 1024).astype(f32), axis=2)
    summed = summed.reshape(4, 2, 8, 2, 4, 128)
    summed = jnp.where(core == 0, summed, summed[:, :, :, ::-1])
    base_grad = summed.transpose(2, 0, 4, 3, 1, 5).reshape(8, 8192)
    grad_inputs = (base_grad + dot_t(scaled_back[:, :16], left_factor)).astype(bf16)
    tail = jnp.sum(back[:, :, 1024:].astype(f32), axis=0)
    tail = tail[:, :64] + tail[:, 64:]
    grad_left = jnp.concatenate([tail[:, :16], tail[:, 16:32]], axis=0) / n_dp
    grad_right = right_sum / n_dp
    grad_singular = adapter_scale * keep_float * tail[0, 32:48] / n_dp
    return (grad_inputs, grad_left, grad_right, grad_singular)


def solution(mesh):
    fine = Mesh(mesh.devices.reshape(4, 4, 2, 2, 8), ("zh", "x", "c", "zl", "y"))
    dp = ("zh", "x", "c")
    tensor = ("zl", "y")
    in_specs = (
        P(dp + tensor, None),
        P(dp, tensor),
        P(dp, tensor),
        P(),
        P(None, tensor),
        P(),
        P(),
    )
    out_specs = (P(dp + tensor, None), P(dp + tensor, None), P(None, tensor), P())
    return jax.shard_map(body, mesh=fine, in_specs=in_specs, out_specs=out_specs, check_vma=False)
```

```python
import jax
import jax.numpy as jnp
from jax import lax
from jax.experimental import pallas as pl
from jax.experimental.pallas import tpu as pltpu
from jax.sharding import Mesh
from jax.sharding import PartitionSpec as P

adapter_scale = 2.0
n_dp = 32
f32 = jnp.float32
bf16 = jnp.bfloat16
in_vmem = pl.BlockSpec(memory_space=pltpu.VMEM)
in_smem = pl.BlockSpec(memory_space=pltpu.SMEM)
anywhere = pl.BlockSpec(memory_space=pl.ANY)
in_hbm = pl.BlockSpec(memory_space=pltpu.HBM)
dma = pltpu.SemaphoreType.DMA


def dot_t(a, b):
    return lax.dot_general(a, b, (((1,), (1,)), ((), ())), preferred_element_type=f32)


def t_dot(a, b):
    return lax.dot_general(a, b, (((0,), (0,)), ((), ())), preferred_element_type=f32)


def swap(a, axis, count, mask):
    return lax.ppermute(a, axis, [(i, i ^ mask) for i in range(count)])


def call(kernel, out_shape, in_specs, flops, moved, out_specs=None, scratch=()):
    return pl.pallas_call(
        kernel,
        out_shape=out_shape,
        in_specs=in_specs,
        out_specs=out_specs or jax.tree.map(lambda _: in_vmem, out_shape),
        scratch_shapes=scratch,
        compiler_params=pltpu.CompilerParams(vmem_limit_bytes=32 << 20),
        cost_estimate=pl.CostEstimate(flops=flops, bytes_accessed=moved, transcendentals=0),
    )


def after(a, *others):
    return pl.pallas_call(
        lambda *refs: None,
        out_shape=jax.ShapeDtypeStruct(a.shape, a.dtype),
        in_specs=[in_vmem] * (1 + len(others)),
        out_specs=in_vmem,
        input_output_aliases={0: 0},
        compiler_params=pltpu.CompilerParams(vmem_limit_bytes=32 << 20),
    )(a, *others)


def rank_kernel(place_ref, cot_any, right_any, weight_any, projected_ref, out_ref, cot_ref, given_ref, right_ref, sems):
    given_rows = pl.ds(pl.multiple_of((1 - place_ref[1]) * 128, 128), 128)
    copies = [
        pltpu.make_async_copy(cot_any, cot_ref, sems.at[0]),
        pltpu.make_async_copy(right_any, right_ref, sems.at[1]),
        pltpu.make_async_copy(weight_any.at[given_rows], given_ref, sems.at[2]),
    ]
    for copy in copies:
        copy.start()
    out_ref[...] = jnp.zeros((16, 8, 128), f32)
    out_ref[:, :, 16:32] = jnp.broadcast_to(projected_ref[...][None], (16, 8, 16))
    for copy in copies:
        copy.wait()
    out_ref[:, :, 0:16] = dot_t(cot_ref[...], right_ref[...]).reshape(16, 8, 16)


def pack_kernel(
    place_ref, sent_ref, rank_ref, coeff_ref, cot_ref, weight_any, got_ref, inputs_any, after1, after2, after3,
    x_any, back_ref, kept_ref, inputs_ref, x_ref, in_sems, out_sems,
):
    kept_rows = pl.ds(pl.multiple_of(place_ref[1] * 128, 128), 128)
    inputs_in = pltpu.make_async_copy(inputs_any, inputs_ref, in_sems.at[0])
    kept_in = pltpu.make_async_copy(weight_any.at[kept_rows], kept_ref, in_sems.at[1])
    inputs_in.start()
    kept_in.start()
    outs = [pltpu.make_async_copy(got_ref, x_any.at[x, 128:256], out_sems.at[x]) for x in range(4)]
    for copy in outs:
        copy.start()
    lane = lax.broadcasted_iota(jnp.int32, (1, 128), 1)
    rank = rank_ref[...]
    coeff = coeff_ref[...]
    own = jnp.where(lane < 16, jnp.sum(rank, axis=0), 0.0)
    back = (own * coeff).astype(bf16)
    back_ref[...] = back
    fwd = (jnp.where((lane >= 16) & (lane < 32), rank, 0.0) * coeff).astype(bf16)
    right = t_dot(fwd.reshape(128, 128), cot_ref[...])[16:32]
    right_high = right.astype(bf16)
    right_low = (right - right_high.astype(f32)).astype(bf16)
    projected = pltpu.roll(sent_ref[0], 112, 1)
    singular = jnp.broadcast_to(jnp.sum(projected * own, axis=0, keepdims=True), (8, 128))
    high = singular.astype(bf16).astype(f32)
    back8 = back.astype(f32)
    none = jnp.zeros((8, 128), f32)
    small = jnp.concatenate(
        [
            jnp.concatenate([back8, pltpu.roll(back8, 16, 1), none, none], axis=1),
            jnp.concatenate([none, none, pltpu.roll(high, 32, 1), pltpu.roll(singular - high, 32, 1)], axis=1),
        ],
        axis=0,
    ).astype(bf16)
    kept_in.wait()
    for x in range(4):
        outs.append(pltpu.make_async_copy(kept_ref, x_any.at[x, 0:128], out_sems.at[4 + x]))
        outs[-1].start()
    inputs_in.wait()
    inputs = inputs_ref[...].astype(f32)
    for x in range(4):
        rows = [inputs[:, (h * 4 + x) * 512 : (h * 4 + x + 1) * 512] for h in range(4)]
        x_ref[x, 0:32, :] = jnp.concatenate(rows, axis=0).astype(bf16)
        x_ref[x, 32:48, :] = small
        x_ref[x, 48:64, :] = right_high
        x_ref[x, 64:80, :] = right_low
        outs.append(pltpu.make_async_copy(x_ref.at[x], x_any.at[x, 256:336], out_sems.at[8 + x]))
        outs[-1].start()
    for copy in outs:
        copy.wait()


def products(parts, ref):
    total = dot_t(parts[0], ref[:, 0:128, :].reshape(512, 512))
    total += dot_t(parts[1], ref[:, 128:256, :].reshape(512, 512))
    return total.astype(bf16).reshape(4, 128, 512)


def own_kernel(own_ref, near_ref, far_ref, out_ref):
    out_ref[...] = products((near_ref[...].reshape(512, 512), far_ref[...].reshape(512, 512)), own_ref)


def other_kernel(
    place_ref, done_ref, own_ref, other_ref, near_ref, far_ref, out_any, right_ref, out_ref, sems
):
    core, z_high = place_ref[0], place_ref[2]
    total = products((near_ref[...].reshape(512, 512), far_ref[...].reshape(512, 512)), other_ref)
    for k in range(4):
        out_ref[z_high ^ k, :, 0:512] = done_ref[k]
        out_ref[z_high ^ k, :, 512:1024] = total[k]
    tok, back, singular = [], [], jnp.zeros((1, 128), f32)
    for ref in (own_ref, other_ref):
        for x in range(4):
            rows = ref[x, 256:288, :]
            tok.append(jnp.where(core == 0, rows[:, :256], rows[:, 256:]))
            small = ref[x, 288:304, :].astype(f32)
            back.extend([small[0:8, :256]] * 4)
            singular += small[8:9, 256:384] + small[8:9, 384:512]
    tok = jnp.concatenate(tok, axis=0)
    back = jnp.concatenate(back, axis=0)
    group = lax.rem(lax.broadcasted_iota(jnp.int32, (256, 1), 0), 32) // 8
    copies = []
    for h in range(4):
        both = t_dot(tok, jnp.where(group == h, back, 0.0).astype(bf16))
        a = both[:, :128].reshape(16, 2, 8, 128)[:, 0]
        b = both[:, 128:].reshape(16, 2, 8, 128)[:, 1]
        z = (a + b + singular).reshape(128, 128)
        high = z.astype(bf16).astype(f32)
        out_ref[h, :, 1024:1152] = (high + pltpu.roll(z - high, 64, 1)).astype(bf16)
        copies.append(pltpu.make_async_copy(out_ref.at[h], out_any.at[h], sems.at[h]))
        copies[-1].start()
    right = jnp.zeros((16, 512), f32)
    for ref in (own_ref, other_ref):
        for x in range(4):
            right += ref[x, 304:320, :].astype(f32) + ref[x, 320:336, :].astype(f32)
    right_ref[...] = right
    for copy in copies:
        copy.wait()


def final_kernel(
    place_ref, back_ref, scaled_ref, left_any, keep_ref, inputs_any, grad_left_any, singular_any,
    left_ref, inputs_ref, grad_left_ref, singular_ref, sems,
):
    left_in = pltpu.make_async_copy(left_any, left_ref, sems.at[0])
    left_in.start()
    core = place_ref[0]
    tail = jnp.sum(back_ref[:, :, 1024:].astype(f32), axis=0)
    tail = (tail + pltpu.roll(tail, 64, 1)) / n_dp
    grad_left_ref[0:8, :] = tail[:, 0:16]
    grad_left_ref[8:16, :] = pltpu.roll(tail, 112, 1)[:, 0:16]
    singular_ref[...] = adapter_scale * keep_ref[...] * pltpu.roll(tail, 96, 1)[0:1, 0:16]
    outs = [
        pltpu.make_async_copy(grad_left_ref, grad_left_any, sems.at[1]),
        pltpu.make_async_copy(singular_ref, singular_any, sems.at[2]),
    ]
    outs[0].start()
    outs[1].start()
    left_in.wait()
    scaled = scaled_ref[:, 0:16]
    for h in range(4):
        for low in range(2):
            first = (h * 2 + low) * 8
            total = jnp.sum(back_ref[first : first + 8, :, 0:1024].astype(f32), axis=0)
            own, other = total[:, :512], total[:, 512:]
            for c, part in enumerate((jnp.where(core == 0, own, other), jnp.where(core == 0, other, own))):
                for x in range(4):
                    at = h * 2048 + x * 512 + c * 256 + low * 128
                    term = jnp.dot(scaled, left_ref[:, at : at + 128], preferred_element_type=f32)
                    inputs_ref[:, at : at + 128] = (part[:, x * 128 : x * 128 + 128] + term).astype(bf16)
    outs.append(pltpu.make_async_copy(inputs_ref, inputs_any, sems.at[3]))
    outs[2].start()
    for copy in outs:
        copy.wait()


def body(inputs, cotangent, weight, left_factor, right_factor, singular, keep_mask):
    core = lax.axis_index("c")
    z_low = lax.axis_index("zl")
    z_high = lax.axis_index("zh")
    place = jnp.stack([core, z_low, z_high]).astype(jnp.int32)
    shape = jax.ShapeDtypeStruct
    keep_float = keep_mask.astype(f32)
    coeff = adapter_scale * singular * keep_float

    own_projected = jnp.dot(inputs, left_factor, preferred_element_type=f32)
    rank_out, cot, given = call(
        rank_kernel,
        (shape((16, 8, 128), f32), shape((128, 512), bf16), shape((128, 512), bf16)),
        [in_smem] + [in_hbm] * 3 + [in_vmem],
        2 << 20,
        1 << 20,
        scratch=[pltpu.VMEM((16, 512), bf16), dma((3,))],
    )(place, cotangent, right_factor, weight, own_projected)
    rank_in = lax.all_to_all(rank_out, ("zl", "y"), 0, 0)

    got = swap(given, "zl", 2, 1)

    cots = [cot] + [swap(cot, "zh", 4, k) for k in (1, 2, 3)]
    near = jnp.stack(cots)
    far = swap(near, "zl", 2, 1)

    coeff_lanes = jnp.pad(jnp.concatenate([coeff, coeff]), (0, 96)).reshape(1, 128)
    x_out, scaled_back = call(
        pack_kernel,
        (shape((4, 336, 512), bf16), shape((8, 128), bf16)),
        [in_smem] + [in_vmem] * 4 + [in_hbm, in_vmem, in_hbm] + [anywhere] * 3,
        16 << 20,
        3 << 20,
        out_specs=(in_hbm, in_vmem),
        scratch=[
            pltpu.VMEM((128, 512), bf16),
            pltpu.VMEM((8, 8192), bf16),
            pltpu.VMEM((4, 80, 512), bf16),
            dma((2,)),
            dma((12,)),
        ],
    )(place, rank_out, rank_in, coeff_lanes, cot, weight, got, inputs, *cots[1:])
    x_in = after(lax.all_to_all(x_out, "x", 0, 0), far)
    x_other = swap(x_in, "c", 2, 1)

    done = call(own_kernel, shape((4, 128, 512), bf16), [in_vmem] * 3, 1 << 29, 3 << 20)(x_in, near, far)
    out, right_part = call(
        other_kernel,
        (shape((4, 128, 1152), bf16), shape((16, 512), f32)),
        [in_smem] + [in_vmem] * 5,
        1 << 29,
        5 << 20,
        out_specs=(in_hbm, in_vmem),
        scratch=[pltpu.VMEM((4, 128, 1152), bf16), dma((4,))],
    )(place, done, x_in, x_other, near, far)
    back = lax.all_to_all(out.reshape(64, 8, 1152), ("zh", "zl", "y"), 0, 0)
    right_sum = right_part + sum(swap(right_part, "zh", 4, k) for k in (1, 2, 3))

    grad_inputs, grad_left, grad_singular = call(
        final_kernel,
        (shape((8, 8192), bf16), shape((16, 16), f32), shape((1, 16), f32)),
        [in_smem, in_vmem, in_vmem, in_hbm, in_vmem],
        2 << 20,
        2 << 20,
        out_specs=(in_hbm, in_hbm, in_hbm),
        scratch=[
            pltpu.VMEM((16, 8192), bf16),
            pltpu.VMEM((8, 8192), bf16),
            pltpu.VMEM((16, 16), f32),
            pltpu.VMEM((1, 16), f32),
            dma((4,)),
        ],
    )(place, back, scaled_back, left_factor.T, keep_float.reshape(1, 16))
    grad_right = right_sum / n_dp
    return (grad_inputs, grad_left, grad_right, grad_singular.reshape(16))


def solution(mesh):
    fine = Mesh(mesh.devices.reshape(4, 4, 2, 2, 8), ("zh", "x", "c", "zl", "y"))
    dp = ("zh", "x", "c")
    tensor = ("zl", "y")
    in_specs = (
        P(dp + tensor, None),
        P(dp, tensor),
        P(dp, tensor),
        P(),
        P(None, tensor),
        P(),
        P(),
    )
    out_specs = (P(dp + tensor, None), P(dp + tensor, None), P(None, tensor), P())
    return jax.shard_map(body, mesh=fine, in_specs=in_specs, out_specs=out_specs, check_vma=False)
```

```python
import jax
import jax.numpy as jnp
from jax import lax
from jax.experimental import pallas as pl
from jax.experimental.pallas import tpu as pltpu
from jax.sharding import Mesh
from jax.sharding import PartitionSpec as P

adapter_scale = 2.0
n_dp = 32
f32 = jnp.float32
bf16 = jnp.bfloat16
in_vmem = pl.BlockSpec(memory_space=pltpu.VMEM)
in_smem = pl.BlockSpec(memory_space=pltpu.SMEM)
anywhere = pl.BlockSpec(memory_space=pl.ANY)
in_hbm = pl.BlockSpec(memory_space=pltpu.HBM)
dma = pltpu.SemaphoreType.DMA


def dot_t(a, b):
    return lax.dot_general(a, b, (((1,), (1,)), ((), ())), preferred_element_type=f32)


def t_dot(a, b):
    return lax.dot_general(a, b, (((0,), (0,)), ((), ())), preferred_element_type=f32)


def swap(a, axis, count, mask):
    return lax.ppermute(a, axis, [(i, i ^ mask) for i in range(count)])


def call(kernel, out_shape, in_specs, flops, moved, out_specs=None, scratch=()):
    return pl.pallas_call(
        kernel,
        out_shape=out_shape,
        in_specs=in_specs,
        out_specs=out_specs or jax.tree.map(lambda _: in_vmem, out_shape),
        scratch_shapes=scratch,
        compiler_params=pltpu.CompilerParams(vmem_limit_bytes=32 << 20),
        cost_estimate=pl.CostEstimate(flops=flops, bytes_accessed=moved, transcendentals=0),
    )


def after(a, *others):
    return pl.pallas_call(
        lambda *refs: None,
        out_shape=jax.ShapeDtypeStruct(a.shape, a.dtype),
        in_specs=[in_vmem] * (1 + len(others)),
        out_specs=in_vmem,
        input_output_aliases={0: 0},
        compiler_params=pltpu.CompilerParams(vmem_limit_bytes=32 << 20),
    )(a, *others)


def pack_kernel(
    place_ref, sent_ref, rank_ref, coeff_ref, cot_ref, weight_any, got_any, slices_ref, after1, after2, after3,
    x_any, back_ref, kept_ref, rest_ref, kept_sem, out_sems,
):
    rows = pl.ds(pl.multiple_of(place_ref[1] * 128, 128), 128)
    kept_in = pltpu.make_async_copy(weight_any.at[rows], kept_ref, kept_sem)
    kept_in.start()
    outs = [pltpu.make_async_copy(got_any.at[rows], x_any.at[x, 128:256], out_sems.at[x]) for x in range(4)]
    outs += [pltpu.make_async_copy(slices_ref.at[x], x_any.at[x, 256:288], out_sems.at[4 + x]) for x in range(4)]
    for copy in outs:
        copy.start()
    lane = lax.broadcasted_iota(jnp.int32, (1, 128), 1)
    rank = rank_ref[...]
    coeff = coeff_ref[...]
    own = jnp.where(lane < 16, jnp.sum(rank, axis=0), 0.0)
    back = (own * coeff).astype(bf16)
    back_ref[...] = back
    fwd = (jnp.where((lane >= 16) & (lane < 32), rank, 0.0) * coeff).astype(bf16)
    right = t_dot(fwd.reshape(128, 128), cot_ref[...])[16:32]
    right_high = right.astype(bf16)
    right_low = (right - right_high.astype(f32)).astype(bf16)
    projected = pltpu.roll(sent_ref[0], 112, 1)
    singular = jnp.broadcast_to(jnp.sum(projected * own, axis=0, keepdims=True), (8, 128))
    high = singular.astype(bf16).astype(f32)
    back8 = back.astype(f32)
    none = jnp.zeros((8, 128), f32)
    small = jnp.concatenate(
        [
            jnp.concatenate([back8, pltpu.roll(back8, 16, 1), none, none], axis=1),
            jnp.concatenate([none, none, pltpu.roll(high, 32, 1), pltpu.roll(singular - high, 32, 1)], axis=1),
        ],
        axis=0,
    ).astype(bf16)
    rest_ref[0:16, :] = small
    rest_ref[16:32, :] = right_high
    rest_ref[32:48, :] = right_low
    kept_in.wait()
    for x in range(4):
        outs.append(pltpu.make_async_copy(kept_ref, x_any.at[x, 0:128], out_sems.at[8 + x]))
        outs.append(pltpu.make_async_copy(rest_ref, x_any.at[x, 288:336], out_sems.at[12 + x]))
        outs[-2].start()
        outs[-1].start()
    for copy in outs:
        copy.wait()


def products(parts, ref):
    total = dot_t(parts[0], ref[:, 0:128, :].reshape(512, 512))
    total += dot_t(parts[1], ref[:, 128:256, :].reshape(512, 512))
    return total.astype(bf16).reshape(4, 128, 512)


def own_kernel(own_ref, near_ref, far_ref, out_ref):
    out_ref[...] = products((near_ref[...].reshape(512, 512), far_ref[...].reshape(512, 512)), own_ref)


def other_kernel(
    place_ref, done_ref, own_ref, other_ref, near_ref, far_ref, out_ref, right_ref
):
    core, z_high = place_ref[0], place_ref[2]
    total = products((near_ref[...].reshape(512, 512), far_ref[...].reshape(512, 512)), other_ref)
    for k in range(4):
        out_ref[z_high ^ k, :, 0:512] = done_ref[k]
        out_ref[z_high ^ k, :, 512:1024] = total[k]
    tok, back, singular = [], [], jnp.zeros((1, 128), f32)
    for ref in (own_ref, other_ref):
        for x in range(4):
            rows = ref[x, 256:288, :]
            tok.append(jnp.where(core == 0, rows[:, :256], rows[:, 256:]))
            small = ref[x, 288:304, :].astype(f32)
            back.extend([small[0:8, :256]] * 4)
            singular += small[8:9, 256:384] + small[8:9, 384:512]
    tok = jnp.concatenate(tok, axis=0)
    back = jnp.concatenate(back, axis=0)
    group = lax.rem(lax.broadcasted_iota(jnp.int32, (256, 1), 0), 32) // 8
    for h in range(4):
        both = t_dot(tok, jnp.where(group == h, back, 0.0).astype(bf16))
        a = both[:, :128].reshape(16, 2, 8, 128)[:, 0]
        b = both[:, 128:].reshape(16, 2, 8, 128)[:, 1]
        z = (a + b + singular).reshape(128, 128)
        high = z.astype(bf16).astype(f32)
        out_ref[h, :, 1024:1152] = (high + pltpu.roll(z - high, 64, 1)).astype(bf16)
    right = jnp.zeros((16, 512), f32)
    for ref in (own_ref, other_ref):
        for x in range(4):
            right += ref[x, 304:320, :].astype(f32) + ref[x, 320:336, :].astype(f32)
    right_ref[...] = right


def final_kernel(
    place_ref, back_ref, scaled_ref, left_any, keep_ref, inputs_any, grad_left_any, singular_any,
    left_ref, inputs_ref, grad_left_ref, singular_ref, sems,
):
    left_in = pltpu.make_async_copy(left_any, left_ref, sems.at[0])
    left_in.start()
    core = place_ref[0]
    tail = jnp.sum(back_ref[:, :, 1024:].astype(f32), axis=0)
    tail = (tail + pltpu.roll(tail, 64, 1)) / n_dp
    grad_left_ref[0:8, :] = tail[:, 0:16]
    grad_left_ref[8:16, :] = pltpu.roll(tail, 112, 1)[:, 0:16]
    singular_ref[...] = adapter_scale * keep_ref[...] * pltpu.roll(tail, 96, 1)[0:1, 0:16]
    outs = [
        pltpu.make_async_copy(grad_left_ref, grad_left_any, sems.at[1]),
        pltpu.make_async_copy(singular_ref, singular_any, sems.at[2]),
    ]
    outs[0].start()
    outs[1].start()
    left_in.wait()
    scaled = scaled_ref[:, 0:16]
    for h in range(4):
        for low in range(2):
            first = (h * 2 + low) * 8
            total = jnp.sum(back_ref[first : first + 8, :, 0:1024].astype(f32), axis=0)
            own, other = total[:, :512], total[:, 512:]
            for c, part in enumerate((jnp.where(core == 0, own, other), jnp.where(core == 0, other, own))):
                for x in range(4):
                    at = h * 2048 + x * 512 + c * 256 + low * 128
                    term = jnp.dot(scaled, left_ref[:, at : at + 128], preferred_element_type=f32)
                    inputs_ref[:, at : at + 128] = (part[:, x * 128 : x * 128 + 128] + term).astype(bf16)
    outs.append(pltpu.make_async_copy(inputs_ref, inputs_any, sems.at[3]))
    outs[2].start()
    for copy in outs:
        copy.wait()


def body(inputs, cotangent, weight, left_factor, right_factor, singular, keep_mask):
    core = lax.axis_index("c")
    z_low = lax.axis_index("zl")
    z_high = lax.axis_index("zh")
    place = jnp.stack([core, z_low, z_high]).astype(jnp.int32)
    shape = jax.ShapeDtypeStruct
    keep_float = keep_mask.astype(f32)
    coeff = adapter_scale * singular * keep_float

    got = swap(weight, "zl", 2, 1)

    back_part = dot_t(cotangent, right_factor).reshape(16, 8, 16)
    own_projected = jnp.dot(inputs, left_factor, preferred_element_type=f32)
    rank_out = jnp.pad(back_part, ((0, 0), (0, 0), (0, 112))) + jnp.pad(own_projected, ((0, 0), (16, 96)))
    rank_in = lax.all_to_all(rank_out, ("zl", "y"), 0, 0)

    cot = after(cotangent, got)
    cots = [cot] + [swap(cot, "zh", 4, k) for k in (1, 2, 3)]
    near = jnp.stack(cots)
    far = swap(near, "zl", 2, 1)

    coeff_lanes = jnp.pad(jnp.concatenate([coeff, coeff]), (0, 96)).reshape(1, 128)
    slices = inputs.reshape(8, 4, 4, 512).transpose(2, 1, 0, 3).reshape(4, 32, 512)
    x_out, scaled_back = call(
        pack_kernel,
        (shape((4, 336, 512), bf16), shape((8, 128), bf16)),
        [in_smem] + [in_vmem] * 4 + [anywhere] * 2 + [in_vmem] + [anywhere] * 3,
        16 << 20,
        3 << 20,
        out_specs=(in_hbm, in_vmem),
        scratch=[pltpu.VMEM((128, 512), bf16), pltpu.VMEM((48, 512), bf16), dma, dma((16,))],
    )(place, rank_out, rank_in, coeff_lanes, cot, weight, got, slices, *cots[1:])
    x_in = after(lax.all_to_all(x_out, "x", 0, 0), far)
    x_other = swap(x_in, "c", 2, 1)

    done = call(own_kernel, shape((4, 128, 512), bf16), [in_vmem] * 3, 1 << 29, 3 << 20)(x_in, near, far)
    out, right_part = call(
        other_kernel,
        (shape((4, 128, 1152), bf16), shape((16, 512), f32)),
        [in_smem] + [in_vmem] * 5,
        1 << 29,
        5 << 20,
    )(place, done, x_in, x_other, near, far)
    back = lax.all_to_all(out.reshape(64, 8, 1152), ("zh", "zl", "y"), 0, 0)
    right_sum = right_part + sum(swap(right_part, "zh", 4, k) for k in (1, 2, 3))

    grad_inputs, grad_left, grad_singular = call(
        final_kernel,
        (shape((8, 8192), bf16), shape((16, 16), f32), shape((1, 16), f32)),
        [in_smem, in_vmem, in_vmem, in_hbm, in_vmem],
        2 << 20,
        2 << 20,
        out_specs=(in_hbm, in_hbm, in_hbm),
        scratch=[
            pltpu.VMEM((16, 8192), bf16),
            pltpu.VMEM((8, 8192), bf16),
            pltpu.VMEM((16, 16), f32),
            pltpu.VMEM((1, 16), f32),
            dma((4,)),
        ],
    )(place, back, scaled_back, left_factor.T, keep_float.reshape(1, 16))
    grad_right = right_sum / n_dp
    return (grad_inputs, grad_left, grad_right, grad_singular.reshape(16))


def solution(mesh):
    fine = Mesh(mesh.devices.reshape(4, 4, 2, 2, 8), ("zh", "x", "c", "zl", "y"))
    dp = ("zh", "x", "c")
    tensor = ("zl", "y")
    in_specs = (
        P(dp + tensor, None),
        P(dp, tensor),
        P(dp, tensor),
        P(),
        P(None, tensor),
        P(),
        P(),
    )
    out_specs = (P(dp + tensor, None), P(dp + tensor, None), P(None, tensor), P())
    return jax.shard_map(body, mesh=fine, in_specs=in_specs, out_specs=out_specs, check_vma=False)
```

```python
import jax
import jax.numpy as jnp
from jax import lax
from jax.experimental import pallas as pl
from jax.experimental.pallas import tpu as pltpu
from jax.sharding import Mesh
from jax.sharding import PartitionSpec as P

adapter_scale = 2.0
n_dp = 32
f32 = jnp.float32
bf16 = jnp.bfloat16
in_vmem = pl.BlockSpec(memory_space=pltpu.VMEM)
in_smem = pl.BlockSpec(memory_space=pltpu.SMEM)
anywhere = pl.BlockSpec(memory_space=pl.ANY)
in_hbm = pl.BlockSpec(memory_space=pltpu.HBM)
dma = pltpu.SemaphoreType.DMA


def dot_t(a, b):
    return lax.dot_general(a, b, (((1,), (1,)), ((), ())), preferred_element_type=f32)


def t_dot(a, b):
    return lax.dot_general(a, b, (((0,), (0,)), ((), ())), preferred_element_type=f32)


def swap(a, axis, count, mask):
    return lax.ppermute(a, axis, [(i, i ^ mask) for i in range(count)])


def call(kernel, out_shape, in_specs, flops, moved, out_specs=None, scratch=()):
    return pl.pallas_call(
        kernel,
        out_shape=out_shape,
        in_specs=in_specs,
        out_specs=out_specs or jax.tree.map(lambda _: in_vmem, out_shape),
        scratch_shapes=scratch,
        compiler_params=pltpu.CompilerParams(vmem_limit_bytes=32 << 20),
        cost_estimate=pl.CostEstimate(flops=flops, bytes_accessed=moved, transcendentals=0),
    )


def after(a, *others):
    return pl.pallas_call(
        lambda *refs: None,
        out_shape=jax.ShapeDtypeStruct(a.shape, a.dtype),
        in_specs=[in_vmem] * (1 + len(others)),
        out_specs=in_vmem,
        input_output_aliases={0: 0},
        compiler_params=pltpu.CompilerParams(vmem_limit_bytes=32 << 20),
    )(a, *others)


def pack_kernel(
    place_ref, sent_ref, rank_ref, coeff_ref, cot_ref, weight_any, got_any, slices_ref, after1, after3,
    x_any, back_ref, kept_ref, rest_ref, kept_sem, out_sems,
):
    rows = pl.ds(pl.multiple_of(place_ref[1] * 128, 128), 128)
    kept_in = pltpu.make_async_copy(weight_any.at[rows], kept_ref, kept_sem)
    kept_in.start()
    outs = [pltpu.make_async_copy(got_any.at[rows], x_any.at[x, 128:256], out_sems.at[x]) for x in range(4)]
    outs += [pltpu.make_async_copy(slices_ref.at[x], x_any.at[x, 256:288], out_sems.at[4 + x]) for x in range(4)]
    for copy in outs:
        copy.start()
    lane = lax.broadcasted_iota(jnp.int32, (1, 128), 1)
    rank = rank_ref[...]
    coeff = coeff_ref[...]
    own = jnp.where(lane < 16, jnp.sum(rank, axis=0), 0.0)
    back = (own * coeff).astype(bf16)
    back_ref[...] = back
    fwd = (jnp.where((lane >= 16) & (lane < 32), rank, 0.0) * coeff).astype(bf16)
    right = t_dot(fwd.reshape(128, 128), cot_ref[...])[16:32]
    projected = pltpu.roll(sent_ref[0], 112, 1)
    singular = jnp.broadcast_to(jnp.sum(projected * own, axis=0, keepdims=True), (8, 128))
    high = singular.astype(bf16).astype(f32)
    back8 = back.astype(f32)
    none = jnp.zeros((8, 128), f32)
    small = jnp.concatenate(
        [
            jnp.concatenate([back8, pltpu.roll(back8, 16, 1), none, none], axis=1),
            jnp.concatenate([none, none, pltpu.roll(high, 32, 1), pltpu.roll(singular - high, 32, 1)], axis=1),
        ],
        axis=0,
    ).astype(bf16)
    rest_ref[0:16, :] = small
    rest_ref[16:32, :] = right.astype(bf16)
    kept_in.wait()
    for x in range(4):
        outs.append(pltpu.make_async_copy(kept_ref, x_any.at[x, 0:128], out_sems.at[8 + x]))
        outs.append(pltpu.make_async_copy(rest_ref, x_any.at[x, 288:320], out_sems.at[12 + x]))
        outs[-2].start()
        outs[-1].start()
    for copy in outs:
        copy.wait()


def products(parts, ref):
    total = dot_t(parts[0], ref[:, 0:128, :].reshape(512, 512))
    total += dot_t(parts[1], ref[:, 128:256, :].reshape(512, 512))
    return total.astype(bf16).reshape(4, 128, 512)


def rows_of(three_ref, last_ref):
    return jnp.concatenate([three_ref[...].reshape(384, 512), last_ref[...]], axis=0)


def own_kernel(own_ref, near_ref, last_ref, far_ref, far_last_ref, out_ref):
    out_ref[...] = products((rows_of(near_ref, last_ref), rows_of(far_ref, far_last_ref)), own_ref)


def other_kernel(
    place_ref, done_ref, own_ref, other_ref, near_ref, last_ref, far_ref, far_last_ref, out_ref, right_ref
):
    core, z_high = place_ref[0], place_ref[2]
    total = products((rows_of(near_ref, last_ref), rows_of(far_ref, far_last_ref)), other_ref)
    for i, k in enumerate((0, 1, 3, 2)):
        out_ref[z_high ^ k, :, 0:512] = done_ref[i]
        out_ref[z_high ^ k, :, 512:1024] = total[i]
    tok, back, singular = [], [], jnp.zeros((1, 128), f32)
    for ref in (own_ref, other_ref):
        for x in range(4):
            rows = ref[x, 256:288, :]
            tok.append(jnp.where(core == 0, rows[:, :256], rows[:, 256:]))
            small = ref[x, 288:304, :].astype(f32)
            back.extend([small[0:8, :256]] * 4)
            singular += small[8:9, 256:384] + small[8:9, 384:512]
    tok = jnp.concatenate(tok, axis=0)
    back = jnp.concatenate(back, axis=0)
    group = lax.rem(lax.broadcasted_iota(jnp.int32, (256, 1), 0), 32) // 8
    for h in range(4):
        both = t_dot(tok, jnp.where(group == h, back, 0.0).astype(bf16))
        a = both[:, :128].reshape(16, 2, 8, 128)[:, 0]
        b = both[:, 128:].reshape(16, 2, 8, 128)[:, 1]
        z = (a + b + singular).reshape(128, 128)
        high = z.astype(bf16).astype(f32)
        out_ref[h, :, 1024:1152] = (high + pltpu.roll(z - high, 64, 1)).astype(bf16)
    right = jnp.zeros((16, 512), f32)
    for ref in (own_ref, other_ref):
        for x in range(4):
            right += ref[x, 304:320, :].astype(f32)
    right_ref[...] = right


def final_kernel(
    place_ref, back_ref, scaled_ref, left_any, keep_ref, inputs_any, grad_left_any, singular_any,
    left_ref, inputs_ref, grad_left_ref, singular_ref, sems,
):
    left_in = pltpu.make_async_copy(left_any, left_ref, sems.at[0])
    left_in.start()
    core = place_ref[0]
    tail = jnp.sum(back_ref[:, :, 1024:].astype(f32), axis=0)
    tail = (tail + pltpu.roll(tail, 64, 1)) / n_dp
    grad_left_ref[0:8, :] = tail[:, 0:16]
    grad_left_ref[8:16, :] = pltpu.roll(tail, 112, 1)[:, 0:16]
    singular_ref[...] = adapter_scale * keep_ref[...] * pltpu.roll(tail, 96, 1)[0:1, 0:16]
    outs = [
        pltpu.make_async_copy(grad_left_ref, grad_left_any, sems.at[1]),
        pltpu.make_async_copy(singular_ref, singular_any, sems.at[2]),
    ]
    outs[0].start()
    outs[1].start()
    left_in.wait()
    scaled = scaled_ref[:, 0:16]
    for h in range(4):
        for low in range(2):
            first = (h * 2 + low) * 8
            total = jnp.sum(back_ref[first : first + 8, :, 0:1024].astype(f32), axis=0)
            own, other = total[:, :512], total[:, 512:]
            for c, part in enumerate((jnp.where(core == 0, own, other), jnp.where(core == 0, other, own))):
                for x in range(4):
                    at = h * 2048 + x * 512 + c * 256 + low * 128
                    term = jnp.dot(scaled, left_ref[:, at : at + 128], preferred_element_type=f32)
                    inputs_ref[:, at : at + 128] = (part[:, x * 128 : x * 128 + 128] + term).astype(bf16)
    outs.append(pltpu.make_async_copy(inputs_ref, inputs_any, sems.at[3]))
    outs[2].start()
    for copy in outs:
        copy.wait()


def body(inputs, cotangent, weight, left_factor, right_factor, singular, keep_mask):
    core = lax.axis_index("c")
    z_low = lax.axis_index("zl")
    z_high = lax.axis_index("zh")
    place = jnp.stack([core, z_low, z_high]).astype(jnp.int32)
    shape = jax.ShapeDtypeStruct
    keep_float = keep_mask.astype(f32)
    coeff = adapter_scale * singular * keep_float

    got = swap(weight, "zl", 2, 1)

    back_part = dot_t(cotangent, right_factor).reshape(16, 8, 16)
    own_projected = jnp.dot(inputs, left_factor, preferred_element_type=f32)
    rank_out = jnp.pad(back_part, ((0, 0), (0, 0), (0, 112))) + jnp.pad(own_projected, ((0, 0), (16, 96)))
    rank_in = lax.all_to_all(rank_out, ("zl", "y"), 0, 0)

    cot = after(cotangent, got)
    cots = [cot] + [swap(cot, "zh", 4, k) for k in (1, 2, 3)]
    near = jnp.stack([cots[0], cots[1], cots[3]])
    far = swap(near, "zl", 2, 1)
    last = cots[2]
    far_last = swap(last, "zl", 2, 1)

    coeff_lanes = jnp.pad(jnp.concatenate([coeff, coeff]), (0, 96)).reshape(1, 128)
    slices = inputs.reshape(8, 4, 4, 512).transpose(2, 1, 0, 3).reshape(4, 32, 512)
    x_out, scaled_back = call(
        pack_kernel,
        (shape((4, 320, 512), bf16), shape((8, 128), bf16)),
        [in_smem] + [in_vmem] * 4 + [anywhere] * 2 + [in_vmem] + [anywhere] * 2,
        16 << 20,
        3 << 20,
        out_specs=(in_hbm, in_vmem),
        scratch=[pltpu.VMEM((128, 512), bf16), pltpu.VMEM((32, 512), bf16), dma, dma((16,))],
    )(place, rank_out, rank_in, coeff_lanes, cot, weight, got, slices, cots[1], cots[3])
    x_in = after(lax.all_to_all(x_out, "x", 0, 0), far, far_last)
    x_other = swap(x_in, "c", 2, 1)

    done = call(own_kernel, shape((4, 128, 512), bf16), [in_vmem] * 5, 1 << 29, 3 << 20)(
        x_in, near, last, far, far_last
    )
    out, right_part = call(
        other_kernel,
        (shape((4, 128, 1152), bf16), shape((16, 512), f32)),
        [in_smem] + [in_vmem] * 7,
        1 << 29,
        5 << 20,
    )(place, done, x_in, x_other, near, last, far, far_last)
    back = lax.all_to_all(out.reshape(64, 8, 1152), ("zh", "zl", "y"), 0, 0)
    right_sent = right_part.astype(bf16)
    right_sum = right_part + sum(swap(right_sent, "zh", 4, k).astype(f32) for k in (1, 2, 3))

    grad_inputs, grad_left, grad_singular = call(
        final_kernel,
        (shape((8, 8192), bf16), shape((16, 16), f32), shape((1, 16), f32)),
        [in_smem, in_vmem, in_vmem, in_hbm, in_vmem],
        2 << 20,
        2 << 20,
        out_specs=(in_hbm, in_hbm, in_hbm),
        scratch=[
            pltpu.VMEM((16, 8192), bf16),
            pltpu.VMEM((8, 8192), bf16),
            pltpu.VMEM((16, 16), f32),
            pltpu.VMEM((1, 16), f32),
            dma((4,)),
        ],
    )(place, back, scaled_back, left_factor.T, keep_float.reshape(1, 16))
    grad_right = right_sum / n_dp
    return (grad_inputs, grad_left, grad_right, grad_singular.reshape(16))


def solution(mesh):
    fine = Mesh(mesh.devices.reshape(4, 4, 2, 2, 8), ("zh", "x", "c", "zl", "y"))
    dp = ("zh", "x", "c")
    tensor = ("zl", "y")
    in_specs = (
        P(dp + tensor, None),
        P(dp, tensor),
        P(dp, tensor),
        P(),
        P(None, tensor),
        P(),
        P(),
    )
    out_specs = (P(dp + tensor, None), P(dp + tensor, None), P(None, tensor), P())
    return jax.shard_map(body, mesh=fine, in_specs=in_specs, out_specs=out_specs, check_vma=False)
```

```python
import jax
import jax.numpy as jnp
from jax import lax
from jax.experimental import pallas as pl
from jax.experimental.pallas import tpu as pltpu
from jax.sharding import Mesh
from jax.sharding import PartitionSpec as P

adapter_scale = 2.0
n_dp = 32
f32 = jnp.float32
bf16 = jnp.bfloat16
in_vmem = pl.BlockSpec(memory_space=pltpu.VMEM)
in_smem = pl.BlockSpec(memory_space=pltpu.SMEM)
anywhere = pl.BlockSpec(memory_space=pl.ANY)
in_hbm = pl.BlockSpec(memory_space=pltpu.HBM)
dma = pltpu.SemaphoreType.DMA


def dot_t(a, b):
    return lax.dot_general(a, b, (((1,), (1,)), ((), ())), preferred_element_type=f32)


def t_dot(a, b):
    return lax.dot_general(a, b, (((0,), (0,)), ((), ())), preferred_element_type=f32)


def swap(a, axis, count, mask):
    return lax.ppermute(a, axis, [(i, i ^ mask) for i in range(count)])


def call(kernel, out_shape, in_specs, flops, moved, out_specs=None, scratch=()):
    return pl.pallas_call(
        kernel,
        out_shape=out_shape,
        in_specs=in_specs,
        out_specs=out_specs or jax.tree.map(lambda _: in_vmem, out_shape),
        scratch_shapes=scratch,
        compiler_params=pltpu.CompilerParams(vmem_limit_bytes=32 << 20),
        cost_estimate=pl.CostEstimate(flops=flops, bytes_accessed=moved, transcendentals=0),
    )


def after(a, *others):
    return pl.pallas_call(
        lambda *refs: None,
        out_shape=jax.ShapeDtypeStruct(a.shape, a.dtype),
        in_specs=[in_vmem] * (1 + len(others)),
        out_specs=in_vmem,
        input_output_aliases={0: 0},
        compiler_params=pltpu.CompilerParams(vmem_limit_bytes=32 << 20),
    )(a, *others)


def pack_kernel(
    place_ref, sent_ref, rank_ref, coeff_ref, cot_ref, weight_any, got_any, slices_ref, after1, after3,
    x_any, back_ref, kept_ref, rest_ref, kept_sem, out_sems,
):
    rows = pl.ds(pl.multiple_of(place_ref[1] * 128, 128), 128)
    kept_in = pltpu.make_async_copy(weight_any.at[rows], kept_ref, kept_sem)
    kept_in.start()
    outs = [pltpu.make_async_copy(got_any.at[rows], x_any.at[x, 128:256], out_sems.at[x]) for x in range(4)]
    outs += [pltpu.make_async_copy(slices_ref.at[x], x_any.at[x, 256:288], out_sems.at[4 + x]) for x in range(4)]
    for copy in outs:
        copy.start()
    lane = lax.broadcasted_iota(jnp.int32, (1, 128), 1)
    rank = rank_ref[...]
    coeff = coeff_ref[...]
    own = jnp.where(lane < 16, jnp.sum(rank, axis=0), 0.0)
    back = (own * coeff).astype(bf16)
    back_ref[...] = back
    fwd = (jnp.where((lane >= 16) & (lane < 32), rank, 0.0) * coeff).astype(bf16)
    right = t_dot(fwd.reshape(128, 128), cot_ref[...])[16:32]
    projected = pltpu.roll(sent_ref[0], 112, 1)
    singular = jnp.broadcast_to(jnp.sum(projected * own, axis=0, keepdims=True), (8, 128))
    high = singular.astype(bf16).astype(f32)
    back8 = back.astype(f32)
    none = jnp.zeros((8, 128), f32)
    small = jnp.concatenate(
        [
            jnp.concatenate([back8, pltpu.roll(back8, 16, 1), none, none], axis=1),
            jnp.concatenate([none, none, pltpu.roll(high, 32, 1), pltpu.roll(singular - high, 32, 1)], axis=1),
        ],
        axis=0,
    ).astype(bf16)
    rest_ref[0:16, :] = small
    rest_ref[16:32, :] = right.astype(bf16)
    kept_in.wait()
    for x in range(4):
        outs.append(pltpu.make_async_copy(kept_ref, x_any.at[x, 0:128], out_sems.at[8 + x]))
        outs.append(pltpu.make_async_copy(rest_ref, x_any.at[x, 288:320], out_sems.at[12 + x]))
        outs[-2].start()
        outs[-1].start()
    for copy in outs:
        copy.wait()


def products(parts, ref):
    total = dot_t(parts[0], ref[:, 0:128, :].reshape(512, 512))
    total += dot_t(parts[1], ref[:, 128:256, :].reshape(512, 512))
    return total.astype(bf16).reshape(4, 128, 512)


def rows_of(three_ref, last_ref):
    return jnp.concatenate([three_ref[...].reshape(384, 512), last_ref[...]], axis=0)


def own_kernel(own_ref, near_ref, last_ref, far_ref, far_last_ref, out_ref):
    out_ref[...] = products((rows_of(near_ref, last_ref), rows_of(far_ref, far_last_ref)), own_ref)


def other_kernel(
    place_ref, done_ref, own_ref, other_ref, near_ref, last_ref, far_ref, far_last_ref, out_ref, right_ref
):
    core, z_high = place_ref[0], place_ref[2]
    total = products((rows_of(near_ref, last_ref), rows_of(far_ref, far_last_ref)), other_ref)
    for i, k in enumerate((0, 1, 3, 2)):
        out_ref[z_high ^ k, :, 0:512] = done_ref[i]
        out_ref[z_high ^ k, :, 512:1024] = total[i]
    tok, back, singular = [], [], jnp.zeros((1, 128), f32)
    for ref in (own_ref, other_ref):
        for x in range(4):
            rows = ref[x, 256:288, :]
            tok.append(jnp.where(core == 0, rows[:, :256], rows[:, 256:]))
            small = ref[x, 288:304, :].astype(f32)
            back.extend([small[0:8, :256]] * 4)
            singular += small[8:9, 256:384] + small[8:9, 384:512]
    tok = jnp.concatenate(tok, axis=0)
    back = jnp.concatenate(back, axis=0)
    group = lax.rem(lax.broadcasted_iota(jnp.int32, (256, 1), 0), 32) // 8
    for h in range(4):
        both = t_dot(tok, jnp.where(group == h, back, 0.0).astype(bf16))
        a = both[:, :128].reshape(16, 2, 8, 128)[:, 0]
        b = both[:, 128:].reshape(16, 2, 8, 128)[:, 1]
        z = (a + b + singular).reshape(128, 128)
        high = z.astype(bf16).astype(f32)
        out_ref[h, :, 1024:1152] = (high + pltpu.roll(z - high, 64, 1)).astype(bf16)
    right = jnp.zeros((16, 512), f32)
    for ref in (own_ref, other_ref):
        for x in range(4):
            right += ref[x, 304:320, :].astype(f32)
    right_ref[...] = right


def final_kernel(
    place_ref, back_ref, scaled_ref, left_any, keep_ref, inputs_any, grad_left_any, singular_any,
    left_ref, inputs_ref, grad_left_ref, singular_ref, sems,
):
    left_in = pltpu.make_async_copy(left_any, left_ref, sems.at[0])
    left_in.start()
    core = place_ref[0]
    tail = jnp.sum(back_ref[:, :, 1024:].astype(f32), axis=0)
    tail = (tail + pltpu.roll(tail, 64, 1)) / n_dp
    grad_left_ref[0:8, :] = tail[:, 0:16]
    grad_left_ref[8:16, :] = pltpu.roll(tail, 112, 1)[:, 0:16]
    singular_ref[...] = adapter_scale * keep_ref[...] * pltpu.roll(tail, 96, 1)[0:1, 0:16]
    outs = [
        pltpu.make_async_copy(grad_left_ref, grad_left_any, sems.at[1]),
        pltpu.make_async_copy(singular_ref, singular_any, sems.at[2]),
    ]
    outs[0].start()
    outs[1].start()
    left_in.wait()
    scaled = scaled_ref[:, 0:16]
    for h in range(4):
        for low in range(2):
            total = sum(back_ref[h * 16 + i * 2 + low, :, 0:1024].astype(f32) for i in range(8))
            own, other = total[:, :512], total[:, 512:]
            for c, part in enumerate((jnp.where(core == 0, own, other), jnp.where(core == 0, other, own))):
                for x in range(4):
                    at = h * 2048 + x * 512 + c * 256 + low * 128
                    term = jnp.dot(scaled, left_ref[:, at : at + 128], preferred_element_type=f32)
                    inputs_ref[:, at : at + 128] = (part[:, x * 128 : x * 128 + 128] + term).astype(bf16)
    outs.append(pltpu.make_async_copy(inputs_ref, inputs_any, sems.at[3]))
    outs[2].start()
    for copy in outs:
        copy.wait()


def body(inputs, cotangent, weight, left_factor, right_factor, singular, keep_mask):
    core = lax.axis_index("c")
    y_low = lax.axis_index("yl")
    z_high = lax.axis_index("zh")
    place = jnp.stack([core, y_low, z_high]).astype(jnp.int32)
    shape = jax.ShapeDtypeStruct
    keep_float = keep_mask.astype(f32)
    coeff = adapter_scale * singular * keep_float

    got = swap(weight, "yl", 2, 1)

    back_part = dot_t(cotangent, right_factor).reshape(16, 8, 16)
    own_projected = jnp.dot(inputs, left_factor, preferred_element_type=f32)
    rank_out = jnp.pad(back_part, ((0, 0), (0, 0), (0, 112))) + jnp.pad(own_projected, ((0, 0), (16, 96)))
    rank_in = lax.all_to_all(rank_out, ("zl", "yh", "yl"), 0, 0)

    cot = after(cotangent, got)
    cots = [cot] + [swap(cot, "zh", 4, k) for k in (1, 2, 3)]
    near = jnp.stack([cots[0], cots[1], cots[3]])
    far = swap(near, "yl", 2, 1)
    last = cots[2]
    far_last = swap(last, "yl", 2, 1)

    coeff_lanes = jnp.pad(jnp.concatenate([coeff, coeff]), (0, 96)).reshape(1, 128)
    slices = inputs.reshape(8, 4, 4, 512).transpose(2, 1, 0, 3).reshape(4, 32, 512)
    x_out, scaled_back = call(
        pack_kernel,
        (shape((4, 320, 512), bf16), shape((8, 128), bf16)),
        [in_smem] + [in_vmem] * 4 + [anywhere] * 2 + [in_vmem] + [anywhere] * 2,
        16 << 20,
        3 << 20,
        out_specs=(in_hbm, in_vmem),
        scratch=[pltpu.VMEM((128, 512), bf16), pltpu.VMEM((32, 512), bf16), dma, dma((16,))],
    )(place, rank_out, rank_in, coeff_lanes, cot, weight, got, slices, cots[1], cots[3])
    x_in = after(lax.all_to_all(x_out, "x", 0, 0), far, far_last)
    x_other = swap(x_in, "c", 2, 1)

    done = call(own_kernel, shape((4, 128, 512), bf16), [in_vmem] * 5, 1 << 29, 3 << 20)(
        x_in, near, last, far, far_last
    )
    out, right_part = call(
        other_kernel,
        (shape((4, 128, 1152), bf16), shape((16, 512), f32)),
        [in_smem] + [in_vmem] * 7,
        1 << 29,
        5 << 20,
    )(place, done, x_in, x_other, near, last, far, far_last)
    back = lax.all_to_all(out.reshape(64, 8, 1152), ("zh", "zl", "yh", "yl"), 0, 0)
    right_sent = right_part.astype(bf16)
    right_sum = right_part + sum(swap(right_sent, "zh", 4, k).astype(f32) for k in (1, 2, 3))

    grad_inputs, grad_left, grad_singular = call(
        final_kernel,
        (shape((8, 8192), bf16), shape((16, 16), f32), shape((1, 16), f32)),
        [in_smem, in_vmem, in_vmem, in_hbm, in_vmem],
        2 << 20,
        2 << 20,
        out_specs=(in_hbm, in_hbm, in_hbm),
        scratch=[
            pltpu.VMEM((16, 8192), bf16),
            pltpu.VMEM((8, 8192), bf16),
            pltpu.VMEM((16, 16), f32),
            pltpu.VMEM((1, 16), f32),
            dma((4,)),
        ],
    )(place, back, scaled_back, left_factor.T, keep_float.reshape(1, 16))
    grad_right = right_sum / n_dp
    return (grad_inputs, grad_left, grad_right, grad_singular.reshape(16))


def solution(mesh):
    fine = Mesh(mesh.devices.reshape(4, 4, 2, 2, 4, 2), ("zh", "x", "c", "zl", "yh", "yl"))
    dp = ("zh", "x", "c")
    tensor = ("zl", "yh", "yl")
    in_specs = (
        P(dp + tensor, None),
        P(dp, tensor),
        P(dp, tensor),
        P(),
        P(None, tensor),
        P(),
        P(),
    )
    out_specs = (P(dp + tensor, None), P(dp + tensor, None), P(None, tensor), P())
    return jax.shard_map(body, mesh=fine, in_specs=in_specs, out_specs=out_specs, check_vma=False)
```

```python
import jax
import jax.numpy as jnp
from jax import lax
from jax.experimental import pallas as pl
from jax.experimental.pallas import tpu as pltpu
from jax.sharding import Mesh
from jax.sharding import PartitionSpec as P

adapter_scale = 2.0
n_dp = 32
f32 = jnp.float32
bf16 = jnp.bfloat16
in_vmem = pl.BlockSpec(memory_space=pltpu.VMEM)
in_smem = pl.BlockSpec(memory_space=pltpu.SMEM)
anywhere = pl.BlockSpec(memory_space=pl.ANY)
in_hbm = pl.BlockSpec(memory_space=pltpu.HBM)
dma = pltpu.SemaphoreType.DMA


def dot_t(a, b):
    return lax.dot_general(a, b, (((1,), (1,)), ((), ())), preferred_element_type=f32)


def t_dot(a, b):
    return lax.dot_general(a, b, (((0,), (0,)), ((), ())), preferred_element_type=f32)


def swap(a, axis, count, mask):
    return lax.ppermute(a, axis, [(i, i ^ mask) for i in range(count)])


def call(kernel, out_shape, in_specs, flops, moved, out_specs=None, scratch=()):
    return pl.pallas_call(
        kernel,
        out_shape=out_shape,
        in_specs=in_specs,
        out_specs=out_specs or jax.tree.map(lambda _: in_vmem, out_shape),
        scratch_shapes=scratch,
        compiler_params=pltpu.CompilerParams(vmem_limit_bytes=32 << 20),
        cost_estimate=pl.CostEstimate(flops=flops, bytes_accessed=moved, transcendentals=0),
    )


def after(a, *others):
    return pl.pallas_call(
        lambda *refs: None,
        out_shape=jax.ShapeDtypeStruct(a.shape, a.dtype),
        in_specs=[in_vmem] * (1 + len(others)),
        out_specs=in_vmem,
        input_output_aliases={0: 0},
        compiler_params=pltpu.CompilerParams(vmem_limit_bytes=32 << 20),
    )(a, *others)


def pack_kernel(
    place_ref, sent_ref, rank_ref, coeff_ref, cot_ref, weight_any, got_any, slices_ref, after1,
    x_any, back_ref, kept_ref, rest_ref, kept_sem, out_sems,
):
    rows = pl.ds(pl.multiple_of(place_ref[1] * 128, 128), 128)
    kept_in = pltpu.make_async_copy(weight_any.at[rows], kept_ref, kept_sem)
    kept_in.start()
    outs = [pltpu.make_async_copy(got_any.at[rows], x_any.at[x, 128:256], out_sems.at[x]) for x in range(4)]
    outs += [pltpu.make_async_copy(slices_ref.at[x], x_any.at[x, 256:288], out_sems.at[4 + x]) for x in range(4)]
    for copy in outs:
        copy.start()
    lane = lax.broadcasted_iota(jnp.int32, (1, 128), 1)
    rank = rank_ref[...]
    coeff = coeff_ref[...]
    own = jnp.where(lane < 16, jnp.sum(rank, axis=0), 0.0)
    back = (own * coeff).astype(bf16)
    back_ref[...] = back
    fwd = (jnp.where((lane >= 16) & (lane < 32), rank, 0.0) * coeff).astype(bf16)
    right = t_dot(fwd.reshape(128, 128), cot_ref[...])[16:32]
    projected = pltpu.roll(sent_ref[0], 112, 1)
    singular = jnp.broadcast_to(jnp.sum(projected * own, axis=0, keepdims=True), (8, 128))
    high = singular.astype(bf16).astype(f32)
    back8 = back.astype(f32)
    none = jnp.zeros((8, 128), f32)
    small = jnp.concatenate(
        [
            jnp.concatenate([back8, pltpu.roll(back8, 16, 1), none, none], axis=1),
            jnp.concatenate([none, none, pltpu.roll(high, 32, 1), pltpu.roll(singular - high, 32, 1)], axis=1),
        ],
        axis=0,
    ).astype(bf16)
    rest_ref[0:16, :] = small
    rest_ref[16:32, :] = right.astype(bf16)
    kept_in.wait()
    for x in range(4):
        outs.append(pltpu.make_async_copy(kept_ref, x_any.at[x, 0:128], out_sems.at[8 + x]))
        outs.append(pltpu.make_async_copy(rest_ref, x_any.at[x, 288:320], out_sems.at[12 + x]))
        outs[-2].start()
        outs[-1].start()
    for copy in outs:
        copy.wait()


def products(parts, ref):
    total = dot_t(parts[0], ref[:, 0:128, :].reshape(512, 512))
    total += dot_t(parts[1], ref[:, 128:256, :].reshape(512, 512))
    return total.astype(bf16).reshape(4, 128, 512)


def rows_of(first_ref, last_ref):
    return jnp.concatenate([first_ref[...].reshape(256, 512), last_ref[...].reshape(256, 512)], axis=0)


def own_kernel(own_ref, near_ref, last_ref, far_ref, far_last_ref, out_ref):
    out_ref[...] = products((rows_of(near_ref, last_ref), rows_of(far_ref, far_last_ref)), own_ref)


def other_kernel(
    place_ref, done_ref, own_ref, other_ref, near_ref, last_ref, far_ref, far_last_ref, out_ref, right_ref
):
    core, z_high = place_ref[0], place_ref[2]
    total = products((rows_of(near_ref, last_ref), rows_of(far_ref, far_last_ref)), other_ref)
    for k in range(4):
        out_ref[z_high ^ k, :, 0:512] = done_ref[k]
        out_ref[z_high ^ k, :, 512:1024] = total[k]
    tok, back, singular = [], [], jnp.zeros((1, 128), f32)
    for ref in (own_ref, other_ref):
        for x in range(4):
            rows = ref[x, 256:288, :]
            tok.append(jnp.where(core == 0, rows[:, :256], rows[:, 256:]))
            small = ref[x, 288:304, :].astype(f32)
            back.extend([small[0:8, :256]] * 4)
            singular += small[8:9, 256:384] + small[8:9, 384:512]
    tok = jnp.concatenate(tok, axis=0)
    back = jnp.concatenate(back, axis=0)
    group = lax.rem(lax.broadcasted_iota(jnp.int32, (256, 1), 0), 32) // 8
    for h in range(4):
        both = t_dot(tok, jnp.where(group == h, back, 0.0).astype(bf16))
        a = both[:, :128].reshape(16, 2, 8, 128)[:, 0]
        b = both[:, 128:].reshape(16, 2, 8, 128)[:, 1]
        z = (a + b + singular).reshape(128, 128)
        high = z.astype(bf16).astype(f32)
        out_ref[h, :, 1024:1152] = (high + pltpu.roll(z - high, 64, 1)).astype(bf16)
    right = jnp.zeros((16, 512), f32)
    for ref in (own_ref, other_ref):
        for x in range(4):
            right += ref[x, 304:320, :].astype(f32)
    right_ref[...] = right


def final_kernel(
    place_ref, back_ref, scaled_ref, left_any, keep_ref, inputs_any, grad_left_any, singular_any,
    left_ref, inputs_ref, grad_left_ref, singular_ref, sems,
):
    left_in = pltpu.make_async_copy(left_any, left_ref, sems.at[0])
    left_in.start()
    core = place_ref[0]
    tail = jnp.sum(back_ref[:, :, 1024:].astype(f32), axis=0)
    tail = (tail + pltpu.roll(tail, 64, 1)) / n_dp
    grad_left_ref[0:8, :] = tail[:, 0:16]
    grad_left_ref[8:16, :] = pltpu.roll(tail, 112, 1)[:, 0:16]
    singular_ref[...] = adapter_scale * keep_ref[...] * pltpu.roll(tail, 96, 1)[0:1, 0:16]
    outs = [
        pltpu.make_async_copy(grad_left_ref, grad_left_any, sems.at[1]),
        pltpu.make_async_copy(singular_ref, singular_any, sems.at[2]),
    ]
    outs[0].start()
    outs[1].start()
    left_in.wait()
    scaled = scaled_ref[:, 0:16]
    for h in range(4):
        for low in range(2):
            total = sum(back_ref[h * 16 + i * 2 + low, :, 0:1024].astype(f32) for i in range(8))
            own, other = total[:, :512], total[:, 512:]
            for c, part in enumerate((jnp.where(core == 0, own, other), jnp.where(core == 0, other, own))):
                for x in range(4):
                    at = h * 2048 + x * 512 + c * 256 + low * 128
                    term = jnp.dot(scaled, left_ref[:, at : at + 128], preferred_element_type=f32)
                    inputs_ref[:, at : at + 128] = (part[:, x * 128 : x * 128 + 128] + term).astype(bf16)
    outs.append(pltpu.make_async_copy(inputs_ref, inputs_any, sems.at[3]))
    outs[2].start()
    for copy in outs:
        copy.wait()


def body(inputs, cotangent, weight, left_factor, right_factor, singular, keep_mask):
    core = lax.axis_index("c")
    y_low = lax.axis_index("yl")
    z_high = lax.axis_index("zh")
    place = jnp.stack([core, y_low, z_high]).astype(jnp.int32)
    shape = jax.ShapeDtypeStruct
    keep_float = keep_mask.astype(f32)
    coeff = adapter_scale * singular * keep_float

    got = swap(weight, "yl", 2, 1)

    back_part = dot_t(cotangent, right_factor).reshape(16, 8, 16)
    own_projected = jnp.dot(inputs, left_factor, preferred_element_type=f32)
    rank_out = jnp.pad(back_part, ((0, 0), (0, 0), (0, 112))) + jnp.pad(own_projected, ((0, 0), (16, 96)))
    rank_in = lax.all_to_all(rank_out, ("zl", "yh", "yl"), 0, 0)

    cot = after(cotangent, got)
    cots = [cot] + [swap(cot, "zh", 4, k) for k in (1, 2, 3)]
    near = jnp.stack(cots[:2])
    far = swap(near, "yl", 2, 1)
    last = jnp.stack(cots[2:])
    far_last = swap(last, "yl", 2, 1)

    coeff_lanes = jnp.pad(jnp.concatenate([coeff, coeff]), (0, 96)).reshape(1, 128)
    slices = inputs.reshape(8, 4, 4, 512).transpose(2, 1, 0, 3).reshape(4, 32, 512)
    x_out, scaled_back = call(
        pack_kernel,
        (shape((4, 320, 512), bf16), shape((8, 128), bf16)),
        [in_smem] + [in_vmem] * 4 + [anywhere] * 2 + [in_vmem] + [anywhere],
        16 << 20,
        3 << 20,
        out_specs=(in_hbm, in_vmem),
        scratch=[pltpu.VMEM((128, 512), bf16), pltpu.VMEM((32, 512), bf16), dma, dma((16,))],
    )(place, rank_out, rank_in, coeff_lanes, cot, weight, got, slices, cots[1])
    x_in = after(lax.all_to_all(x_out, "x", 0, 0), far, far_last)
    x_other = swap(x_in, "c", 2, 1)

    done = call(own_kernel, shape((4, 128, 512), bf16), [in_vmem] * 5, 1 << 29, 3 << 20)(
        x_in, near, last, far, far_last
    )
    out, right_part = call(
        other_kernel,
        (shape((4, 128, 1152), bf16), shape((16, 512), f32)),
        [in_smem] + [in_vmem] * 7,
        1 << 29,
        5 << 20,
    )(place, done, x_in, x_other, near, last, far, far_last)
    back = lax.all_to_all(out.reshape(64, 8, 1152), ("zh", "zl", "yh", "yl"), 0, 0)
    right_sent = right_part.astype(bf16)
    right_sum = right_part + sum(swap(right_sent, "zh", 4, k).astype(f32) for k in (1, 2, 3))

    grad_inputs, grad_left, grad_singular = call(
        final_kernel,
        (shape((8, 8192), bf16), shape((16, 16), f32), shape((1, 16), f32)),
        [in_smem, in_vmem, in_vmem, in_hbm, in_vmem],
        2 << 20,
        2 << 20,
        out_specs=(in_hbm, in_hbm, in_hbm),
        scratch=[
            pltpu.VMEM((16, 8192), bf16),
            pltpu.VMEM((8, 8192), bf16),
            pltpu.VMEM((16, 16), f32),
            pltpu.VMEM((1, 16), f32),
            dma((4,)),
        ],
    )(place, back, scaled_back, left_factor.T, keep_float.reshape(1, 16))
    grad_right = right_sum / n_dp
    return (grad_inputs, grad_left, grad_right, grad_singular.reshape(16))


def solution(mesh):
    fine = Mesh(mesh.devices.reshape(4, 4, 2, 2, 4, 2), ("zh", "x", "c", "zl", "yh", "yl"))
    dp = ("zh", "x", "c")
    tensor = ("zl", "yh", "yl")
    in_specs = (
        P(dp + tensor, None),
        P(dp, tensor),
        P(dp, tensor),
        P(),
        P(None, tensor),
        P(),
        P(),
    )
    out_specs = (P(dp + tensor, None), P(dp + tensor, None), P(None, tensor), P())
    return jax.shard_map(body, mesh=fine, in_specs=in_specs, out_specs=out_specs, check_vma=False)
```

```python
import jax
import jax.numpy as jnp
from jax import lax
from jax.experimental import pallas as pl
from jax.experimental.pallas import tpu as pltpu
from jax.sharding import Mesh
from jax.sharding import PartitionSpec as P

adapter_scale = 2.0
n_dp = 32
f32 = jnp.float32
bf16 = jnp.bfloat16
in_vmem = pl.BlockSpec(memory_space=pltpu.VMEM)
in_smem = pl.BlockSpec(memory_space=pltpu.SMEM)
anywhere = pl.BlockSpec(memory_space=pl.ANY)
in_hbm = pl.BlockSpec(memory_space=pltpu.HBM)
dma = pltpu.SemaphoreType.DMA


def dot_t(a, b):
    return lax.dot_general(a, b, (((1,), (1,)), ((), ())), preferred_element_type=f32)


def t_dot(a, b):
    return lax.dot_general(a, b, (((0,), (0,)), ((), ())), preferred_element_type=f32)


def swap(a, axis, count, mask):
    return lax.ppermute(a, axis, [(i, i ^ mask) for i in range(count)])


def call(kernel, out_shape, in_specs, flops, moved, out_specs=None, scratch=()):
    return pl.pallas_call(
        kernel,
        out_shape=out_shape,
        in_specs=in_specs,
        out_specs=out_specs or jax.tree.map(lambda _: in_vmem, out_shape),
        scratch_shapes=scratch,
        compiler_params=pltpu.CompilerParams(vmem_limit_bytes=32 << 20),
        cost_estimate=pl.CostEstimate(flops=flops, bytes_accessed=moved, transcendentals=0),
    )


def after(a, *others):
    return pl.pallas_call(
        lambda *refs: None,
        out_shape=jax.ShapeDtypeStruct(a.shape, a.dtype),
        in_specs=[in_vmem] * (1 + len(others)),
        out_specs=in_vmem,
        input_output_aliases={0: 0},
        compiler_params=pltpu.CompilerParams(vmem_limit_bytes=32 << 20),
    )(a, *others)


def stack_kernel(c0_ref, c1_ref, c2_ref, c3_ref, out_ref):
    for k, ref in enumerate((c0_ref, c1_ref, c2_ref, c3_ref)):
        out_ref[k] = ref[...]


def pack_kernel(
    place_ref, sent_ref, rank_ref, coeff_ref, cot_ref, weight_any, got_any, slices_ref,
    x_any, back_ref, kept_ref, rest_ref, kept_sem, out_sems,
):
    rows = pl.ds(pl.multiple_of(place_ref[1] * 128, 128), 128)
    kept_in = pltpu.make_async_copy(weight_any.at[rows], kept_ref, kept_sem)
    kept_in.start()
    outs = [pltpu.make_async_copy(got_any.at[rows], x_any.at[x, 128:256], out_sems.at[x]) for x in range(4)]
    outs += [pltpu.make_async_copy(slices_ref.at[x], x_any.at[x, 256:288], out_sems.at[4 + x]) for x in range(4)]
    for copy in outs:
        copy.start()
    lane = lax.broadcasted_iota(jnp.int32, (1, 128), 1)
    rank = rank_ref[...]
    coeff = coeff_ref[...]
    own = jnp.where(lane < 16, jnp.sum(rank, axis=0), 0.0)
    back = (own * coeff).astype(bf16)
    back_ref[...] = back
    fwd = (jnp.where((lane >= 16) & (lane < 32), rank, 0.0) * coeff).astype(bf16)
    right = t_dot(fwd.reshape(128, 128), cot_ref[...])[16:32]
    projected = pltpu.roll(sent_ref[0], 112, 1)
    singular = jnp.broadcast_to(jnp.sum(projected * own, axis=0, keepdims=True), (8, 128))
    high = singular.astype(bf16).astype(f32)
    back8 = back.astype(f32)
    none = jnp.zeros((8, 128), f32)
    small = jnp.concatenate(
        [
            jnp.concatenate([back8, pltpu.roll(back8, 16, 1), none, none], axis=1),
            jnp.concatenate([none, none, pltpu.roll(high, 32, 1), pltpu.roll(singular - high, 32, 1)], axis=1),
        ],
        axis=0,
    ).astype(bf16)
    rest_ref[0:16, :] = small
    rest_ref[16:32, :] = right.astype(bf16)
    kept_in.wait()
    for x in range(4):
        outs.append(pltpu.make_async_copy(kept_ref, x_any.at[x, 0:128], out_sems.at[8 + x]))
        outs.append(pltpu.make_async_copy(rest_ref, x_any.at[x, 288:320], out_sems.at[12 + x]))
        outs[-2].start()
        outs[-1].start()
    for copy in outs:
        copy.wait()


def products(parts, ref):
    total = dot_t(parts[0], ref[:, 0:128, :].reshape(512, 512))
    total += dot_t(parts[1], ref[:, 128:256, :].reshape(512, 512))
    return total.astype(bf16).reshape(4, 128, 512)


def own_kernel(own_ref, near_ref, far_ref, out_ref):
    out_ref[...] = products((near_ref[...].reshape(512, 512), far_ref[...].reshape(512, 512)), own_ref)


def other_kernel(
    place_ref, done_ref, own_ref, other_ref, near_ref, far_ref, out_ref, right_ref
):
    core, z_high = place_ref[0], place_ref[2]
    total = products((near_ref[...].reshape(512, 512), far_ref[...].reshape(512, 512)), other_ref)
    for k in range(4):
        out_ref[z_high ^ k, :, 0:512] = done_ref[k]
        out_ref[z_high ^ k, :, 512:1024] = total[k]
    tok, back, singular = [], [], jnp.zeros((1, 128), f32)
    for ref in (own_ref, other_ref):
        for x in range(4):
            rows = ref[x, 256:288, :]
            tok.append(jnp.where(core == 0, rows[:, :256], rows[:, 256:]))
            small = ref[x, 288:304, :].astype(f32)
            back.extend([small[0:8, :256]] * 4)
            singular += small[8:9, 256:384] + small[8:9, 384:512]
    tok = jnp.concatenate(tok, axis=0)
    back = jnp.concatenate(back, axis=0)
    group = lax.rem(lax.broadcasted_iota(jnp.int32, (256, 1), 0), 32) // 8
    for h in range(4):
        both = t_dot(tok, jnp.where(group == h, back, 0.0).astype(bf16))
        a = both[:, :128].reshape(16, 2, 8, 128)[:, 0]
        b = both[:, 128:].reshape(16, 2, 8, 128)[:, 1]
        z = (a + b + singular).reshape(128, 128)
        high = z.astype(bf16).astype(f32)
        out_ref[h, :, 1024:1152] = (high + pltpu.roll(z - high, 64, 1)).astype(bf16)
    right = jnp.zeros((16, 512), f32)
    for ref in (own_ref, other_ref):
        for x in range(4):
            right += ref[x, 304:320, :].astype(f32)
    right_ref[...] = right


def final_kernel(
    place_ref, back_ref, scaled_ref, left_any, keep_ref, inputs_any, grad_left_any, singular_any,
    left_ref, inputs_ref, grad_left_ref, singular_ref, sems,
):
    left_in = pltpu.make_async_copy(left_any, left_ref, sems.at[0])
    left_in.start()
    core = place_ref[0]
    tail = jnp.sum(back_ref[:, :, 1024:].astype(f32), axis=0)
    tail = (tail + pltpu.roll(tail, 64, 1)) / n_dp
    grad_left_ref[0:8, :] = tail[:, 0:16]
    grad_left_ref[8:16, :] = pltpu.roll(tail, 112, 1)[:, 0:16]
    singular_ref[...] = adapter_scale * keep_ref[...] * pltpu.roll(tail, 96, 1)[0:1, 0:16]
    outs = [
        pltpu.make_async_copy(grad_left_ref, grad_left_any, sems.at[1]),
        pltpu.make_async_copy(singular_ref, singular_any, sems.at[2]),
    ]
    outs[0].start()
    outs[1].start()
    left_in.wait()
    scaled = scaled_ref[:, 0:16]
    for h in range(4):
        for low in range(2):
            total = sum(back_ref[h * 16 + i * 2 + low, :, 0:1024].astype(f32) for i in range(8))
            own, other = total[:, :512], total[:, 512:]
            for c, part in enumerate((jnp.where(core == 0, own, other), jnp.where(core == 0, other, own))):
                for x in range(4):
                    at = h * 2048 + x * 512 + c * 256 + low * 128
                    term = jnp.dot(scaled, left_ref[:, at : at + 128], preferred_element_type=f32)
                    inputs_ref[:, at : at + 128] = (part[:, x * 128 : x * 128 + 128] + term).astype(bf16)
    outs.append(pltpu.make_async_copy(inputs_ref, inputs_any, sems.at[3]))
    outs[2].start()
    for copy in outs:
        copy.wait()


def body(inputs, cotangent, weight, left_factor, right_factor, singular, keep_mask):
    core = lax.axis_index("c")
    y_low = lax.axis_index("yl")
    z_high = lax.axis_index("zh")
    place = jnp.stack([core, y_low, z_high]).astype(jnp.int32)
    shape = jax.ShapeDtypeStruct
    keep_float = keep_mask.astype(f32)
    coeff = adapter_scale * singular * keep_float

    got = swap(weight, "yl", 2, 1)

    back_part = dot_t(cotangent, right_factor).reshape(16, 8, 16)
    own_projected = jnp.dot(inputs, left_factor, preferred_element_type=f32)
    rank_out = jnp.pad(back_part, ((0, 0), (0, 0), (0, 112))) + jnp.pad(own_projected, ((0, 0), (16, 96)))
    rank_in = lax.all_to_all(rank_out, ("zl", "yh", "yl"), 0, 0)

    cot = after(cotangent, got)
    cots = [cot] + [swap(cot, "zh", 4, k) for k in (1, 2, 3)]
    near = call(stack_kernel, shape((4, 128, 512), bf16), [in_vmem] * 4, 30 << 30, 1 << 20)(*cots)
    far = swap(near, "yl", 2, 1)

    coeff_lanes = jnp.pad(jnp.concatenate([coeff, coeff]), (0, 96)).reshape(1, 128)
    slices = inputs.reshape(8, 4, 4, 512).transpose(2, 1, 0, 3).reshape(4, 32, 512)
    x_out, scaled_back = call(
        pack_kernel,
        (shape((4, 320, 512), bf16), shape((8, 128), bf16)),
        [in_smem] + [in_vmem] * 4 + [anywhere] * 2 + [in_vmem],
        30 << 30,
        3 << 20,
        out_specs=(in_hbm, in_vmem),
        scratch=[pltpu.VMEM((128, 512), bf16), pltpu.VMEM((32, 512), bf16), dma, dma((16,))],
    )(place, rank_out, rank_in, coeff_lanes, cot, weight, got, slices)
    x_in = after(lax.all_to_all(x_out, "x", 0, 0), far)
    x_other = swap(x_in, "c", 2, 1)

    done = call(own_kernel, shape((4, 128, 512), bf16), [in_vmem] * 3, 1 << 29, 3 << 20)(x_in, near, far)
    out, right_part = call(
        other_kernel,
        (shape((4, 128, 1152), bf16), shape((16, 512), f32)),
        [in_smem] + [in_vmem] * 5,
        1 << 29,
        5 << 20,
    )(place, done, x_in, x_other, near, far)
    back = lax.all_to_all(out.reshape(64, 8, 1152), ("zh", "zl", "yh", "yl"), 0, 0)
    right_sent = right_part.astype(bf16)
    right_sum = right_part + sum(swap(right_sent, "zh", 4, k).astype(f32) for k in (1, 2, 3))

    grad_inputs, grad_left, grad_singular = call(
        final_kernel,
        (shape((8, 8192), bf16), shape((16, 16), f32), shape((1, 16), f32)),
        [in_smem, in_vmem, in_vmem, in_hbm, in_vmem],
        2 << 20,
        2 << 20,
        out_specs=(in_hbm, in_hbm, in_hbm),
        scratch=[
            pltpu.VMEM((16, 8192), bf16),
            pltpu.VMEM((8, 8192), bf16),
            pltpu.VMEM((16, 16), f32),
            pltpu.VMEM((1, 16), f32),
            dma((4,)),
        ],
    )(place, back, scaled_back, left_factor.T, keep_float.reshape(1, 16))
    grad_right = right_sum / n_dp
    return (grad_inputs, grad_left, grad_right, grad_singular.reshape(16))


def solution(mesh):
    fine = Mesh(mesh.devices.reshape(4, 4, 2, 2, 4, 2), ("zh", "x", "c", "zl", "yh", "yl"))
    dp = ("zh", "x", "c")
    tensor = ("zl", "yh", "yl")
    in_specs = (
        P(dp + tensor, None),
        P(dp, tensor),
        P(dp, tensor),
        P(),
        P(None, tensor),
        P(),
        P(),
    )
    out_specs = (P(dp + tensor, None), P(dp + tensor, None), P(None, tensor), P())
    return jax.shard_map(body, mesh=fine, in_specs=in_specs, out_specs=out_specs, check_vma=False)
```

```python
import jax
import jax.numpy as jnp
from jax import lax
from jax.experimental import pallas as pl
from jax.experimental.pallas import tpu as pltpu
from jax.sharding import Mesh
from jax.sharding import PartitionSpec as P

adapter_scale = 2.0
n_dp = 32
f32 = jnp.float32
bf16 = jnp.bfloat16
in_vmem = pl.BlockSpec(memory_space=pltpu.VMEM)
in_smem = pl.BlockSpec(memory_space=pltpu.SMEM)
anywhere = pl.BlockSpec(memory_space=pl.ANY)
in_hbm = pl.BlockSpec(memory_space=pltpu.HBM)
dma = pltpu.SemaphoreType.DMA


def dot_t(a, b):
    return lax.dot_general(a, b, (((1,), (1,)), ((), ())), preferred_element_type=f32)


def t_dot(a, b):
    return lax.dot_general(a, b, (((0,), (0,)), ((), ())), preferred_element_type=f32)


def swap(a, axis, count, mask):
    return lax.ppermute(a, axis, [(i, i ^ mask) for i in range(count)])


def call(kernel, out_shape, in_specs, flops, moved, out_specs=None, scratch=()):
    return pl.pallas_call(
        kernel,
        out_shape=out_shape,
        in_specs=in_specs,
        out_specs=out_specs or jax.tree.map(lambda _: in_vmem, out_shape),
        scratch_shapes=scratch,
        compiler_params=pltpu.CompilerParams(vmem_limit_bytes=32 << 20),
        cost_estimate=pl.CostEstimate(flops=flops, bytes_accessed=moved, transcendentals=0),
    )


def after(a, *others):
    return pl.pallas_call(
        lambda *refs: None,
        out_shape=jax.ShapeDtypeStruct(a.shape, a.dtype),
        in_specs=[in_vmem] * (1 + len(others)),
        out_specs=in_vmem,
        input_output_aliases={0: 0},
        compiler_params=pltpu.CompilerParams(vmem_limit_bytes=32 << 20),
    )(a, *others)


def copy_kernel(in_ref, out_ref):
    out_ref[...] = in_ref[...]


def rows_of(first_ref, last_ref):
    return jnp.concatenate([first_ref[...].reshape(256, 512), last_ref[...].reshape(256, 512)], axis=0)


def pack_kernel(
    place_ref, sent_ref, rank_ref, coeff_ref, cot_ref, weight_any, got_any, slices_ref,
    x_any, back_ref, rest_ref, out_sems,
):
    rows = pl.ds(pl.multiple_of(place_ref[1] * 128, 128), 128)
    outs = [pltpu.make_async_copy(got_any.at[rows], x_any.at[x, 128:256], out_sems.at[x]) for x in range(4)]
    outs += [pltpu.make_async_copy(weight_any.at[rows], x_any.at[x, 0:128], out_sems.at[8 + x]) for x in range(4)]
    outs += [pltpu.make_async_copy(slices_ref.at[x], x_any.at[x, 256:288], out_sems.at[4 + x]) for x in range(4)]
    for copy in outs:
        copy.start()
    lane = lax.broadcasted_iota(jnp.int32, (1, 128), 1)
    rank = rank_ref[...]
    coeff = coeff_ref[...]
    own = jnp.where(lane < 16, jnp.sum(rank, axis=0), 0.0)
    back = (own * coeff).astype(bf16)
    back_ref[...] = back
    fwd = (jnp.where((lane >= 16) & (lane < 32), rank, 0.0) * coeff).astype(bf16)
    right = t_dot(fwd.reshape(128, 128), cot_ref[...])[16:32]
    projected = pltpu.roll(sent_ref[0], 112, 1)
    singular = jnp.broadcast_to(jnp.sum(projected * own, axis=0, keepdims=True), (8, 128))
    high = singular.astype(bf16).astype(f32)
    back8 = back.astype(f32)
    none = jnp.zeros((8, 128), f32)
    small = jnp.concatenate(
        [
            jnp.concatenate([back8, pltpu.roll(back8, 16, 1), none, none], axis=1),
            jnp.concatenate([none, none, pltpu.roll(high, 32, 1), pltpu.roll(singular - high, 32, 1)], axis=1),
        ],
        axis=0,
    ).astype(bf16)
    rest_ref[0:16, :] = small
    rest_ref[16:32, :] = right.astype(bf16)
    for x in range(4):
        outs.append(pltpu.make_async_copy(rest_ref, x_any.at[x, 288:320], out_sems.at[12 + x]))
        outs[-1].start()
    for copy in outs:
        copy.wait()


def products(parts, ref):
    total = dot_t(parts[0], ref[:, 0:128, :].reshape(512, 512))
    total += dot_t(parts[1], ref[:, 128:256, :].reshape(512, 512))
    return total.astype(bf16).reshape(4, 128, 512)


def own_kernel(own_ref, near_ref, last_ref, far_ref, far_last_ref, out_ref):
    out_ref[...] = products((rows_of(near_ref, last_ref), rows_of(far_ref, far_last_ref)), own_ref)


def other_kernel(
    place_ref, done_ref, own_ref, other_ref, near_ref, last_ref, far_ref, far_last_ref, out_ref, right_ref
):
    core, z_high = place_ref[0], place_ref[2]
    total = products((rows_of(near_ref, last_ref), rows_of(far_ref, far_last_ref)), other_ref)
    for i, k in enumerate((0, 1, 3, 2)):
        out_ref[z_high ^ k, :, 0:512] = done_ref[i]
        out_ref[z_high ^ k, :, 512:1024] = total[i]
    tok, back, singular = [], [], jnp.zeros((1, 128), f32)
    for ref in (own_ref, other_ref):
        for x in range(4):
            rows = ref[x, 256:288, :]
            tok.append(jnp.where(core == 0, rows[:, :256], rows[:, 256:]))
            small = ref[x, 288:304, :].astype(f32)
            back.extend([small[0:8, :256]] * 4)
            singular += small[8:9, 256:384] + small[8:9, 384:512]
    tok = jnp.concatenate(tok, axis=0)
    back = jnp.concatenate(back, axis=0)
    group = lax.rem(lax.broadcasted_iota(jnp.int32, (256, 1), 0), 32) // 8
    for h in range(4):
        both = t_dot(tok, jnp.where(group == h, back, 0.0).astype(bf16))
        a = both[:, :128].reshape(16, 2, 8, 128)[:, 0]
        b = both[:, 128:].reshape(16, 2, 8, 128)[:, 1]
        z = (a + b + singular).reshape(128, 128)
        high = z.astype(bf16).astype(f32)
        out_ref[h, :, 1024:1152] = (high + pltpu.roll(z - high, 64, 1)).astype(bf16)
    right = jnp.zeros((16, 512), f32)
    for ref in (own_ref, other_ref):
        for x in range(4):
            right += ref[x, 304:320, :].astype(f32)
    right_ref[...] = right


def final_kernel(
    place_ref, back_ref, scaled_ref, left_any, keep_ref, inputs_any, grad_left_any, singular_any,
    left_ref, inputs_ref, grad_left_ref, singular_ref, sems,
):
    left_in = pltpu.make_async_copy(left_any, left_ref, sems.at[0])
    left_in.start()
    core = place_ref[0]
    tail = jnp.sum(back_ref[:, :, 1024:].astype(f32), axis=0)
    tail = (tail + pltpu.roll(tail, 64, 1)) / n_dp
    grad_left_ref[0:8, :] = tail[:, 0:16]
    grad_left_ref[8:16, :] = pltpu.roll(tail, 112, 1)[:, 0:16]
    singular_ref[...] = adapter_scale * keep_ref[...] * pltpu.roll(tail, 96, 1)[0:1, 0:16]
    outs = [
        pltpu.make_async_copy(grad_left_ref, grad_left_any, sems.at[1]),
        pltpu.make_async_copy(singular_ref, singular_any, sems.at[2]),
    ]
    outs[0].start()
    outs[1].start()
    left_in.wait()
    scaled = scaled_ref[:, 0:16]
    for h in range(4):
        for low in range(2):
            total = sum(back_ref[h * 16 + i * 2 + low, :, 0:1024].astype(f32) for i in range(8))
            own, other = total[:, :512], total[:, 512:]
            for c, part in enumerate((jnp.where(core == 0, own, other), jnp.where(core == 0, other, own))):
                for x in range(4):
                    at = h * 2048 + x * 512 + c * 256 + low * 128
                    term = jnp.dot(scaled, left_ref[:, at : at + 128], preferred_element_type=f32)
                    inputs_ref[:, at : at + 128] = (part[:, x * 128 : x * 128 + 128] + term).astype(bf16)
    outs.append(pltpu.make_async_copy(inputs_ref, inputs_any, sems.at[3]))
    outs[2].start()
    for copy in outs:
        copy.wait()


def body(inputs, cotangent, weight, left_factor, right_factor, singular, keep_mask):
    core = lax.axis_index("c")
    y_low = lax.axis_index("yl")
    z_high = lax.axis_index("zh")
    place = jnp.stack([core, y_low, z_high]).astype(jnp.int32)
    shape = jax.ShapeDtypeStruct
    keep_float = keep_mask.astype(f32)
    coeff = adapter_scale * singular * keep_float

    got = swap(weight, "yl", 2, 1)

    back_part = dot_t(cotangent, right_factor).reshape(16, 8, 16)
    own_projected = jnp.dot(inputs, left_factor, preferred_element_type=f32)
    rank_out = jnp.pad(back_part, ((0, 0), (0, 0), (0, 112))) + jnp.pad(own_projected, ((0, 0), (16, 96)))
    rank_in = lax.all_to_all(rank_out, ("zl", "yh", "yl"), 0, 0)

    cot = after(cotangent, got)
    near = jnp.stack([cot, swap(cot, "zh", 4, 1)])
    far = swap(near, "yl", 2, 1)
    last = call(copy_kernel, shape((2, 128, 512), bf16), [in_vmem], 30 << 30, 1 << 20)(swap(near, "zh", 4, 3))
    far_last = swap(last, "yl", 2, 1)

    coeff_lanes = jnp.pad(jnp.concatenate([coeff, coeff]), (0, 96)).reshape(1, 128)
    slices = inputs.reshape(8, 4, 4, 512).transpose(2, 1, 0, 3).reshape(4, 32, 512)
    x_out, scaled_back = call(
        pack_kernel,
        (shape((4, 320, 512), bf16), shape((8, 128), bf16)),
        [in_smem] + [in_vmem] * 4 + [anywhere] * 2 + [in_vmem],
        30 << 30,
        3 << 20,
        out_specs=(in_hbm, in_vmem),
        scratch=[pltpu.VMEM((32, 512), bf16), dma((16,))],
    )(place, rank_out, rank_in, coeff_lanes, cot, weight, got, slices)
    x_in = after(lax.all_to_all(x_out, "x", 0, 0), far, far_last)
    x_other = swap(x_in, "c", 2, 1)

    done = call(own_kernel, shape((4, 128, 512), bf16), [in_vmem] * 5, 1 << 29, 3 << 20)(
        x_in, near, last, far, far_last
    )
    out, right_part = call(
        other_kernel,
        (shape((4, 128, 1152), bf16), shape((16, 512), f32)),
        [in_smem] + [in_vmem] * 7,
        1 << 29,
        5 << 20,
    )(place, done, x_in, x_other, near, last, far, far_last)
    back = lax.all_to_all(out.reshape(64, 8, 1152), ("zh", "zl", "yh", "yl"), 0, 0)
    right_sent = right_part.astype(bf16)
    right_sum = right_part + sum(swap(right_sent, "zh", 4, k).astype(f32) for k in (1, 2, 3))

    grad_inputs, grad_left, grad_singular = call(
        final_kernel,
        (shape((8, 8192), bf16), shape((16, 16), f32), shape((1, 16), f32)),
        [in_smem, in_vmem, in_vmem, in_hbm, in_vmem],
        2 << 20,
        2 << 20,
        out_specs=(in_hbm, in_hbm, in_hbm),
        scratch=[
            pltpu.VMEM((16, 8192), bf16),
            pltpu.VMEM((8, 8192), bf16),
            pltpu.VMEM((16, 16), f32),
            pltpu.VMEM((1, 16), f32),
            dma((4,)),
        ],
    )(place, back, scaled_back, left_factor.T, keep_float.reshape(1, 16))
    grad_right = right_sum / n_dp
    return (grad_inputs, grad_left, grad_right, grad_singular.reshape(16))


def solution(mesh):
    fine = Mesh(mesh.devices.reshape(4, 4, 2, 2, 4, 2), ("zh", "x", "c", "zl", "yh", "yl"))
    dp = ("zh", "x", "c")
    tensor = ("zl", "yh", "yl")
    in_specs = (
        P(dp + tensor, None),
        P(dp, tensor),
        P(dp, tensor),
        P(),
        P(None, tensor),
        P(),
        P(),
    )
    out_specs = (P(dp + tensor, None), P(dp + tensor, None), P(None, tensor), P())
    return jax.shard_map(body, mesh=fine, in_specs=in_specs, out_specs=out_specs, check_vma=False)
```

```python
import jax
import jax.numpy as jnp
from jax import lax
from jax.experimental import pallas as pl
from jax.experimental.pallas import tpu as pltpu
from jax.sharding import Mesh
from jax.sharding import PartitionSpec as P

adapter_scale = 2.0
n_dp = 32
f32 = jnp.float32
bf16 = jnp.bfloat16
in_vmem = pl.BlockSpec(memory_space=pltpu.VMEM)
in_smem = pl.BlockSpec(memory_space=pltpu.SMEM)
anywhere = pl.BlockSpec(memory_space=pl.ANY)
in_hbm = pl.BlockSpec(memory_space=pltpu.HBM)
dma = pltpu.SemaphoreType.DMA


def dot_t(a, b):
    return lax.dot_general(a, b, (((1,), (1,)), ((), ())), preferred_element_type=f32)


def t_dot(a, b):
    return lax.dot_general(a, b, (((0,), (0,)), ((), ())), preferred_element_type=f32)


def swap(a, axis, count, mask):
    return lax.ppermute(a, axis, [(i, i ^ mask) for i in range(count)])


def call(kernel, out_shape, in_specs, flops, moved, out_specs=None, scratch=()):
    return pl.pallas_call(
        kernel,
        out_shape=out_shape,
        in_specs=in_specs,
        out_specs=out_specs or jax.tree.map(lambda _: in_vmem, out_shape),
        scratch_shapes=scratch,
        compiler_params=pltpu.CompilerParams(vmem_limit_bytes=32 << 20),
        cost_estimate=pl.CostEstimate(flops=flops, bytes_accessed=moved, transcendentals=0),
    )


def after(a, *others):
    return pl.pallas_call(
        lambda *refs: None,
        out_shape=jax.ShapeDtypeStruct(a.shape, a.dtype),
        in_specs=[in_vmem] * (1 + len(others)),
        out_specs=in_vmem,
        input_output_aliases={0: 0},
        compiler_params=pltpu.CompilerParams(vmem_limit_bytes=32 << 20),
    )(a, *others)


def stack_kernel(first_ref, second_ref, out_ref):
    out_ref[0] = first_ref[...]
    out_ref[1] = second_ref[...]


def rows_of(first_ref, last_ref):
    return jnp.concatenate([first_ref[...].reshape(256, 512), last_ref[...].reshape(256, 512)], axis=0)


def pack_kernel(
    place_ref, sent_ref, rank_ref, coeff_ref, cot_ref, weight_any, got_any, slices_ref,
    x_any, back_ref, rest_ref, out_sems,
):
    rows = pl.ds(pl.multiple_of(place_ref[1] * 128, 128), 128)
    outs = [pltpu.make_async_copy(got_any.at[rows], x_any.at[x, 128:256], out_sems.at[x]) for x in range(4)]
    outs += [pltpu.make_async_copy(weight_any.at[rows], x_any.at[x, 0:128], out_sems.at[8 + x]) for x in range(4)]
    outs += [pltpu.make_async_copy(slices_ref.at[x], x_any.at[x, 256:288], out_sems.at[4 + x]) for x in range(4)]
    for copy in outs:
        copy.start()
    lane = lax.broadcasted_iota(jnp.int32, (1, 128), 1)
    rank = rank_ref[...]
    coeff = coeff_ref[...]
    own = jnp.where(lane < 16, jnp.sum(rank, axis=0), 0.0)
    back = (own * coeff).astype(bf16)
    back_ref[...] = back
    fwd = (jnp.where((lane >= 16) & (lane < 32), rank, 0.0) * coeff).astype(bf16)
    right = t_dot(fwd.reshape(128, 128), cot_ref[...])[16:32]
    projected = pltpu.roll(sent_ref[0], 112, 1)
    singular = jnp.broadcast_to(jnp.sum(projected * own, axis=0, keepdims=True), (8, 128))
    high = singular.astype(bf16).astype(f32)
    back8 = back.astype(f32)
    none = jnp.zeros((8, 128), f32)
    small = jnp.concatenate(
        [
            jnp.concatenate([back8, pltpu.roll(back8, 16, 1), none, none], axis=1),
            jnp.concatenate([none, none, pltpu.roll(high, 32, 1), pltpu.roll(singular - high, 32, 1)], axis=1),
        ],
        axis=0,
    ).astype(bf16)
    rest_ref[0:16, :] = small
    rest_ref[16:32, :] = right.astype(bf16)
    for x in range(4):
        outs.append(pltpu.make_async_copy(rest_ref, x_any.at[x, 288:320], out_sems.at[12 + x]))
        outs[-1].start()
    for copy in outs:
        copy.wait()


def products(parts, ref):
    total = dot_t(parts[0], ref[:, 0:128, :].reshape(512, 512))
    total += dot_t(parts[1], ref[:, 128:256, :].reshape(512, 512))
    return total.astype(bf16).reshape(4, 128, 512)


def own_kernel(own_ref, near_ref, last_ref, far_ref, far_last_ref, out_ref):
    out_ref[...] = products((rows_of(near_ref, last_ref), rows_of(far_ref, far_last_ref)), own_ref)


def other_kernel(
    place_ref, done_ref, own_ref, other_ref, near_ref, last_ref, far_ref, far_last_ref, out_ref, right_ref
):
    core, z_high = place_ref[0], place_ref[2]
    total = products((rows_of(near_ref, last_ref), rows_of(far_ref, far_last_ref)), other_ref)
    for i, k in enumerate((0, 1, 3, 2)):
        out_ref[z_high ^ k, :, 0:512] = done_ref[i]
        out_ref[z_high ^ k, :, 512:1024] = total[i]
    tok, back, singular = [], [], jnp.zeros((1, 128), f32)
    for ref in (own_ref, other_ref):
        for x in range(4):
            rows = ref[x, 256:288, :]
            tok.append(jnp.where(core == 0, rows[:, :256], rows[:, 256:]))
            small = ref[x, 288:304, :].astype(f32)
            back.extend([small[0:8, :256]] * 4)
            singular += small[8:9, 256:384] + small[8:9, 384:512]
    tok = jnp.concatenate(tok, axis=0)
    back = jnp.concatenate(back, axis=0)
    group = lax.rem(lax.broadcasted_iota(jnp.int32, (256, 1), 0), 32) // 8
    for h in range(4):
        both = t_dot(tok, jnp.where(group == h, back, 0.0).astype(bf16))
        a = both[:, :128].reshape(16, 2, 8, 128)[:, 0]
        b = both[:, 128:].reshape(16, 2, 8, 128)[:, 1]
        z = (a + b + singular).reshape(128, 128)
        high = z.astype(bf16).astype(f32)
        out_ref[h, :, 1024:1152] = (high + pltpu.roll(z - high, 64, 1)).astype(bf16)
    right = jnp.zeros((16, 512), f32)
    for ref in (own_ref, other_ref):
        for x in range(4):
            right += ref[x, 304:320, :].astype(f32)
    right_ref[...] = right


def final_kernel(
    place_ref, back_ref, scaled_ref, left_any, keep_ref, inputs_any, grad_left_any, singular_any,
    left_ref, inputs_ref, grad_left_ref, singular_ref, sems,
):
    left_in = pltpu.make_async_copy(left_any, left_ref, sems.at[0])
    left_in.start()
    core = place_ref[0]
    tail = jnp.sum(back_ref[:, :, 1024:].astype(f32), axis=0)
    tail = (tail + pltpu.roll(tail, 64, 1)) / n_dp
    grad_left_ref[0:8, :] = tail[:, 0:16]
    grad_left_ref[8:16, :] = pltpu.roll(tail, 112, 1)[:, 0:16]
    singular_ref[...] = adapter_scale * keep_ref[...] * pltpu.roll(tail, 96, 1)[0:1, 0:16]
    outs = [
        pltpu.make_async_copy(grad_left_ref, grad_left_any, sems.at[1]),
        pltpu.make_async_copy(singular_ref, singular_any, sems.at[2]),
    ]
    outs[0].start()
    outs[1].start()
    left_in.wait()
    scaled = scaled_ref[:, 0:16]
    for h in range(4):
        for low in range(2):
            total = sum(back_ref[h * 16 + i * 2 + low, :, 0:1024].astype(f32) for i in range(8))
            own, other = total[:, :512], total[:, 512:]
            for c, part in enumerate((jnp.where(core == 0, own, other), jnp.where(core == 0, other, own))):
                for x in range(4):
                    at = h * 2048 + x * 512 + c * 256 + low * 128
                    term = jnp.dot(scaled, left_ref[:, at : at + 128], preferred_element_type=f32)
                    inputs_ref[:, at : at + 128] = (part[:, x * 128 : x * 128 + 128] + term).astype(bf16)
    outs.append(pltpu.make_async_copy(inputs_ref, inputs_any, sems.at[3]))
    outs[2].start()
    for copy in outs:
        copy.wait()


def body(inputs, cotangent, weight, left_factor, right_factor, singular, keep_mask):
    core = lax.axis_index("c")
    y_low = lax.axis_index("yl")
    z_high = lax.axis_index("zh")
    place = jnp.stack([core, y_low, z_high]).astype(jnp.int32)
    shape = jax.ShapeDtypeStruct
    keep_float = keep_mask.astype(f32)
    coeff = adapter_scale * singular * keep_float

    got = swap(weight, "yl", 2, 1)

    back_part = dot_t(cotangent, right_factor).reshape(16, 8, 16)
    own_projected = jnp.dot(inputs, left_factor, preferred_element_type=f32)
    rank_out = jnp.pad(back_part, ((0, 0), (0, 0), (0, 112))) + jnp.pad(own_projected, ((0, 0), (16, 96)))
    rank_in = lax.all_to_all(rank_out, ("zl", "yh", "yl"), 0, 0)

    cot = after(cotangent, got)
    first, third = swap(cot, "zh", 4, 1), swap(cot, "zh", 4, 3)

    coeff_lanes = jnp.pad(jnp.concatenate([coeff, coeff]), (0, 96)).reshape(1, 128)
    slices = inputs.reshape(8, 4, 4, 512).transpose(2, 1, 0, 3).reshape(4, 32, 512)
    x_out, scaled_back = call(
        pack_kernel,
        (shape((4, 320, 512), bf16), shape((8, 128), bf16)),
        [in_smem] + [in_vmem] * 4 + [anywhere] * 2 + [in_vmem],
        30 << 30,
        3 << 20,
        out_specs=(in_hbm, in_vmem),
        scratch=[pltpu.VMEM((32, 512), bf16), dma((16,))],
    )(place, rank_out, rank_in, coeff_lanes, cot, weight, got, slices)
    first = after(first, scaled_back)
    near = call(stack_kernel, shape((2, 128, 512), bf16), [in_vmem] * 2, 30 << 30, 1 << 20)(cot, first)
    far = swap(near, "yl", 2, 1)
    last = call(stack_kernel, shape((2, 128, 512), bf16), [in_vmem] * 2, 30 << 30, 1 << 20)(
        third, swap(first, "zh", 4, 3)
    )
    far_last = swap(last, "yl", 2, 1)
    x_in = after(lax.all_to_all(x_out, "x", 0, 0), far, far_last)
    x_other = swap(x_in, "c", 2, 1)

    done = call(own_kernel, shape((4, 128, 512), bf16), [in_vmem] * 5, 1 << 29, 3 << 20)(
        x_in, near, last, far, far_last
    )
    out, right_part = call(
        other_kernel,
        (shape((4, 128, 1152), bf16), shape((16, 512), f32)),
        [in_smem] + [in_vmem] * 7,
        1 << 29,
        5 << 20,
    )(place, done, x_in, x_other, near, last, far, far_last)
    back = lax.all_to_all(out.reshape(64, 8, 1152), ("zh", "zl", "yh", "yl"), 0, 0)
    right_sent = right_part.astype(bf16)
    right_sum = right_part + sum(swap(right_sent, "zh", 4, k).astype(f32) for k in (1, 2, 3))

    grad_inputs, grad_left, grad_singular = call(
        final_kernel,
        (shape((8, 8192), bf16), shape((16, 16), f32), shape((1, 16), f32)),
        [in_smem, in_vmem, in_vmem, in_hbm, in_vmem],
        2 << 20,
        2 << 20,
        out_specs=(in_hbm, in_hbm, in_hbm),
        scratch=[
            pltpu.VMEM((16, 8192), bf16),
            pltpu.VMEM((8, 8192), bf16),
            pltpu.VMEM((16, 16), f32),
            pltpu.VMEM((1, 16), f32),
            dma((4,)),
        ],
    )(place, back, scaled_back, left_factor.T, keep_float.reshape(1, 16))
    grad_right = right_sum / n_dp
    return (grad_inputs, grad_left, grad_right, grad_singular.reshape(16))


def solution(mesh):
    fine = Mesh(mesh.devices.reshape(4, 4, 2, 2, 4, 2), ("zh", "x", "c", "zl", "yh", "yl"))
    dp = ("zh", "x", "c")
    tensor = ("zl", "yh", "yl")
    in_specs = (
        P(dp + tensor, None),
        P(dp, tensor),
        P(dp, tensor),
        P(),
        P(None, tensor),
        P(),
        P(),
    )
    out_specs = (P(dp + tensor, None), P(dp + tensor, None), P(None, tensor), P())
    return jax.shard_map(body, mesh=fine, in_specs=in_specs, out_specs=out_specs, check_vma=False)
```

```python
import jax
import jax.numpy as jnp
from jax import lax
from jax.experimental import pallas as pl
from jax.experimental.pallas import tpu as pltpu
from jax.sharding import Mesh
from jax.sharding import PartitionSpec as P

adapter_scale = 2.0
n_dp = 32
f32 = jnp.float32
bf16 = jnp.bfloat16
in_vmem = pl.BlockSpec(memory_space=pltpu.VMEM)
in_smem = pl.BlockSpec(memory_space=pltpu.SMEM)
anywhere = pl.BlockSpec(memory_space=pl.ANY)
in_hbm = pl.BlockSpec(memory_space=pltpu.HBM)
dma = pltpu.SemaphoreType.DMA


def dot_t(a, b):
    return lax.dot_general(a, b, (((1,), (1,)), ((), ())), preferred_element_type=f32)


def t_dot(a, b):
    return lax.dot_general(a, b, (((0,), (0,)), ((), ())), preferred_element_type=f32)


def swap(a, axis, count, mask):
    return lax.ppermute(a, axis, [(i, i ^ mask) for i in range(count)])


def call(kernel, out_shape, in_specs, flops, moved, out_specs=None, scratch=()):
    return pl.pallas_call(
        kernel,
        out_shape=out_shape,
        in_specs=in_specs,
        out_specs=out_specs or jax.tree.map(lambda _: in_vmem, out_shape),
        scratch_shapes=scratch,
        compiler_params=pltpu.CompilerParams(vmem_limit_bytes=32 << 20),
        cost_estimate=pl.CostEstimate(flops=flops, bytes_accessed=moved, transcendentals=0),
    )


def after(a, *others):
    return pl.pallas_call(
        lambda *refs: None,
        out_shape=jax.ShapeDtypeStruct(a.shape, a.dtype),
        in_specs=[in_vmem] * (1 + len(others)),
        out_specs=in_vmem,
        input_output_aliases={0: 0},
        compiler_params=pltpu.CompilerParams(vmem_limit_bytes=32 << 20),
    )(a, *others)


def hold_kernel(in_ref, after_ref, out_ref):
    out_ref[...] = in_ref[...]


def stack_kernel(first_ref, second_ref, out_ref):
    out_ref[0] = first_ref[...]
    out_ref[1] = second_ref[...]


def rows_of(first_ref, last_ref):
    return jnp.concatenate([first_ref[...].reshape(256, 512), last_ref[...].reshape(256, 512)], axis=0)


def pack_kernel(
    place_ref, singular_ref, keep_ref, sent_ref, rank_ref, cot_ref, weight_any, got_any, slices_ref,
    x_any, back_ref, rest_ref, out_sems,
):
    rows = pl.ds(pl.multiple_of(place_ref[1] * 128, 128), 128)
    outs = [pltpu.make_async_copy(got_any.at[rows], x_any.at[x, 128:256], out_sems.at[x]) for x in range(4)]
    outs += [pltpu.make_async_copy(weight_any.at[rows], x_any.at[x, 0:128], out_sems.at[8 + x]) for x in range(4)]
    outs += [pltpu.make_async_copy(slices_ref.at[x], x_any.at[x, 256:288], out_sems.at[4 + x]) for x in range(4)]
    for copy in outs:
        copy.start()
    lane = lax.broadcasted_iota(jnp.int32, (1, 128), 1)
    rank = rank_ref[...]
    coeff = jnp.zeros((1, 128), f32)
    for r in range(16):
        value = adapter_scale * singular_ref[r] * keep_ref[r].astype(f32)
        coeff = jnp.where((lane == r) | (lane == 16 + r), value, coeff)
    own = jnp.where(lane < 16, jnp.sum(rank, axis=0), 0.0)
    back = (own * coeff).astype(bf16)
    back_ref[...] = back
    fwd = (jnp.where((lane >= 16) & (lane < 32), rank, 0.0) * coeff).astype(bf16)
    right = t_dot(fwd.reshape(128, 128), cot_ref[...])[16:32]
    projected = pltpu.roll(sent_ref[0], 112, 1)
    singular = jnp.broadcast_to(jnp.sum(projected * own, axis=0, keepdims=True), (8, 128))
    high = singular.astype(bf16).astype(f32)
    back8 = back.astype(f32)
    none = jnp.zeros((8, 128), f32)
    small = jnp.concatenate(
        [
            jnp.concatenate([back8, pltpu.roll(back8, 16, 1), none, none], axis=1),
            jnp.concatenate([none, none, pltpu.roll(high, 32, 1), pltpu.roll(singular - high, 32, 1)], axis=1),
        ],
        axis=0,
    ).astype(bf16)
    rest_ref[0:16, :] = small
    rest_ref[16:32, :] = right.astype(bf16)
    for x in range(4):
        outs.append(pltpu.make_async_copy(rest_ref, x_any.at[x, 288:320], out_sems.at[12 + x]))
        outs[-1].start()
    for copy in outs:
        copy.wait()


def products(parts, ref):
    total = dot_t(parts[0], ref[:, 0:128, :].reshape(512, 512))
    total += dot_t(parts[1], ref[:, 128:256, :].reshape(512, 512))
    return total.astype(bf16).reshape(4, 128, 512)


def adapter_terms(ref, core):
    tok, back, singular = [], [], jnp.zeros((1, 128), f32)
    for x in range(4):
        rows = ref[x, 256:288, :]
        tok.append(jnp.where(core == 0, rows[:, :256], rows[:, 256:]))
        small = ref[x, 288:304, :].astype(f32)
        back.extend([small[0:8, :256]] * 4)
        singular += small[8:9, 256:384] + small[8:9, 384:512]
    tok = jnp.concatenate(tok, axis=0)
    back = jnp.concatenate(back, axis=0)
    group = lax.rem(lax.broadcasted_iota(jnp.int32, (128, 1), 0), 32) // 8
    out = []
    for h in range(4):
        both = t_dot(tok, jnp.where(group == h, back, 0.0).astype(bf16))
        a = both[:, :128].reshape(16, 2, 8, 128)[:, 0]
        b = both[:, 128:].reshape(16, 2, 8, 128)[:, 1]
        out.append((a + b + singular).reshape(128, 128))
    right = sum(ref[x, 304:320, :].astype(f32) for x in range(4))
    return out, right


def own_kernel(
    place_ref, own_ref, near_ref, last_ref, far_ref, far_last_ref, out_ref, terms_ref, right_ref
):
    out_ref[...] = products((rows_of(near_ref, last_ref), rows_of(far_ref, far_last_ref)), own_ref)
    terms, right_ref[...] = adapter_terms(own_ref, place_ref[0])
    for h in range(4):
        terms_ref[h] = terms[h]


def other_kernel(
    place_ref, done_ref, terms_ref, own_right_ref, other_ref, near_ref, last_ref, far_ref, far_last_ref,
    out_ref, right_ref,
):
    z_high = place_ref[2]
    total = products((rows_of(near_ref, last_ref), rows_of(far_ref, far_last_ref)), other_ref)
    for i, k in enumerate((0, 1, 3, 2)):
        out_ref[z_high ^ k, :, 0:512] = done_ref[i]
        out_ref[z_high ^ k, :, 512:1024] = total[i]
    terms, right = adapter_terms(other_ref, place_ref[0])
    right_ref[...] = own_right_ref[...] + right
    for h in range(4):
        z = terms_ref[h] + terms[h]
        high = z.astype(bf16).astype(f32)
        out_ref[h, :, 1024:1152] = (high + pltpu.roll(z - high, 64, 1)).astype(bf16)


def final_kernel(
    place_ref, back_ref, scaled_ref, left_any, keep_ref, inputs_any, grad_left_any, singular_any,
    left_ref, inputs_ref, grad_left_ref, singular_ref, sems,
):
    left_in = pltpu.make_async_copy(left_any, left_ref, sems.at[0])
    left_in.start()
    core = place_ref[0]
    tail = jnp.sum(back_ref[:, :, 1024:].astype(f32), axis=0)
    tail = (tail + pltpu.roll(tail, 64, 1)) / n_dp
    grad_left_ref[0:8, :] = tail[:, 0:16]
    grad_left_ref[8:16, :] = pltpu.roll(tail, 112, 1)[:, 0:16]
    singular_ref[...] = adapter_scale * keep_ref[...] * pltpu.roll(tail, 96, 1)[0:1, 0:16]
    outs = [
        pltpu.make_async_copy(grad_left_ref, grad_left_any, sems.at[1]),
        pltpu.make_async_copy(singular_ref, singular_any, sems.at[2]),
    ]
    outs[0].start()
    outs[1].start()
    left_in.wait()
    scaled = scaled_ref[:, 0:16]
    for h in range(4):
        for low in range(2):
            total = sum(back_ref[h * 16 + i * 2 + low, :, 0:1024].astype(f32) for i in range(8))
            own, other = total[:, :512], total[:, 512:]
            for c, part in enumerate((jnp.where(core == 0, own, other), jnp.where(core == 0, other, own))):
                for x in range(4):
                    at = h * 2048 + x * 512 + c * 256 + low * 128
                    term = jnp.dot(scaled, left_ref[:, at : at + 128], preferred_element_type=f32)
                    inputs_ref[:, at : at + 128] = (part[:, x * 128 : x * 128 + 128] + term).astype(bf16)
    outs.append(pltpu.make_async_copy(inputs_ref, inputs_any, sems.at[3]))
    outs[2].start()
    for copy in outs:
        copy.wait()


def body(inputs, cotangent, weight, left_factor, right_factor, singular, keep_mask):
    core = lax.axis_index("c")
    y_low = lax.axis_index("yl")
    z_high = lax.axis_index("zh")
    place = jnp.stack([core, y_low, z_high]).astype(jnp.int32)
    shape = jax.ShapeDtypeStruct

    got = swap(weight, "yl", 2, 1)

    back_part = dot_t(cotangent, right_factor).reshape(16, 8, 16)
    own_projected = jnp.dot(inputs, left_factor, preferred_element_type=f32)
    rank_out = jnp.pad(back_part, ((0, 0), (0, 0), (0, 112))) + jnp.pad(own_projected, ((0, 0), (16, 96)))
    rank_in = lax.all_to_all(rank_out, ("zl", "yh", "yl"), 0, 0)

    cot = call(hold_kernel, shape((128, 512), bf16), [in_vmem, anywhere], 1, 1 << 18)(cotangent, got)
    first, third = swap(cot, "zh", 4, 1), swap(cot, "zh", 4, 3)

    slices = inputs.reshape(8, 4, 4, 512).transpose(2, 1, 0, 3).reshape(4, 32, 512)
    x_out, scaled_back = call(
        pack_kernel,
        (shape((4, 320, 512), bf16), shape((8, 128), bf16)),
        [in_smem] * 3 + [in_vmem] * 3 + [anywhere] * 2 + [in_vmem],
        30 << 30,
        3 << 20,
        out_specs=(in_hbm, in_vmem),
        scratch=[pltpu.VMEM((32, 512), bf16), dma((16,))],
    )(place, singular, keep_mask, rank_out, rank_in, cot, weight, got, slices)
    first = after(first, scaled_back)
    near = call(stack_kernel, shape((2, 128, 512), bf16), [in_vmem] * 2, 30 << 30, 1 << 20)(cot, first)
    far = swap(near, "yl", 2, 1)
    last = call(stack_kernel, shape((2, 128, 512), bf16), [in_vmem] * 2, 30 << 30, 1 << 20)(
        third, swap(first, "zh", 4, 3)
    )
    far_last = swap(last, "yl", 2, 1)
    x_in = after(lax.all_to_all(x_out, "x", 0, 0), far, far_last)
    x_other = swap(x_in, "c", 2, 1)

    done, terms, own_right = call(
        own_kernel,
        (shape((4, 128, 512), bf16), shape((4, 128, 128), f32), shape((16, 512), f32)),
        [in_smem] + [in_vmem] * 5,
        1 << 29,
        3 << 20,
    )(place, x_in, near, last, far, far_last)
    out, right_part = call(
        other_kernel,
        (shape((4, 128, 1152), bf16), shape((16, 512), f32)),
        [in_smem] + [in_vmem] * 8,
        1 << 29,
        5 << 20,
    )(place, done, terms, own_right, x_other, near, last, far, far_last)
    back = lax.all_to_all(out.reshape(64, 8, 1152), ("zh", "zl", "yh", "yl"), 0, 0)
    right_sent = right_part.astype(bf16)
    right_sum = right_part + sum(swap(right_sent, "zh", 4, k).astype(f32) for k in (1, 2, 3))

    grad_inputs, grad_left, grad_singular = call(
        final_kernel,
        (shape((8, 8192), bf16), shape((16, 16), f32), shape((1, 16), f32)),
        [in_smem, in_vmem, in_vmem, in_hbm, in_vmem],
        2 << 20,
        2 << 20,
        out_specs=(in_hbm, in_hbm, in_hbm),
        scratch=[
            pltpu.VMEM((16, 8192), bf16),
            pltpu.VMEM((8, 8192), bf16),
            pltpu.VMEM((16, 16), f32),
            pltpu.VMEM((1, 16), f32),
            dma((4,)),
        ],
    )(place, back, scaled_back, left_factor.T, keep_mask.astype(f32).reshape(1, 16))
    grad_right = right_sum / n_dp
    return (grad_inputs, grad_left, grad_right, grad_singular.reshape(16))


def solution(mesh):
    fine = Mesh(mesh.devices.reshape(4, 4, 2, 2, 4, 2), ("zh", "x", "c", "zl", "yh", "yl"))
    dp = ("zh", "x", "c")
    tensor = ("zl", "yh", "yl")
    in_specs = (
        P(dp + tensor, None),
        P(dp, tensor),
        P(dp, tensor),
        P(),
        P(None, tensor),
        P(),
        P(),
    )
    out_specs = (P(dp + tensor, None), P(dp + tensor, None), P(None, tensor), P())
    return jax.shard_map(body, mesh=fine, in_specs=in_specs, out_specs=out_specs, check_vma=False)
```

```python
import jax
import jax.numpy as jnp
from jax import lax
from jax.experimental import pallas as pl
from jax.experimental.pallas import tpu as pltpu
from jax.sharding import Mesh
from jax.sharding import PartitionSpec as P

adapter_scale = 2.0
n_dp = 32
f32 = jnp.float32
bf16 = jnp.bfloat16
in_vmem = pl.BlockSpec(memory_space=pltpu.VMEM)
in_smem = pl.BlockSpec(memory_space=pltpu.SMEM)
anywhere = pl.BlockSpec(memory_space=pl.ANY)
in_hbm = pl.BlockSpec(memory_space=pltpu.HBM)
dma = pltpu.SemaphoreType.DMA


def dot_t(a, b):
    return lax.dot_general(a, b, (((1,), (1,)), ((), ())), preferred_element_type=f32)


def t_dot(a, b):
    return lax.dot_general(a, b, (((0,), (0,)), ((), ())), preferred_element_type=f32)


def swap(a, axis, count, mask):
    return lax.ppermute(a, axis, [(i, i ^ mask) for i in range(count)])


def call(kernel, out_shape, in_specs, flops, moved, out_specs=None, scratch=()):
    return pl.pallas_call(
        kernel,
        out_shape=out_shape,
        in_specs=in_specs,
        out_specs=out_specs or jax.tree.map(lambda _: in_vmem, out_shape),
        scratch_shapes=scratch,
        compiler_params=pltpu.CompilerParams(vmem_limit_bytes=32 << 20),
        cost_estimate=pl.CostEstimate(flops=flops, bytes_accessed=moved, transcendentals=0),
    )


def after(a, *others):
    return pl.pallas_call(
        lambda *refs: None,
        out_shape=jax.ShapeDtypeStruct(a.shape, a.dtype),
        in_specs=[in_vmem] * (1 + len(others)),
        out_specs=in_vmem,
        input_output_aliases={0: 0},
        compiler_params=pltpu.CompilerParams(vmem_limit_bytes=32 << 20),
    )(a, *others)


def stack_kernel(first_ref, second_ref, out_ref):
    out_ref[0] = first_ref[...]
    out_ref[1] = second_ref[...]


def rows_of(first_ref, last_ref):
    return jnp.concatenate([first_ref[...].reshape(256, 512), last_ref[...].reshape(256, 512)], axis=0)


def pack_kernel(
    place_ref, singular_ref, keep_ref, sent_ref, rank_ref, cot_ref, weight_any, got_any, inputs_ref,
    x_any, back_ref, rest_ref, out_sems,
):
    rows = pl.ds(pl.multiple_of(place_ref[1] * 128, 128), 128)
    outs = [pltpu.make_async_copy(got_any.at[rows], x_any.at[x, 128:256], out_sems.at[x]) for x in range(4)]
    outs += [pltpu.make_async_copy(weight_any.at[rows], x_any.at[x, 0:128], out_sems.at[8 + x]) for x in range(4)]
    for copy in outs:
        copy.start()
    lane = lax.broadcasted_iota(jnp.int32, (1, 128), 1)
    rank = rank_ref[...]
    coeff = jnp.zeros((1, 128), f32)
    for r in range(16):
        value = adapter_scale * singular_ref[r] * keep_ref[r].astype(f32)
        coeff = jnp.where((lane == r) | (lane == 16 + r), value, coeff)
    own = jnp.where(lane < 16, jnp.sum(rank, axis=0), 0.0)
    back = (own * coeff).astype(bf16)
    back_ref[...] = back
    fwd = (jnp.where((lane >= 16) & (lane < 32), rank, 0.0) * coeff).astype(bf16)
    right = t_dot(fwd.reshape(128, 128), cot_ref[...])[16:32]
    projected = pltpu.roll(sent_ref[0], 112, 1)
    singular = jnp.broadcast_to(jnp.sum(projected * own, axis=0, keepdims=True), (8, 128))
    high = singular.astype(bf16).astype(f32)
    back8 = back.astype(f32)
    none = jnp.zeros((8, 128), f32)
    small = jnp.concatenate(
        [
            jnp.concatenate([back8, pltpu.roll(back8, 16, 1), none, none], axis=1),
            jnp.concatenate([none, none, pltpu.roll(high, 32, 1), pltpu.roll(singular - high, 32, 1)], axis=1),
        ],
        axis=0,
    ).astype(bf16)
    inputs = inputs_ref[...].astype(f32)
    for x in range(4):
        parts = [inputs[:, (h * 4 + x) * 512 : (h * 4 + x + 1) * 512] for h in range(4)]
        rest_ref[x, 0:32, :] = jnp.concatenate(parts, axis=0).astype(bf16)
        rest_ref[x, 32:48, :] = small
        rest_ref[x, 48:64, :] = right.astype(bf16)
        outs.append(pltpu.make_async_copy(rest_ref.at[x], x_any.at[x, 256:320], out_sems.at[4 + x]))
        outs[-1].start()
    for copy in outs:
        copy.wait()


def products(parts, ref):
    total = dot_t(parts[0], ref[:, 0:128, :].reshape(512, 512))
    total += dot_t(parts[1], ref[:, 128:256, :].reshape(512, 512))
    return total.astype(bf16)


def adapter_terms(ref, core):
    tok, back, singular = [], [], jnp.zeros((1, 128), f32)
    for x in range(4):
        rows = ref[x, 256:288, :]
        tok.append(jnp.where(core == 0, rows[:, :256], rows[:, 256:]))
        small = ref[x, 288:304, :].astype(f32)
        back.extend([small[0:8, :256]] * 4)
        singular += small[8:9, 256:384] + small[8:9, 384:512]
    tok = jnp.concatenate(tok, axis=0)
    back = jnp.concatenate(back, axis=0)
    group = lax.rem(lax.broadcasted_iota(jnp.int32, (128, 1), 0), 32) // 8
    out = []
    for h in range(4):
        both = t_dot(tok, jnp.where(group == h, back, 0.0).astype(bf16))
        a = both[:, :128].reshape(16, 2, 8, 128)[:, 0]
        b = both[:, 128:].reshape(16, 2, 8, 128)[:, 1]
        out.append((a + b + singular).reshape(128, 128))
    right = sum(ref[x, 304:320, :].astype(f32) for x in range(4))
    return out, right


def own_kernel(
    place_ref, own_ref, near_ref, last_ref, far_ref, far_last_ref, out_ref, terms_ref, right_ref
):
    parts = (rows_of(near_ref, last_ref), rows_of(far_ref, far_last_ref))
    out_ref[...] = products(parts, own_ref).reshape(4, 128, 512)
    terms, right_ref[...] = adapter_terms(own_ref, place_ref[0])
    for h in range(4):
        terms_ref[h] = terms[h]


def other_kernel(
    place_ref, done_ref, terms_ref, own_right_ref, other_ref, near_ref, last_ref, far_ref, far_last_ref,
    out_any, right_ref, out_ref, sems,
):
    z_high = place_ref[2]
    terms, right = adapter_terms(other_ref, place_ref[0])
    right_ref[...] = own_right_ref[...] + right
    for h in range(4):
        z = terms_ref[h] + terms[h]
        high = z.astype(bf16).astype(f32)
        out_ref[h, :, 1024:1152] = (high + pltpu.roll(z - high, 64, 1)).astype(bf16)
    copies = []
    for half, (first, second) in enumerate(((near_ref, far_ref), (last_ref, far_last_ref))):
        parts = (first[...].reshape(256, 512), second[...].reshape(256, 512))
        total = products(parts, other_ref).reshape(2, 128, 512)
        for i in range(2):
            at = z_high ^ ((0, 1), (3, 2))[half][i]
            out_ref[at, :, 0:512] = done_ref[half * 2 + i]
            out_ref[at, :, 512:1024] = total[i]
            copies.append(pltpu.make_async_copy(out_ref.at[at], out_any.at[at], sems.at[half * 2 + i]))
            copies[-1].start()
    for copy in copies:
        copy.wait()


def final_kernel(
    place_ref, back_ref, scaled_ref, left_any, keep_ref, inputs_any, grad_left_any, singular_any,
    left_ref, inputs_ref, grad_left_ref, singular_ref, sems,
):
    left_in = pltpu.make_async_copy(left_any, left_ref, sems.at[0])
    left_in.start()
    core = place_ref[0]
    tail = jnp.sum(back_ref[:, :, 1024:].astype(f32), axis=0)
    tail = (tail + pltpu.roll(tail, 64, 1)) / n_dp
    grad_left_ref[0:8, :] = tail[:, 0:16]
    grad_left_ref[8:16, :] = pltpu.roll(tail, 112, 1)[:, 0:16]
    singular_ref[...] = adapter_scale * keep_ref[...] * pltpu.roll(tail, 96, 1)[0:1, 0:16]
    outs = [
        pltpu.make_async_copy(grad_left_ref, grad_left_any, sems.at[1]),
        pltpu.make_async_copy(singular_ref, singular_any, sems.at[2]),
    ]
    outs[0].start()
    outs[1].start()
    left_in.wait()
    scaled = scaled_ref[:, 0:16]
    for h in range(4):
        for low in range(2):
            total = sum(back_ref[h * 16 + i * 2 + low, :, 0:1024].astype(f32) for i in range(8))
            own, other = total[:, :512], total[:, 512:]
            for c, part in enumerate((jnp.where(core == 0, own, other), jnp.where(core == 0, other, own))):
                for x in range(4):
                    at = h * 2048 + x * 512 + c * 256 + low * 128
                    term = jnp.dot(scaled, left_ref[:, at : at + 128], preferred_element_type=f32)
                    inputs_ref[:, at : at + 128] = (part[:, x * 128 : x * 128 + 128] + term).astype(bf16)
    outs.append(pltpu.make_async_copy(inputs_ref, inputs_any, sems.at[3]))
    outs[2].start()
    for copy in outs:
        copy.wait()


def body(inputs, cotangent, weight, left_factor, right_factor, singular, keep_mask):
    core = lax.axis_index("c")
    y_low = lax.axis_index("yl")
    z_high = lax.axis_index("zh")
    place = jnp.stack([core, y_low, z_high]).astype(jnp.int32)
    shape = jax.ShapeDtypeStruct

    got = swap(weight, "yl", 2, 1)

    back_part = dot_t(cotangent, right_factor).reshape(16, 8, 16)
    own_projected = jnp.dot(inputs, left_factor, preferred_element_type=f32)
    rank_out = jnp.pad(back_part, ((0, 0), (0, 0), (0, 112))) + jnp.pad(own_projected, ((0, 0), (16, 96)))
    rank_in = lax.all_to_all(rank_out, ("zl", "yh", "yl"), 0, 0)

    cot = after(cotangent, got)
    first, third = swap(cot, "zh", 4, 1), swap(cot, "zh", 4, 3)

    x_out, scaled_back = call(
        pack_kernel,
        (shape((4, 320, 512), bf16), shape((8, 128), bf16)),
        [in_smem] * 3 + [in_vmem] * 3 + [anywhere] * 2 + [in_vmem],
        30 << 30,
        3 << 20,
        out_specs=(in_hbm, in_vmem),
        scratch=[pltpu.VMEM((4, 64, 512), bf16), dma((12,))],
    )(place, singular, keep_mask, rank_out, rank_in, cot, weight, got, inputs)
    first = after(first, scaled_back)
    near = call(stack_kernel, shape((2, 128, 512), bf16), [in_vmem] * 2, 30 << 30, 1 << 20)(cot, first)
    far = swap(near, "yl", 2, 1)
    last = call(stack_kernel, shape((2, 128, 512), bf16), [in_vmem] * 2, 30 << 30, 1 << 20)(
        third, swap(first, "zh", 4, 3)
    )
    far_last = swap(last, "yl", 2, 1)
    x_in = after(lax.all_to_all(x_out, "x", 0, 0), far, far_last)
    x_other = swap(x_in, "c", 2, 1)

    done, terms, own_right = call(
        own_kernel,
        (shape((4, 128, 512), bf16), shape((4, 128, 128), f32), shape((16, 512), f32)),
        [in_smem] + [in_vmem] * 5,
        1 << 29,
        3 << 20,
    )(place, x_in, near, last, far, far_last)
    out, right_part = call(
        other_kernel,
        (shape((4, 128, 1152), bf16), shape((16, 512), f32)),
        [in_smem] + [in_vmem] * 8,
        1 << 29,
        5 << 20,
        out_specs=(in_hbm, in_vmem),
        scratch=[pltpu.VMEM((4, 128, 1152), bf16), dma((4,))],
    )(place, done, terms, own_right, x_other, near, last, far, far_last)
    back = lax.all_to_all(out.reshape(64, 8, 1152), ("zh", "zl", "yh", "yl"), 0, 0)
    right_sent = right_part.astype(bf16)
    right_sum = right_part + sum(swap(right_sent, "zh", 4, k).astype(f32) for k in (1, 2, 3))

    grad_inputs, grad_left, grad_singular = call(
        final_kernel,
        (shape((8, 8192), bf16), shape((16, 16), f32), shape((1, 16), f32)),
        [in_smem, in_vmem, in_vmem, in_hbm, in_vmem],
        2 << 20,
        2 << 20,
        out_specs=(in_hbm, in_hbm, in_hbm),
        scratch=[
            pltpu.VMEM((16, 8192), bf16),
            pltpu.VMEM((8, 8192), bf16),
            pltpu.VMEM((16, 16), f32),
            pltpu.VMEM((1, 16), f32),
            dma((4,)),
        ],
    )(place, back, scaled_back, left_factor.T, keep_mask.astype(f32).reshape(1, 16))
    grad_right = right_sum / n_dp
    return (grad_inputs, grad_left, grad_right, grad_singular.reshape(16))


def solution(mesh):
    fine = Mesh(mesh.devices.reshape(4, 4, 2, 2, 4, 2), ("zh", "x", "c", "zl", "yh", "yl"))
    dp = ("zh", "x", "c")
    tensor = ("zl", "yh", "yl")
    in_specs = (
        P(dp + tensor, None),
        P(dp, tensor),
        P(dp, tensor),
        P(),
        P(None, tensor),
        P(),
        P(),
    )
    out_specs = (P(dp + tensor, None), P(dp + tensor, None), P(None, tensor), P())
    return jax.shard_map(body, mesh=fine, in_specs=in_specs, out_specs=out_specs, check_vma=False)
```

```python
import jax
import jax.numpy as jnp
from jax import lax
from jax.experimental import pallas as pl
from jax.experimental.pallas import tpu as pltpu
from jax.sharding import Mesh
from jax.sharding import PartitionSpec as P

adapter_scale = 2.0
n_dp = 32
f32 = jnp.float32
bf16 = jnp.bfloat16
in_vmem = pl.BlockSpec(memory_space=pltpu.VMEM)
in_smem = pl.BlockSpec(memory_space=pltpu.SMEM)
anywhere = pl.BlockSpec(memory_space=pl.ANY)
in_hbm = pl.BlockSpec(memory_space=pltpu.HBM)
dma = pltpu.SemaphoreType.DMA


def dot_t(a, b):
    return lax.dot_general(a, b, (((1,), (1,)), ((), ())), preferred_element_type=f32)


def t_dot(a, b):
    return lax.dot_general(a, b, (((0,), (0,)), ((), ())), preferred_element_type=f32)


def swap(a, axis, count, mask):
    return lax.ppermute(a, axis, [(i, i ^ mask) for i in range(count)])


def call(kernel, out_shape, in_specs, flops, moved, out_specs=None, scratch=()):
    return pl.pallas_call(
        kernel,
        out_shape=out_shape,
        in_specs=in_specs,
        out_specs=out_specs or jax.tree.map(lambda _: in_vmem, out_shape),
        scratch_shapes=scratch,
        compiler_params=pltpu.CompilerParams(vmem_limit_bytes=32 << 20),
        cost_estimate=pl.CostEstimate(flops=flops, bytes_accessed=moved, transcendentals=0),
    )


def after(a, *others):
    return pl.pallas_call(
        lambda *refs: None,
        out_shape=jax.ShapeDtypeStruct(a.shape, a.dtype),
        in_specs=[in_vmem] * (1 + len(others)),
        out_specs=in_vmem,
        input_output_aliases={0: 0},
        compiler_params=pltpu.CompilerParams(vmem_limit_bytes=32 << 20),
    )(a, *others)


def rank_kernel(mixed_ref, right_ref, projected_ref, out_ref):
    out_ref[...] = jnp.zeros((16, 8, 128), f32)
    out_ref[:, :, 16:32] = jnp.broadcast_to(projected_ref[...][None], (16, 8, 16))
    out_ref[:, :, 0:16] = dot_t(mixed_ref[0:128, :], right_ref[...]).reshape(16, 8, 16)


def pick_kernel(mixed_ref, after_ref, out_ref):
    out_ref[...] = mixed_ref[0:128, :]


def copy_kernel(in_ref, out_ref):
    out_ref[...] = in_ref[...]


def stack_kernel(first_ref, second_ref, after_ref, out_ref):
    out_ref[0] = first_ref[...]
    out_ref[1] = second_ref[...]


def rows_of(own, first_ref, last_ref):
    return jnp.concatenate([own, first_ref[...], last_ref[...].reshape(256, 512)], axis=0)


def pack_kernel(
    place_ref, singular_ref, keep_ref, sent_ref, rank_ref, cot_ref, weight_any, got_any, inputs_ref,
    x_any, back_ref, rest_ref, out_sems,
):
    rows = pl.ds(pl.multiple_of(place_ref[1] * 128, 128), 128)
    outs = [pltpu.make_async_copy(got_any.at[128:256], x_any.at[x, 128:256], out_sems.at[x]) for x in range(4)]
    outs += [pltpu.make_async_copy(weight_any.at[rows], x_any.at[x, 0:128], out_sems.at[8 + x]) for x in range(4)]
    for copy in outs:
        copy.start()
    lane = lax.broadcasted_iota(jnp.int32, (1, 128), 1)
    rank = rank_ref[...]
    coeff = jnp.zeros((1, 128), f32)
    for r in range(16):
        value = adapter_scale * singular_ref[r] * keep_ref[r].astype(f32)
        coeff = jnp.where((lane == r) | (lane == 16 + r), value, coeff)
    own = jnp.where(lane < 16, jnp.sum(rank, axis=0), 0.0)
    back = (own * coeff).astype(bf16)
    back_ref[...] = back
    fwd = (jnp.where((lane >= 16) & (lane < 32), rank, 0.0) * coeff).astype(bf16)
    right = t_dot(fwd.reshape(128, 128), cot_ref[...])[16:32]
    projected = pltpu.roll(sent_ref[0], 112, 1)
    singular = jnp.broadcast_to(jnp.sum(projected * own, axis=0, keepdims=True), (8, 128))
    high = singular.astype(bf16).astype(f32)
    back8 = back.astype(f32)
    none = jnp.zeros((8, 128), f32)
    small = jnp.concatenate(
        [
            jnp.concatenate([back8, pltpu.roll(back8, 16, 1), none, none], axis=1),
            jnp.concatenate([none, none, pltpu.roll(high, 32, 1), pltpu.roll(singular - high, 32, 1)], axis=1),
        ],
        axis=0,
    ).astype(bf16)
    inputs = inputs_ref[...].astype(f32)
    for x in range(4):
        parts = [inputs[:, (h * 4 + x) * 512 : (h * 4 + x + 1) * 512] for h in range(4)]
        rest_ref[x, 0:32, :] = jnp.concatenate(parts, axis=0).astype(bf16)
        rest_ref[x, 32:48, :] = small
        rest_ref[x, 48:64, :] = right.astype(bf16)
        outs.append(pltpu.make_async_copy(rest_ref.at[x], x_any.at[x, 256:320], out_sems.at[4 + x]))
        outs[-1].start()
    for copy in outs:
        copy.wait()


def products(parts, ref):
    total = dot_t(parts[0], ref[:, 0:128, :].reshape(512, 512))
    total += dot_t(parts[1], ref[:, 128:256, :].reshape(512, 512))
    return total.astype(bf16)


def adapter_terms(ref, core):
    tok, back, singular = [], [], jnp.zeros((1, 128), f32)
    for x in range(4):
        rows = ref[x, 256:288, :]
        tok.append(jnp.where(core == 0, rows[:, :256], rows[:, 256:]))
        small = ref[x, 288:304, :].astype(f32)
        back.extend([small[0:8, :256]] * 4)
        singular += small[8:9, 256:384] + small[8:9, 384:512]
    tok = jnp.concatenate(tok, axis=0)
    back = jnp.concatenate(back, axis=0)
    group = lax.rem(lax.broadcasted_iota(jnp.int32, (128, 1), 0), 32) // 8
    out = []
    for h in range(4):
        both = t_dot(tok, jnp.where(group == h, back, 0.0).astype(bf16))
        a = both[:, :128].reshape(16, 2, 8, 128)[:, 0]
        b = both[:, 128:].reshape(16, 2, 8, 128)[:, 1]
        out.append((a + b + singular).reshape(128, 128))
    right = sum(ref[x, 304:320, :].astype(f32) for x in range(4))
    return out, right


def own_kernel(
    place_ref, own_ref, cot_ref, first_ref, last_ref, got_ref, far_ref, far_last_ref, out_ref, terms_ref, right_ref
):
    parts = (rows_of(cot_ref[...], first_ref, last_ref), rows_of(got_ref[0:128, :], far_ref, far_last_ref))
    out_ref[...] = products(parts, own_ref).reshape(4, 128, 512)
    terms, right_ref[...] = adapter_terms(own_ref, place_ref[0])
    for h in range(4):
        terms_ref[h] = terms[h]


def other_kernel(
    place_ref, done_ref, terms_ref, own_right_ref, other_ref, cot_ref, first_ref, last_ref, got_ref, far_ref, far_last_ref,
    out_any, right_ref, out_ref, sems,
):
    z_high = place_ref[2]
    terms, right = adapter_terms(other_ref, place_ref[0])
    right_ref[...] = own_right_ref[...] + right
    for h in range(4):
        z = terms_ref[h] + terms[h]
        high = z.astype(bf16).astype(f32)
        out_ref[h, :, 1024:1152] = (high + pltpu.roll(z - high, 64, 1)).astype(bf16)
    copies = []
    for half in range(2):
        if half == 0:
            near = jnp.concatenate([cot_ref[...], first_ref[...]], axis=0)
            far = jnp.concatenate([got_ref[0:128, :], far_ref[...]], axis=0)
        else:
            near, far = last_ref[...].reshape(256, 512), far_last_ref[...].reshape(256, 512)
        parts = (near, far)
        total = products(parts, other_ref).reshape(2, 128, 512)
        for i in range(2):
            at = z_high ^ ((0, 1), (3, 2))[half][i]
            out_ref[at, :, 0:512] = done_ref[half * 2 + i]
            out_ref[at, :, 512:1024] = total[i]
            copies.append(pltpu.make_async_copy(out_ref.at[at], out_any.at[at], sems.at[half * 2 + i]))
            copies[-1].start()
    for copy in copies:
        copy.wait()


def final_kernel(
    place_ref, back_ref, scaled_ref, left_ref, keep_ref, inputs_any, grad_left_any, singular_any,
    inputs_ref, grad_left_ref, singular_ref, sems,
):
    core = place_ref[0]
    tail = jnp.sum(back_ref[:, :, 1024:].astype(f32), axis=0)
    tail = (tail + pltpu.roll(tail, 64, 1)) / n_dp
    grad_left_ref[0:8, :] = tail[:, 0:16]
    grad_left_ref[8:16, :] = pltpu.roll(tail, 112, 1)[:, 0:16]
    singular_ref[...] = adapter_scale * keep_ref[...] * pltpu.roll(tail, 96, 1)[0:1, 0:16]
    outs = [
        pltpu.make_async_copy(grad_left_ref, grad_left_any, sems.at[1]),
        pltpu.make_async_copy(singular_ref, singular_any, sems.at[2]),
    ]
    outs[0].start()
    outs[1].start()
    scaled = scaled_ref[:, 0:16]
    for h in range(4):
        for low in range(2):
            total = sum(back_ref[h * 16 + i * 2 + low, :, 0:1024].astype(f32) for i in range(8))
            own, other = total[:, :512], total[:, 512:]
            for c, part in enumerate((jnp.where(core == 0, own, other), jnp.where(core == 0, other, own))):
                for x in range(4):
                    at = h * 2048 + x * 512 + c * 256 + low * 128
                    term = jnp.dot(scaled, left_ref[:, at : at + 128], preferred_element_type=f32)
                    inputs_ref[:, at : at + 128] = (part[:, x * 128 : x * 128 + 128] + term).astype(bf16)
    outs.append(pltpu.make_async_copy(inputs_ref, inputs_any, sems.at[3]))
    outs[2].start()
    for copy in outs:
        copy.wait()


def body(inputs, cotangent, weight, left_factor, right_factor, singular, keep_mask):
    core = lax.axis_index("c")
    y_low = lax.axis_index("yl")
    z_high = lax.axis_index("zh")
    place = jnp.stack([core, y_low, z_high]).astype(jnp.int32)
    shape = jax.ShapeDtypeStruct

    given = jnp.where(y_low == 0, weight[128:], weight[:128])
    mixed = jnp.concatenate([cotangent, given], axis=0)
    got = swap(mixed, "yl", 2, 1)

    own_projected = jnp.dot(inputs, left_factor, preferred_element_type=f32)
    rank_out = call(rank_kernel, shape((16, 8, 128), f32), [in_vmem] * 3, 2 << 20, 1 << 20)(
        mixed, right_factor, own_projected
    )
    rank_in = lax.all_to_all(rank_out, ("zl", "yh", "yl"), 0, 0)

    cot = call(pick_kernel, shape((128, 512), bf16), [in_vmem, anywhere], 1, 1 << 18)(mixed, got)
    first, third = swap(cot, "zh", 4, 1), swap(cot, "zh", 4, 3)

    x_out, scaled_back = call(
        pack_kernel,
        (shape((4, 320, 512), bf16), shape((8, 128), bf16)),
        [in_smem] * 3 + [in_vmem] * 3 + [anywhere] * 2 + [in_vmem],
        30 << 30,
        3 << 20,
        out_specs=(in_hbm, in_vmem),
        scratch=[pltpu.VMEM((4, 64, 512), bf16), dma((12,))],
    )(place, singular, keep_mask, rank_out, rank_in, cot, weight, got, inputs)
    first = after(first, scaled_back)
    held = call(copy_kernel, shape((128, 512), bf16), [in_vmem], 30 << 30, 1 << 18)(first)
    far = call(copy_kernel, shape((128, 512), bf16), [in_vmem], 30 << 30, 1 << 18)(swap(held, "yl", 2, 1))
    last = call(stack_kernel, shape((2, 128, 512), bf16), [in_vmem] * 2 + [anywhere], 30 << 30, 1 << 20)(
        third, swap(first, "zh", 4, 3), held
    )
    far_last = swap(last, "yl", 2, 1)
    x_in = after(lax.all_to_all(x_out, "x", 0, 0), far, far_last)
    x_other = swap(x_in, "c", 2, 1)

    done, terms, own_right = call(
        own_kernel,
        (shape((4, 128, 512), bf16), shape((4, 128, 128), f32), shape((16, 512), f32)),
        [in_smem] + [in_vmem] * 7,
        1 << 29,
        3 << 20,
    )(place, x_in, cot, held, last, got, far, far_last)
    out, right_part = call(
        other_kernel,
        (shape((4, 128, 1152), bf16), shape((16, 512), f32)),
        [in_smem] + [in_vmem] * 10,
        1 << 29,
        5 << 20,
        out_specs=(in_hbm, in_vmem),
        scratch=[pltpu.VMEM((4, 128, 1152), bf16), dma((4,))],
    )(place, done, terms, own_right, x_other, cot, held, last, got, far, far_last)
    back = lax.all_to_all(out.reshape(64, 8, 1152), ("zh", "zl", "yh", "yl"), 0, 0)
    right_sent = right_part.astype(bf16)
    right_sum = right_part + sum(swap(right_sent, "zh", 4, k).astype(f32) for k in (1, 2, 3))

    grad_inputs, grad_left, grad_singular = call(
        final_kernel,
        (shape((8, 8192), bf16), shape((16, 16), f32), shape((1, 16), f32)),
        [in_smem] + [in_vmem] * 4,
        2 << 20,
        2 << 20,
        out_specs=(in_hbm, in_hbm, in_hbm),
        scratch=[
            pltpu.VMEM((8, 8192), bf16),
            pltpu.VMEM((16, 16), f32),
            pltpu.VMEM((1, 16), f32),
            dma((4,)),
        ],
    )(place, back, scaled_back, left_factor.T, keep_mask.astype(f32).reshape(1, 16))
    grad_right = right_sum / n_dp
    return (grad_inputs, grad_left, grad_right, grad_singular.reshape(16))


def solution(mesh):
    fine = Mesh(mesh.devices.reshape(4, 4, 2, 2, 4, 2), ("zh", "x", "c", "zl", "yh", "yl"))
    dp = ("zh", "x", "c")
    tensor = ("zl", "yh", "yl")
    in_specs = (
        P(dp + tensor, None),
        P(dp, tensor),
        P(dp, tensor),
        P(),
        P(None, tensor),
        P(),
        P(),
    )
    out_specs = (P(dp + tensor, None), P(dp + tensor, None), P(None, tensor), P())
    return jax.shard_map(body, mesh=fine, in_specs=in_specs, out_specs=out_specs, check_vma=False)
```

```python
import jax
import jax.numpy as jnp
from jax import lax
from jax.experimental import pallas as pl
from jax.experimental.pallas import tpu as pltpu
from jax.sharding import Mesh
from jax.sharding import PartitionSpec as P

adapter_scale = 2.0
n_dp = 32
f32 = jnp.float32
bf16 = jnp.bfloat16
in_vmem = pl.BlockSpec(memory_space=pltpu.VMEM)
in_smem = pl.BlockSpec(memory_space=pltpu.SMEM)
anywhere = pl.BlockSpec(memory_space=pl.ANY)
in_hbm = pl.BlockSpec(memory_space=pltpu.HBM)
dma = pltpu.SemaphoreType.DMA


def dot_t(a, b):
    return lax.dot_general(a, b, (((1,), (1,)), ((), ())), preferred_element_type=f32)


def t_dot(a, b):
    return lax.dot_general(a, b, (((0,), (0,)), ((), ())), preferred_element_type=f32)


def swap(a, axis, count, mask):
    return lax.ppermute(a, axis, [(i, i ^ mask) for i in range(count)])


def call(kernel, out_shape, in_specs, flops, moved, out_specs=None, scratch=()):
    return pl.pallas_call(
        kernel,
        out_shape=out_shape,
        in_specs=in_specs,
        out_specs=out_specs or jax.tree.map(lambda _: in_vmem, out_shape),
        scratch_shapes=scratch,
        compiler_params=pltpu.CompilerParams(vmem_limit_bytes=32 << 20),
        cost_estimate=pl.CostEstimate(flops=flops, bytes_accessed=moved, transcendentals=0),
    )


def after(a, *others):
    return pl.pallas_call(
        lambda *refs: None,
        out_shape=jax.ShapeDtypeStruct(a.shape, a.dtype),
        in_specs=[in_vmem] * (1 + len(others)),
        out_specs=in_vmem,
        input_output_aliases={0: 0},
        compiler_params=pltpu.CompilerParams(vmem_limit_bytes=32 << 20),
    )(a, *others)


def rank_kernel(mixed_ref, right_ref, projected_ref, out_ref):
    out_ref[...] = jnp.zeros((16, 8, 128), f32)
    out_ref[:, :, 16:32] = jnp.broadcast_to(projected_ref[...][None], (16, 8, 16))
    out_ref[:, :, 0:16] = dot_t(mixed_ref[0:128, :], right_ref[...]).reshape(16, 8, 16)


def pick_kernel(mixed_ref, after_ref, out_ref):
    out_ref[...] = mixed_ref[0:128, :]


def copy_kernel(in_ref, out_ref):
    out_ref[...] = in_ref[...]


def stack_kernel(first_ref, second_ref, after_ref, out_ref):
    out_ref[0] = first_ref[...]
    out_ref[1] = second_ref[...]


def rows_of(own, first_ref, last_ref):
    return jnp.concatenate([own, first_ref[...], last_ref[...].reshape(256, 512)], axis=0)


def pack_kernel(
    place_ref, singular_ref, keep_ref, sent_ref, rank_ref, cot_ref, weight_any, got_any, inputs_ref,
    x_any, back_ref, slices_ref, rest_ref, out_sems,
):
    rows = pl.ds(pl.multiple_of(place_ref[1] * 128, 128), 128)
    outs = [pltpu.make_async_copy(got_any.at[128:256], x_any.at[x, 128:256], out_sems.at[x]) for x in range(4)]
    outs += [pltpu.make_async_copy(weight_any.at[rows], x_any.at[x, 0:128], out_sems.at[8 + x]) for x in range(4)]
    for copy in outs:
        copy.start()
    inputs = inputs_ref[...].astype(f32)
    for x in range(4):
        parts = [inputs[:, (h * 4 + x) * 512 : (h * 4 + x + 1) * 512] for h in range(4)]
        slices_ref[x] = jnp.concatenate(parts, axis=0).astype(bf16)
        outs.append(pltpu.make_async_copy(slices_ref.at[x], x_any.at[x, 256:288], out_sems.at[4 + x]))
        outs[-1].start()
    lane = lax.broadcasted_iota(jnp.int32, (1, 128), 1)
    rank = rank_ref[...]
    coeff = jnp.zeros((1, 128), f32)
    for r in range(16):
        value = adapter_scale * singular_ref[r] * keep_ref[r].astype(f32)
        coeff = jnp.where((lane == r) | (lane == 16 + r), value, coeff)
    own = jnp.where(lane < 16, jnp.sum(rank, axis=0), 0.0)
    back = (own * coeff).astype(bf16)
    back_ref[...] = back
    fwd = (jnp.where((lane >= 16) & (lane < 32), rank, 0.0) * coeff).astype(bf16)
    right = t_dot(fwd.reshape(128, 128), cot_ref[...])[16:32]
    projected = pltpu.roll(sent_ref[0], 112, 1)
    singular = jnp.broadcast_to(jnp.sum(projected * own, axis=0, keepdims=True), (8, 128))
    high = singular.astype(bf16).astype(f32)
    back8 = back.astype(f32)
    none = jnp.zeros((8, 128), f32)
    small = jnp.concatenate(
        [
            jnp.concatenate([back8, pltpu.roll(back8, 16, 1), none, none], axis=1),
            jnp.concatenate([none, none, pltpu.roll(high, 32, 1), pltpu.roll(singular - high, 32, 1)], axis=1),
        ],
        axis=0,
    ).astype(bf16)
    rest_ref[0:16, :] = small
    rest_ref[16:32, :] = right.astype(bf16)
    for x in range(4):
        outs.append(pltpu.make_async_copy(rest_ref, x_any.at[x, 288:320], out_sems.at[12 + x]))
        outs[-1].start()
    for copy in outs:
        copy.wait()


def products(parts, ref):
    total = dot_t(parts[0], ref[:, 0:128, :].reshape(512, 512))
    total += dot_t(parts[1], ref[:, 128:256, :].reshape(512, 512))
    return total.astype(bf16)


def adapter_terms(ref, core):
    tok, back, singular = [], [], jnp.zeros((1, 128), f32)
    for x in range(4):
        rows = ref[x, 256:288, :]
        tok.append(jnp.where(core == 0, rows[:, :256], rows[:, 256:]))
        small = ref[x, 288:304, :].astype(f32)
        back.extend([small[0:8, :256]] * 4)
        singular += small[8:9, 256:384] + small[8:9, 384:512]
    tok = jnp.concatenate(tok, axis=0)
    back = jnp.concatenate(back, axis=0)
    group = lax.rem(lax.broadcasted_iota(jnp.int32, (128, 1), 0), 32) // 8
    out = []
    for h in range(4):
        both = t_dot(tok, jnp.where(group == h, back, 0.0).astype(bf16))
        a = both[:, :128].reshape(16, 2, 8, 128)[:, 0]
        b = both[:, 128:].reshape(16, 2, 8, 128)[:, 1]
        out.append((a + b + singular).reshape(128, 128))
    right = sum(ref[x, 304:320, :].astype(f32) for x in range(4))
    return out, right


def own_kernel(
    place_ref, own_ref, cot_ref, first_ref, last_ref, got_ref, far_ref, far_last_ref, out_ref, terms_ref, right_ref
):
    parts = (rows_of(cot_ref[...], first_ref, last_ref), rows_of(got_ref[0:128, :], far_ref, far_last_ref))
    out_ref[...] = products(parts, own_ref).reshape(4, 128, 512)
    terms, right_ref[...] = adapter_terms(own_ref, place_ref[0])
    for h in range(4):
        terms_ref[h] = terms[h]


def other_kernel(
    place_ref, done_ref, terms_ref, own_right_ref, other_ref, cot_ref, first_ref, last_ref, got_ref, far_ref, far_last_ref,
    out_any, right_ref, out_ref, sems,
):
    z_high = place_ref[2]
    terms, right = adapter_terms(other_ref, place_ref[0])
    right_ref[...] = own_right_ref[...] + right
    for h in range(4):
        z = terms_ref[h] + terms[h]
        high = z.astype(bf16).astype(f32)
        out_ref[h, :, 1024:1152] = (high + pltpu.roll(z - high, 64, 1)).astype(bf16)
    copies = []
    for half in range(2):
        if half == 0:
            near = jnp.concatenate([cot_ref[...], first_ref[...]], axis=0)
            far = jnp.concatenate([got_ref[0:128, :], far_ref[...]], axis=0)
        else:
            near, far = last_ref[...].reshape(256, 512), far_last_ref[...].reshape(256, 512)
        parts = (near, far)
        total = products(parts, other_ref).reshape(2, 128, 512)
        for i in range(2):
            at = z_high ^ ((0, 1), (3, 2))[half][i]
            out_ref[at, :, 0:512] = done_ref[half * 2 + i]
            out_ref[at, :, 512:1024] = total[i]
            copies.append(pltpu.make_async_copy(out_ref.at[at], out_any.at[at], sems.at[half * 2 + i]))
            copies[-1].start()
    for copy in copies:
        copy.wait()


def final_kernel(
    place_ref, back_ref, scaled_ref, left_ref, keep_ref, inputs_any, grad_left_any, singular_any,
    inputs_ref, grad_left_ref, singular_ref, sems,
):
    core = place_ref[0]
    tail = jnp.sum(back_ref[:, :, 1024:].astype(f32), axis=0)
    tail = (tail + pltpu.roll(tail, 64, 1)) / n_dp
    grad_left_ref[0:8, :] = tail[:, 0:16]
    grad_left_ref[8:16, :] = pltpu.roll(tail, 112, 1)[:, 0:16]
    singular_ref[...] = adapter_scale * keep_ref[...] * pltpu.roll(tail, 96, 1)[0:1, 0:16]
    outs = [
        pltpu.make_async_copy(grad_left_ref, grad_left_any, sems.at[1]),
        pltpu.make_async_copy(singular_ref, singular_any, sems.at[2]),
    ]
    outs[0].start()
    outs[1].start()
    scaled = scaled_ref[:, 0:16]
    for h in range(4):
        for low in range(2):
            total = sum(back_ref[h * 16 + i * 2 + low, :, 0:1024].astype(f32) for i in range(8))
            own, other = total[:, :512], total[:, 512:]
            for c, part in enumerate((jnp.where(core == 0, own, other), jnp.where(core == 0, other, own))):
                for x in range(4):
                    at = h * 2048 + x * 512 + c * 256 + low * 128
                    term = jnp.dot(scaled, left_ref[:, at : at + 128], preferred_element_type=f32)
                    inputs_ref[:, at : at + 128] = (part[:, x * 128 : x * 128 + 128] + term).astype(bf16)
    outs.append(pltpu.make_async_copy(inputs_ref, inputs_any, sems.at[3]))
    outs[2].start()
    for copy in outs:
        copy.wait()


def body(inputs, cotangent, weight, left_factor, right_factor, singular, keep_mask):
    core = lax.axis_index("c")
    y_low = lax.axis_index("yl")
    z_high = lax.axis_index("zh")
    place = jnp.stack([core, y_low, z_high]).astype(jnp.int32)
    shape = jax.ShapeDtypeStruct

    both = jnp.concatenate([cotangent, weight], axis=0)
    mixed = jnp.where(y_low == 0, jnp.concatenate([both[:128], both[256:]]), both[:256])
    got = swap(mixed, "yl", 2, 1)

    own_projected = jnp.dot(inputs, left_factor, preferred_element_type=f32)
    rank_out = call(rank_kernel, shape((16, 8, 128), f32), [in_vmem] * 3, 2 << 20, 1 << 20)(
        mixed, right_factor, own_projected
    )
    rank_in = lax.all_to_all(rank_out, ("zl", "yh", "yl"), 0, 0)

    cot = call(pick_kernel, shape((128, 512), bf16), [in_vmem, anywhere], 1, 1 << 18)(mixed, got)
    first, third = swap(cot, "zh", 4, 1), swap(cot, "zh", 4, 3)

    x_out, scaled_back = call(
        pack_kernel,
        (shape((4, 320, 512), bf16), shape((8, 128), bf16)),
        [in_smem] * 3 + [in_vmem] * 3 + [anywhere] * 2 + [in_vmem],
        30 << 30,
        3 << 20,
        out_specs=(in_hbm, in_vmem),
        scratch=[pltpu.VMEM((4, 32, 512), bf16), pltpu.VMEM((32, 512), bf16), dma((16,))],
    )(place, singular, keep_mask, rank_out, rank_in, cot, weight, got, inputs)
    first = after(first, scaled_back)
    held = call(copy_kernel, shape((128, 512), bf16), [in_vmem], 30 << 30, 1 << 18)(first)
    far = call(copy_kernel, shape((128, 512), bf16), [in_vmem], 30 << 30, 1 << 18)(swap(held, "yl", 2, 1))
    last = call(stack_kernel, shape((2, 128, 512), bf16), [in_vmem] * 2 + [anywhere], 30 << 30, 1 << 20)(
        third, swap(first, "zh", 4, 3), held
    )
    far_last = swap(last, "yl", 2, 1)
    x_in = after(lax.all_to_all(x_out, "x", 0, 0), far, far_last)
    x_other = swap(x_in, "c", 2, 1)

    done, terms, own_right = call(
        own_kernel,
        (shape((4, 128, 512), bf16), shape((4, 128, 128), f32), shape((16, 512), f32)),
        [in_smem] + [in_vmem] * 7,
        1 << 29,
        3 << 20,
    )(place, x_in, cot, held, last, got, far, far_last)
    out, right_part = call(
        other_kernel,
        (shape((4, 128, 1152), bf16), shape((16, 512), f32)),
        [in_smem] + [in_vmem] * 10,
        1 << 29,
        5 << 20,
        out_specs=(in_hbm, in_vmem),
        scratch=[pltpu.VMEM((4, 128, 1152), bf16), dma((4,))],
    )(place, done, terms, own_right, x_other, cot, held, last, got, far, far_last)
    back = lax.all_to_all(out.reshape(64, 8, 1152), ("zh", "zl", "yh", "yl"), 0, 0)
    right_sent = right_part.astype(bf16)
    right_sum = right_part + sum(swap(right_sent, "zh", 4, k).astype(f32) for k in (1, 2, 3))

    grad_inputs, grad_left, grad_singular = call(
        final_kernel,
        (shape((8, 8192), bf16), shape((16, 16), f32), shape((1, 16), f32)),
        [in_smem] + [in_vmem] * 4,
        2 << 20,
        2 << 20,
        out_specs=(in_hbm, in_hbm, in_hbm),
        scratch=[
            pltpu.VMEM((8, 8192), bf16),
            pltpu.VMEM((16, 16), f32),
            pltpu.VMEM((1, 16), f32),
            dma((4,)),
        ],
    )(place, back, scaled_back, left_factor.T, keep_mask.astype(f32).reshape(1, 16))
    grad_right = right_sum / n_dp
    return (grad_inputs, grad_left, grad_right, grad_singular.reshape(16))


def solution(mesh):
    fine = Mesh(mesh.devices.reshape(4, 4, 2, 2, 4, 2), ("zh", "x", "c", "zl", "yh", "yl"))
    dp = ("zh", "x", "c")
    tensor = ("zl", "yh", "yl")
    in_specs = (
        P(dp + tensor, None),
        P(dp, tensor),
        P(dp, tensor),
        P(),
        P(None, tensor),
        P(),
        P(),
    )
    out_specs = (P(dp + tensor, None), P(dp + tensor, None), P(None, tensor), P())
    return jax.shard_map(body, mesh=fine, in_specs=in_specs, out_specs=out_specs, check_vma=False)
```

```python
import jax
import jax.numpy as jnp
from jax import lax
from jax.experimental import pallas as pl
from jax.experimental.pallas import tpu as pltpu
from jax.sharding import Mesh
from jax.sharding import PartitionSpec as P

adapter_scale = 2.0
n_dp = 32
f32 = jnp.float32
bf16 = jnp.bfloat16
in_vmem = pl.BlockSpec(memory_space=pltpu.VMEM)
in_smem = pl.BlockSpec(memory_space=pltpu.SMEM)
anywhere = pl.BlockSpec(memory_space=pl.ANY)
in_hbm = pl.BlockSpec(memory_space=pltpu.HBM)
dma = pltpu.SemaphoreType.DMA


def dot_t(a, b):
    return lax.dot_general(a, b, (((1,), (1,)), ((), ())), preferred_element_type=f32)


def t_dot(a, b):
    return lax.dot_general(a, b, (((0,), (0,)), ((), ())), preferred_element_type=f32)


def swap(a, axis, count, mask):
    return lax.ppermute(a, axis, [(i, i ^ mask) for i in range(count)])


def call(kernel, out_shape, in_specs, flops, moved, out_specs=None, scratch=()):
    return pl.pallas_call(
        kernel,
        out_shape=out_shape,
        in_specs=in_specs,
        out_specs=out_specs or jax.tree.map(lambda _: in_vmem, out_shape),
        scratch_shapes=scratch,
        compiler_params=pltpu.CompilerParams(vmem_limit_bytes=32 << 20),
        cost_estimate=pl.CostEstimate(flops=flops, bytes_accessed=moved, transcendentals=0),
    )


def after(a, *others):
    return pl.pallas_call(
        lambda *refs: None,
        out_shape=jax.ShapeDtypeStruct(a.shape, a.dtype),
        in_specs=[in_vmem] * (1 + len(others)),
        out_specs=in_vmem,
        input_output_aliases={0: 0},
        compiler_params=pltpu.CompilerParams(vmem_limit_bytes=32 << 20),
    )(a, *others)


def rank_kernel(mixed_ref, right_ref, projected_ref, out_ref):
    out_ref[...] = jnp.zeros((16, 8, 128), f32)
    out_ref[:, :, 16:32] = jnp.broadcast_to(projected_ref[...][None], (16, 8, 16))
    out_ref[:, :, 0:16] = dot_t(mixed_ref[0:128, :], right_ref[...]).reshape(16, 8, 16)


def pick_kernel(mixed_ref, got_ref, out_ref):
    out_ref[0] = mixed_ref[0:128, :]
    out_ref[1] = got_ref[0:128, :]


def copy_kernel(in_ref, out_ref):
    out_ref[...] = in_ref[...]


def stack_kernel(first_ref, second_ref, after_ref, out_ref):
    out_ref[0] = first_ref[...]
    out_ref[1] = second_ref[...]


def rows_of(refs):
    return [jnp.concatenate([ref[half] for ref in refs], axis=0) for half in (0, 1)]


def pack_kernel(
    place_ref, singular_ref, keep_ref, sent_ref, rank_ref, cot_ref, weight_any, got_any, inputs_ref,
    x_any, back_ref, rest_ref, out_sems,
):
    rows = pl.ds(pl.multiple_of(place_ref[1] * 128, 128), 128)
    outs = [pltpu.make_async_copy(got_any.at[128:256], x_any.at[x, 128:256], out_sems.at[x]) for x in range(4)]
    outs += [pltpu.make_async_copy(weight_any.at[rows], x_any.at[x, 0:128], out_sems.at[8 + x]) for x in range(4)]
    for copy in outs:
        copy.start()
    lane = lax.broadcasted_iota(jnp.int32, (1, 128), 1)
    rank = rank_ref[...]
    coeff = jnp.zeros((1, 128), f32)
    for r in range(16):
        value = adapter_scale * singular_ref[r] * keep_ref[r].astype(f32)
        coeff = jnp.where((lane == r) | (lane == 16 + r), value, coeff)
    own = jnp.where(lane < 16, jnp.sum(rank, axis=0), 0.0)
    back = (own * coeff).astype(bf16)
    back_ref[...] = back
    fwd = (jnp.where((lane >= 16) & (lane < 32), rank, 0.0) * coeff).astype(bf16)
    right = t_dot(fwd.reshape(128, 128), cot_ref[0])[16:32]
    projected = pltpu.roll(sent_ref[0], 112, 1)
    singular = jnp.broadcast_to(jnp.sum(projected * own, axis=0, keepdims=True), (8, 128))
    high = singular.astype(bf16).astype(f32)
    back8 = back.astype(f32)
    none = jnp.zeros((8, 128), f32)
    small = jnp.concatenate(
        [
            jnp.concatenate([back8, pltpu.roll(back8, 16, 1), none, none], axis=1),
            jnp.concatenate([none, none, pltpu.roll(high, 32, 1), pltpu.roll(singular - high, 32, 1)], axis=1),
        ],
        axis=0,
    ).astype(bf16)
    inputs = inputs_ref[...].astype(f32)
    for x in range(4):
        parts = [inputs[:, (h * 4 + x) * 512 : (h * 4 + x + 1) * 512] for h in range(4)]
        rest_ref[x, 0:32, :] = jnp.concatenate(parts, axis=0).astype(bf16)
        rest_ref[x, 32:48, :] = small
        rest_ref[x, 48:64, :] = right.astype(bf16)
        outs.append(pltpu.make_async_copy(rest_ref.at[x], x_any.at[x, 256:320], out_sems.at[4 + x]))
        outs[-1].start()
    for copy in outs:
        copy.wait()


def products(parts, ref):
    total = dot_t(parts[0], ref[:, 0:128, :].reshape(512, 512))
    total += dot_t(parts[1], ref[:, 128:256, :].reshape(512, 512))
    return total.astype(bf16)


def adapter_terms(ref, core):
    tok, back, singular = [], [], jnp.zeros((1, 128), f32)
    for x in range(4):
        rows = ref[x, 256:288, :]
        tok.append(jnp.where(core == 0, rows[:, :256], rows[:, 256:]))
        small = ref[x, 288:304, :].astype(f32)
        back.extend([small[0:8, :256]] * 4)
        singular += small[8:9, 256:384] + small[8:9, 384:512]
    tok = jnp.concatenate(tok, axis=0)
    back = jnp.concatenate(back, axis=0)
    group = lax.rem(lax.broadcasted_iota(jnp.int32, (128, 1), 0), 32) // 8
    out = []
    for h in range(4):
        both = t_dot(tok, jnp.where(group == h, back, 0.0).astype(bf16))
        a = both[:, :128].reshape(16, 2, 8, 128)[:, 0]
        b = both[:, 128:].reshape(16, 2, 8, 128)[:, 1]
        out.append((a + b + singular).reshape(128, 128))
    right = sum(ref[x, 304:320, :].astype(f32) for x in range(4))
    return out, right


def own_kernel(
    place_ref, own_ref, cot_ref, first_ref, third_ref, last_ref, out_ref, terms_ref, right_ref
):
    parts = rows_of((cot_ref, first_ref, third_ref, last_ref))
    out_ref[...] = products(parts, own_ref).reshape(4, 128, 512)
    terms, right_ref[...] = adapter_terms(own_ref, place_ref[0])
    for h in range(4):
        terms_ref[h] = terms[h]


def other_kernel(
    place_ref, done_ref, terms_ref, own_right_ref, other_ref, cot_ref, first_ref, third_ref, last_ref,
    out_any, right_ref, out_ref, sems,
):
    z_high = place_ref[2]
    terms, right = adapter_terms(other_ref, place_ref[0])
    right_ref[...] = own_right_ref[...] + right
    for h in range(4):
        z = terms_ref[h] + terms[h]
        high = z.astype(bf16).astype(f32)
        out_ref[h, :, 1024:1152] = (high + pltpu.roll(z - high, 64, 1)).astype(bf16)
    copies = []
    for half, refs in enumerate(((cot_ref, first_ref), (third_ref, last_ref))):
        parts = rows_of(refs)
        total = products(parts, other_ref).reshape(2, 128, 512)
        for i in range(2):
            at = z_high ^ ((0, 1), (3, 2))[half][i]
            out_ref[at, :, 0:512] = done_ref[half * 2 + i]
            out_ref[at, :, 512:1024] = total[i]
            copies.append(pltpu.make_async_copy(out_ref.at[at], out_any.at[at], sems.at[half * 2 + i]))
            copies[-1].start()
    for copy in copies:
        copy.wait()


def final_kernel(
    place_ref, back_ref, scaled_ref, left_ref, keep_ref, inputs_any, grad_left_any, singular_any,
    inputs_ref, grad_left_ref, singular_ref, sems,
):
    core = place_ref[0]
    tail = jnp.sum(back_ref[:, :, 1024:].astype(f32), axis=0)
    tail = (tail + pltpu.roll(tail, 64, 1)) / n_dp
    grad_left_ref[0:8, :] = tail[:, 0:16]
    grad_left_ref[8:16, :] = pltpu.roll(tail, 112, 1)[:, 0:16]
    singular_ref[...] = adapter_scale * keep_ref[...] * pltpu.roll(tail, 96, 1)[0:1, 0:16]
    outs = [
        pltpu.make_async_copy(grad_left_ref, grad_left_any, sems.at[1]),
        pltpu.make_async_copy(singular_ref, singular_any, sems.at[2]),
    ]
    outs[0].start()
    outs[1].start()
    scaled = scaled_ref[:, 0:16]
    for h in range(4):
        for low in range(2):
            total = sum(back_ref[h * 16 + i * 2 + low, :, 0:1024].astype(f32) for i in range(8))
            own, other = total[:, :512], total[:, 512:]
            for c, part in enumerate((jnp.where(core == 0, own, other), jnp.where(core == 0, other, own))):
                for x in range(4):
                    at = h * 2048 + x * 512 + c * 256 + low * 128
                    term = jnp.dot(scaled, left_ref[:, at : at + 128], preferred_element_type=f32)
                    inputs_ref[:, at : at + 128] = (part[:, x * 128 : x * 128 + 128] + term).astype(bf16)
    outs.append(pltpu.make_async_copy(inputs_ref, inputs_any, sems.at[3]))
    outs[2].start()
    for copy in outs:
        copy.wait()


def body(inputs, cotangent, weight, left_factor, right_factor, singular, keep_mask):
    core = lax.axis_index("c")
    y_low = lax.axis_index("yl")
    z_high = lax.axis_index("zh")
    place = jnp.stack([core, y_low, z_high]).astype(jnp.int32)
    shape = jax.ShapeDtypeStruct

    given = jnp.where(y_low == 0, weight[128:], weight[:128])
    mixed = jnp.concatenate([cotangent, given], axis=0)
    got = swap(mixed, "yl", 2, 1)

    own_projected = jnp.dot(inputs, left_factor, preferred_element_type=f32)
    rank_out = call(rank_kernel, shape((16, 8, 128), f32), [in_vmem] * 3, 2 << 20, 1 << 20)(
        mixed, right_factor, own_projected
    )
    rank_in = lax.all_to_all(rank_out, ("zl", "yh", "yl"), 0, 0)

    cot = call(pick_kernel, shape((2, 128, 512), bf16), [in_vmem] * 2, 1, 1 << 18)(mixed, got)
    first, third = swap(cot, "zh", 4, 1), swap(cot, "zh", 4, 3)

    x_out, scaled_back = call(
        pack_kernel,
        (shape((4, 320, 512), bf16), shape((8, 128), bf16)),
        [in_smem] * 3 + [in_vmem] * 3 + [anywhere] * 2 + [in_vmem],
        30 << 30,
        3 << 20,
        out_specs=(in_hbm, in_vmem),
        scratch=[pltpu.VMEM((4, 64, 512), bf16), dma((12,))],
    )(place, singular, keep_mask, rank_out, rank_in, cot, weight, got, inputs)
    first = after(first, scaled_back)
    held = call(copy_kernel, shape((2, 128, 512), bf16), [in_vmem], 30 << 30, 1 << 18)(first)
    last = call(stack_kernel, shape((2, 128, 512), bf16), [in_vmem] * 2 + [anywhere], 30 << 30, 1 << 20)(
        swap(first[0], "zh", 4, 3), swap(third[1], "zh", 4, 1), held
    )
    x_in = after(lax.all_to_all(x_out, "x", 0, 0), last)
    x_other = swap(x_in, "c", 2, 1)

    done, terms, own_right = call(
        own_kernel,
        (shape((4, 128, 512), bf16), shape((4, 128, 128), f32), shape((16, 512), f32)),
        [in_smem] + [in_vmem] * 5,
        1 << 29,
        3 << 20,
    )(place, x_in, cot, held, third, last)
    out, right_part = call(
        other_kernel,
        (shape((4, 128, 1152), bf16), shape((16, 512), f32)),
        [in_smem] + [in_vmem] * 8,
        1 << 29,
        5 << 20,
        out_specs=(in_hbm, in_vmem),
        scratch=[pltpu.VMEM((4, 128, 1152), bf16), dma((4,))],
    )(place, done, terms, own_right, x_other, cot, held, third, last)
    back = lax.all_to_all(out.reshape(64, 8, 1152), ("zh", "zl", "yh", "yl"), 0, 0)
    right_sent = right_part.astype(bf16)
    right_sum = right_part + sum(swap(right_sent, "zh", 4, k).astype(f32) for k in (1, 2, 3))

    grad_inputs, grad_left, grad_singular = call(
        final_kernel,
        (shape((8, 8192), bf16), shape((16, 16), f32), shape((1, 16), f32)),
        [in_smem] + [in_vmem] * 4,
        2 << 20,
        2 << 20,
        out_specs=(in_hbm, in_hbm, in_hbm),
        scratch=[
            pltpu.VMEM((8, 8192), bf16),
            pltpu.VMEM((16, 16), f32),
            pltpu.VMEM((1, 16), f32),
            dma((4,)),
        ],
    )(place, back, scaled_back, left_factor.T, keep_mask.astype(f32).reshape(1, 16))
    grad_right = right_sum / n_dp
    return (grad_inputs, grad_left, grad_right, grad_singular.reshape(16))


def solution(mesh):
    fine = Mesh(mesh.devices.reshape(4, 4, 2, 2, 4, 2), ("zh", "x", "c", "zl", "yh", "yl"))
    dp = ("zh", "x", "c")
    tensor = ("zl", "yh", "yl")
    in_specs = (
        P(dp + tensor, None),
        P(dp, tensor),
        P(dp, tensor),
        P(),
        P(None, tensor),
        P(),
        P(),
    )
    out_specs = (P(dp + tensor, None), P(dp + tensor, None), P(None, tensor), P())
    return jax.shard_map(body, mesh=fine, in_specs=in_specs, out_specs=out_specs, check_vma=False)
```

```python
import jax
import jax.numpy as jnp
from jax import lax
from jax.experimental import pallas as pl
from jax.experimental.pallas import tpu as pltpu
from jax.sharding import Mesh
from jax.sharding import PartitionSpec as P

adapter_scale = 2.0
n_dp = 32
f32 = jnp.float32
bf16 = jnp.bfloat16
in_vmem = pl.BlockSpec(memory_space=pltpu.VMEM)
in_smem = pl.BlockSpec(memory_space=pltpu.SMEM)
anywhere = pl.BlockSpec(memory_space=pl.ANY)
in_hbm = pl.BlockSpec(memory_space=pltpu.HBM)
dma = pltpu.SemaphoreType.DMA


def dot_t(a, b):
    return lax.dot_general(a, b, (((1,), (1,)), ((), ())), preferred_element_type=f32)


def t_dot(a, b):
    return lax.dot_general(a, b, (((0,), (0,)), ((), ())), preferred_element_type=f32)


def swap(a, axis, count, mask):
    return lax.ppermute(a, axis, [(i, i ^ mask) for i in range(count)])


def call(kernel, out_shape, in_specs, flops, moved, out_specs=None, scratch=()):
    return pl.pallas_call(
        kernel,
        out_shape=out_shape,
        in_specs=in_specs,
        out_specs=out_specs or jax.tree.map(lambda _: in_vmem, out_shape),
        scratch_shapes=scratch,
        compiler_params=pltpu.CompilerParams(vmem_limit_bytes=32 << 20),
        cost_estimate=pl.CostEstimate(flops=flops, bytes_accessed=moved, transcendentals=0),
    )


def after(a, *others):
    return pl.pallas_call(
        lambda *refs: None,
        out_shape=jax.ShapeDtypeStruct(a.shape, a.dtype),
        in_specs=[in_vmem] * (1 + len(others)),
        out_specs=in_vmem,
        input_output_aliases={0: 0},
        compiler_params=pltpu.CompilerParams(vmem_limit_bytes=32 << 20),
    )(a, *others)


def rank_kernel(mixed_ref, right_ref, projected_ref, out_ref):
    out_ref[...] = jnp.zeros((16, 8, 128), f32)
    out_ref[:, :, 16:32] = jnp.broadcast_to(projected_ref[...][None], (16, 8, 16))
    out_ref[:, :, 0:16] = dot_t(mixed_ref[0:128, :], right_ref[...]).reshape(16, 8, 16)


def pick_kernel(mixed_ref, got_ref, out_ref, own_ref):
    own_ref[...] = mixed_ref[0:128, :]
    out_ref[0] = mixed_ref[0:128, :]
    out_ref[1] = got_ref[0:128, :]


def copy_kernel(in_ref, out_ref):
    out_ref[...] = in_ref[...]


def stack_kernel(first_ref, second_ref, after_ref, out_ref):
    out_ref[0] = first_ref[...]
    out_ref[1] = second_ref[...]


def rows_of(*pairs):
    return [jnp.concatenate([pair[half] for pair in pairs], axis=0) for half in (0, 1)]


def pack_kernel(
    place_ref, singular_ref, keep_ref, sent_ref, rank_ref, cot_ref, weight_any, got_any, inputs_ref,
    x_any, back_ref, rest_ref, out_sems,
):
    rows = pl.ds(pl.multiple_of(place_ref[1] * 128, 128), 128)
    outs = [pltpu.make_async_copy(got_any.at[128:256], x_any.at[x, 128:256], out_sems.at[x]) for x in range(4)]
    outs += [pltpu.make_async_copy(weight_any.at[rows], x_any.at[x, 0:128], out_sems.at[8 + x]) for x in range(4)]
    for copy in outs:
        copy.start()
    lane = lax.broadcasted_iota(jnp.int32, (1, 128), 1)
    rank = rank_ref[...]
    coeff = jnp.zeros((1, 128), f32)
    for r in range(16):
        value = adapter_scale * singular_ref[r] * keep_ref[r].astype(f32)
        coeff = jnp.where((lane == r) | (lane == 16 + r), value, coeff)
    own = jnp.where(lane < 16, jnp.sum(rank, axis=0), 0.0)
    back = (own * coeff).astype(bf16)
    back_ref[...] = back
    fwd = (jnp.where((lane >= 16) & (lane < 32), rank, 0.0) * coeff).astype(bf16)
    right = t_dot(fwd.reshape(128, 128), cot_ref[0])[16:32]
    projected = pltpu.roll(sent_ref[0], 112, 1)
    singular = jnp.broadcast_to(jnp.sum(projected * own, axis=0, keepdims=True), (8, 128))
    high = singular.astype(bf16).astype(f32)
    back8 = back.astype(f32)
    none = jnp.zeros((8, 128), f32)
    small = jnp.concatenate(
        [
            jnp.concatenate([back8, pltpu.roll(back8, 16, 1), none, none], axis=1),
            jnp.concatenate([none, none, pltpu.roll(high, 32, 1), pltpu.roll(singular - high, 32, 1)], axis=1),
        ],
        axis=0,
    ).astype(bf16)
    inputs = inputs_ref[...].astype(f32)
    for x in range(4):
        parts = [inputs[:, (h * 4 + x) * 512 : (h * 4 + x + 1) * 512] for h in range(4)]
        rest_ref[x, 0:32, :] = jnp.concatenate(parts, axis=0).astype(bf16)
        rest_ref[x, 32:48, :] = small
        rest_ref[x, 48:64, :] = right.astype(bf16)
        outs.append(pltpu.make_async_copy(rest_ref.at[x], x_any.at[x, 256:320], out_sems.at[4 + x]))
        outs[-1].start()
    for copy in outs:
        copy.wait()


def products(parts, ref):
    total = dot_t(parts[0], ref[:, 0:128, :].reshape(512, 512))
    total += dot_t(parts[1], ref[:, 128:256, :].reshape(512, 512))
    return total.astype(bf16)


def adapter_terms(ref, core):
    tok, back, singular = [], [], jnp.zeros((1, 128), f32)
    for x in range(4):
        rows = ref[x, 256:288, :]
        tok.append(jnp.where(core == 0, rows[:, :256], rows[:, 256:]))
        small = ref[x, 288:304, :].astype(f32)
        back.extend([small[0:8, :256]] * 4)
        singular += small[8:9, 256:384] + small[8:9, 384:512]
    tok = jnp.concatenate(tok, axis=0)
    back = jnp.concatenate(back, axis=0)
    group = lax.rem(lax.broadcasted_iota(jnp.int32, (128, 1), 0), 32) // 8
    out = []
    for h in range(4):
        both = t_dot(tok, jnp.where(group == h, back, 0.0).astype(bf16))
        a = both[:, :128].reshape(16, 2, 8, 128)[:, 0]
        b = both[:, 128:].reshape(16, 2, 8, 128)[:, 1]
        out.append((a + b + singular).reshape(128, 128))
    right = sum(ref[x, 304:320, :].astype(f32) for x in range(4))
    return out, right


def own_kernel(
    place_ref, own_ref, cot_ref, first_ref, far_ref, third_ref, last_ref, out_ref, terms_ref, right_ref
):
    parts = rows_of(cot_ref, (first_ref[...], far_ref[...]), third_ref, last_ref)
    out_ref[...] = products(parts, own_ref).reshape(4, 128, 512)
    terms, right_ref[...] = adapter_terms(own_ref, place_ref[0])
    for h in range(4):
        terms_ref[h] = terms[h]


def other_kernel(
    place_ref, done_ref, terms_ref, own_right_ref, other_ref, cot_ref, first_ref, far_ref, third_ref, last_ref,
    out_any, right_ref, out_ref, sems,
):
    z_high = place_ref[2]
    terms, right = adapter_terms(other_ref, place_ref[0])
    right_ref[...] = own_right_ref[...] + right
    for h in range(4):
        z = terms_ref[h] + terms[h]
        high = z.astype(bf16).astype(f32)
        out_ref[h, :, 1024:1152] = (high + pltpu.roll(z - high, 64, 1)).astype(bf16)
    copies = []
    first_half = rows_of(cot_ref, (first_ref[...], far_ref[...]))
    for half, parts in enumerate((first_half, rows_of(third_ref, last_ref))):
        total = products(parts, other_ref).reshape(2, 128, 512)
        for i in range(2):
            at = z_high ^ ((0, 1), (3, 2))[half][i]
            out_ref[at, :, 0:512] = done_ref[half * 2 + i]
            out_ref[at, :, 512:1024] = total[i]
            copies.append(pltpu.make_async_copy(out_ref.at[at], out_any.at[at], sems.at[half * 2 + i]))
            copies[-1].start()
    for copy in copies:
        copy.wait()


def final_kernel(
    place_ref, back_ref, scaled_ref, left_ref, keep_ref, inputs_any, grad_left_any, singular_any,
    inputs_ref, grad_left_ref, singular_ref, sems,
):
    core = place_ref[0]
    tail = jnp.sum(back_ref[:, :, 1024:].astype(f32), axis=0)
    tail = (tail + pltpu.roll(tail, 64, 1)) / n_dp
    grad_left_ref[0:8, :] = tail[:, 0:16]
    grad_left_ref[8:16, :] = pltpu.roll(tail, 112, 1)[:, 0:16]
    singular_ref[...] = adapter_scale * keep_ref[...] * pltpu.roll(tail, 96, 1)[0:1, 0:16]
    outs = [
        pltpu.make_async_copy(grad_left_ref, grad_left_any, sems.at[1]),
        pltpu.make_async_copy(singular_ref, singular_any, sems.at[2]),
    ]
    outs[0].start()
    outs[1].start()
    scaled = scaled_ref[:, 0:16]
    for h in range(4):
        for low in range(2):
            total = sum(back_ref[h * 16 + i * 2 + low, :, 0:1024].astype(f32) for i in range(8))
            own, other = total[:, :512], total[:, 512:]
            for c, part in enumerate((jnp.where(core == 0, own, other), jnp.where(core == 0, other, own))):
                for x in range(4):
                    at = h * 2048 + x * 512 + c * 256 + low * 128
                    term = jnp.dot(scaled, left_ref[:, at : at + 128], preferred_element_type=f32)
                    inputs_ref[:, at : at + 128] = (part[:, x * 128 : x * 128 + 128] + term).astype(bf16)
    outs.append(pltpu.make_async_copy(inputs_ref, inputs_any, sems.at[3]))
    outs[2].start()
    for copy in outs:
        copy.wait()


def body(inputs, cotangent, weight, left_factor, right_factor, singular, keep_mask):
    core = lax.axis_index("c")
    y_low = lax.axis_index("yl")
    z_high = lax.axis_index("zh")
    place = jnp.stack([core, y_low, z_high]).astype(jnp.int32)
    shape = jax.ShapeDtypeStruct

    given = jnp.where(y_low == 0, weight[128:], weight[:128])
    mixed = jnp.concatenate([cotangent, given], axis=0)
    got = swap(mixed, "yl", 2, 1)

    own_projected = jnp.dot(inputs, left_factor, preferred_element_type=f32)
    rank_out = call(rank_kernel, shape((16, 8, 128), f32), [in_vmem] * 3, 2 << 20, 1 << 20)(
        mixed, right_factor, own_projected
    )
    rank_in = lax.all_to_all(rank_out, ("zl", "yh", "yl"), 0, 0)

    cot, own = call(
        pick_kernel, (shape((2, 128, 512), bf16), shape((128, 512), bf16)), [in_vmem] * 2, 1, 1 << 18
    )(mixed, got)
    first, third = swap(own, "zh", 4, 1), swap(cot, "zh", 4, 3)

    x_out, scaled_back = call(
        pack_kernel,
        (shape((4, 320, 512), bf16), shape((8, 128), bf16)),
        [in_smem] * 3 + [in_vmem] * 3 + [anywhere] * 2 + [in_vmem],
        30 << 30,
        3 << 20,
        out_specs=(in_hbm, in_vmem),
        scratch=[pltpu.VMEM((4, 64, 512), bf16), dma((12,))],
    )(place, singular, keep_mask, rank_out, rank_in, cot, weight, got, inputs)
    first = after(first, scaled_back)
    held = call(copy_kernel, shape((128, 512), bf16), [in_vmem], 30 << 30, 1 << 18)(first)
    far = call(copy_kernel, shape((128, 512), bf16), [in_vmem], 30 << 30, 1 << 18)(swap(held, "yl", 2, 1))
    last = call(stack_kernel, shape((2, 128, 512), bf16), [in_vmem] * 2 + [anywhere], 30 << 30, 1 << 20)(
        swap(first, "zh", 4, 3), swap(third[1], "zh", 4, 1), held
    )
    x_in = after(lax.all_to_all(x_out, "x", 0, 0), last, far)
    x_other = swap(x_in, "c", 2, 1)

    done, terms, own_right = call(
        own_kernel,
        (shape((4, 128, 512), bf16), shape((4, 128, 128), f32), shape((16, 512), f32)),
        [in_smem] + [in_vmem] * 6,
        1 << 29,
        3 << 20,
    )(place, x_in, cot, held, far, third, last)
    out, right_part = call(
        other_kernel,
        (shape((4, 128, 1152), bf16), shape((16, 512), f32)),
        [in_smem] + [in_vmem] * 9,
        1 << 29,
        5 << 20,
        out_specs=(in_hbm, in_vmem),
        scratch=[pltpu.VMEM((4, 128, 1152), bf16), dma((4,))],
    )(place, done, terms, own_right, x_other, cot, held, far, third, last)
    back = lax.all_to_all(out.reshape(64, 8, 1152), ("zh", "zl", "yh", "yl"), 0, 0)
    right_sent = right_part.astype(bf16)
    right_sum = right_part + sum(swap(right_sent, "zh", 4, k).astype(f32) for k in (1, 2, 3))

    grad_inputs, grad_left, grad_singular = call(
        final_kernel,
        (shape((8, 8192), bf16), shape((16, 16), f32), shape((1, 16), f32)),
        [in_smem] + [in_vmem] * 4,
        2 << 20,
        2 << 20,
        out_specs=(in_hbm, in_hbm, in_hbm),
        scratch=[
            pltpu.VMEM((8, 8192), bf16),
            pltpu.VMEM((16, 16), f32),
            pltpu.VMEM((1, 16), f32),
            dma((4,)),
        ],
    )(place, back, scaled_back, left_factor.T, keep_mask.astype(f32).reshape(1, 16))
    grad_right = right_sum / n_dp
    return (grad_inputs, grad_left, grad_right, grad_singular.reshape(16))


def solution(mesh):
    fine = Mesh(mesh.devices.reshape(4, 4, 2, 2, 4, 2), ("zh", "x", "c", "zl", "yh", "yl"))
    dp = ("zh", "x", "c")
    tensor = ("zl", "yh", "yl")
    in_specs = (
        P(dp + tensor, None),
        P(dp, tensor),
        P(dp, tensor),
        P(),
        P(None, tensor),
        P(),
        P(),
    )
    out_specs = (P(dp + tensor, None), P(dp + tensor, None), P(None, tensor), P())
    return jax.shard_map(body, mesh=fine, in_specs=in_specs, out_specs=out_specs, check_vma=False)
```

```python
import jax
import jax.numpy as jnp
from jax import lax
from jax.experimental import pallas as pl
from jax.experimental.pallas import tpu as pltpu
from jax.sharding import Mesh
from jax.sharding import PartitionSpec as P

adapter_scale = 2.0
n_dp = 32
f32 = jnp.float32
bf16 = jnp.bfloat16
in_vmem = pl.BlockSpec(memory_space=pltpu.VMEM)
in_smem = pl.BlockSpec(memory_space=pltpu.SMEM)
anywhere = pl.BlockSpec(memory_space=pl.ANY)
in_hbm = pl.BlockSpec(memory_space=pltpu.HBM)
dma = pltpu.SemaphoreType.DMA


def dot_t(a, b):
    return lax.dot_general(a, b, (((1,), (1,)), ((), ())), preferred_element_type=f32)


def t_dot(a, b):
    return lax.dot_general(a, b, (((0,), (0,)), ((), ())), preferred_element_type=f32)


def swap(a, axis, count, mask):
    return lax.ppermute(a, axis, [(i, i ^ mask) for i in range(count)])


def call(kernel, out_shape, in_specs, flops, moved, out_specs=None, scratch=()):
    return pl.pallas_call(
        kernel,
        out_shape=out_shape,
        in_specs=in_specs,
        out_specs=out_specs or jax.tree.map(lambda _: in_vmem, out_shape),
        scratch_shapes=scratch,
        compiler_params=pltpu.CompilerParams(vmem_limit_bytes=32 << 20),
        cost_estimate=pl.CostEstimate(flops=flops, bytes_accessed=moved, transcendentals=0),
    )


def after(a, *others):
    return pl.pallas_call(
        lambda *refs: None,
        out_shape=jax.ShapeDtypeStruct(a.shape, a.dtype),
        in_specs=[in_vmem] * (1 + len(others)),
        out_specs=in_vmem,
        input_output_aliases={0: 0},
        compiler_params=pltpu.CompilerParams(vmem_limit_bytes=32 << 20),
    )(a, *others)


def rank_kernel(mixed_ref, right_ref, projected_ref, out_ref):
    out_ref[...] = jnp.zeros((16, 8, 128), f32)
    out_ref[:, :, 16:32] = jnp.broadcast_to(projected_ref[...][None], (16, 8, 16))
    out_ref[:, :, 0:16] = dot_t(mixed_ref[0:128, :], right_ref[...]).reshape(16, 8, 16)


def pick_kernel(mixed_ref, got_ref, out_ref):
    out_ref[0] = mixed_ref[0:128, :]
    out_ref[1] = got_ref[0:128, :]


def copy_kernel(in_ref, out_ref):
    out_ref[...] = in_ref[...]


def stack_kernel(first_ref, second_ref, after_ref, out_ref):
    out_ref[0] = first_ref[...]
    out_ref[1] = second_ref[...]


def rows_of(refs):
    return [jnp.concatenate([ref[half] for ref in refs], axis=0) for half in (0, 1)]


def pack_kernel(
    place_ref, singular_ref, keep_ref, sent_ref, rank_ref, cot_ref, weight_any, got_any, inputs_ref,
    x_any, back_ref, rest_ref, out_sems,
):
    rows = pl.ds(pl.multiple_of(place_ref[1] * 128, 128), 128)
    outs = [pltpu.make_async_copy(got_any.at[128:256], x_any.at[x, 128:256], out_sems.at[x]) for x in range(4)]
    outs += [pltpu.make_async_copy(weight_any.at[rows], x_any.at[x, 0:128], out_sems.at[8 + x]) for x in range(4)]
    for copy in outs:
        copy.start()
    lane = lax.broadcasted_iota(jnp.int32, (1, 128), 1)
    rank = rank_ref[...]
    coeff = jnp.zeros((1, 128), f32)
    for r in range(16):
        value = adapter_scale * singular_ref[r] * keep_ref[r].astype(f32)
        coeff = jnp.where((lane == r) | (lane == 16 + r), value, coeff)
    own = jnp.where(lane < 16, jnp.sum(rank, axis=0), 0.0)
    back = (own * coeff).astype(bf16)
    back_ref[...] = back
    fwd = (jnp.where((lane >= 16) & (lane < 32), rank, 0.0) * coeff).astype(bf16)
    right = t_dot(fwd.reshape(128, 128), cot_ref[0])[16:32]
    projected = pltpu.roll(sent_ref[0], 112, 1)
    singular = jnp.broadcast_to(jnp.sum(projected * own, axis=0, keepdims=True), (8, 128))
    high = singular.astype(bf16).astype(f32)
    back8 = back.astype(f32)
    none = jnp.zeros((8, 128), f32)
    small = jnp.concatenate(
        [
            jnp.concatenate([back8, pltpu.roll(back8, 16, 1), none, none], axis=1),
            jnp.concatenate([none, none, pltpu.roll(high, 32, 1), pltpu.roll(singular - high, 32, 1)], axis=1),
        ],
        axis=0,
    ).astype(bf16)
    inputs = inputs_ref[...].astype(f32)
    for x in range(4):
        parts = [inputs[:, (h * 4 + x) * 512 : (h * 4 + x + 1) * 512] for h in range(4)]
        rest_ref[x, 0:32, :] = jnp.concatenate(parts, axis=0).astype(bf16)
        rest_ref[x, 32:48, :] = small
        rest_ref[x, 48:64, :] = right.astype(bf16)
        outs.append(pltpu.make_async_copy(rest_ref.at[x], x_any.at[x, 256:320], out_sems.at[4 + x]))
        outs[-1].start()
    for copy in outs:
        copy.wait()


def products(parts, ref):
    total = dot_t(parts[0], ref[:, 0:128, :].reshape(512, 512))
    total += dot_t(parts[1], ref[:, 128:256, :].reshape(512, 512))
    return total.astype(bf16)


def adapter_terms(ref, core):
    tok, back, singular = [], [], jnp.zeros((1, 128), f32)
    for x in range(4):
        rows = ref[x, 256:288, :]
        tok.append(jnp.where(core == 0, rows[:, :256], rows[:, 256:]))
        small = ref[x, 288:304, :].astype(f32)
        back.extend([small[0:8, :256]] * 4)
        singular += small[8:9, 256:384] + small[8:9, 384:512]
    tok = jnp.concatenate(tok, axis=0)
    back = jnp.concatenate(back, axis=0)
    group = lax.rem(lax.broadcasted_iota(jnp.int32, (128, 1), 0), 32) // 8
    out = []
    for h in range(4):
        both = t_dot(tok, jnp.where(group == h, back, 0.0).astype(bf16))
        a = both[:, :128].reshape(16, 2, 8, 128)[:, 0]
        b = both[:, 128:].reshape(16, 2, 8, 128)[:, 1]
        out.append((a + b + singular).reshape(128, 128))
    right = sum(ref[x, 304:320, :].astype(f32) for x in range(4))
    return out, right


def own_kernel(
    place_ref, own_ref, cot_ref, first_ref, third_ref, last_ref, out_ref, terms_ref, right_ref
):
    parts = rows_of((cot_ref, first_ref, third_ref, last_ref))
    out_ref[...] = products(parts, own_ref).reshape(4, 128, 512)
    terms, right_ref[...] = adapter_terms(own_ref, place_ref[0])
    for h in range(4):
        terms_ref[h] = terms[h]


def other_kernel(
    place_ref, done_ref, terms_ref, own_right_ref, other_ref, cot_ref, first_ref, third_ref, last_ref,
    out_any, right_ref, out_ref, sems,
):
    z_high = place_ref[2]
    terms, right = adapter_terms(other_ref, place_ref[0])
    right_ref[...] = own_right_ref[...] + right
    for h in range(4):
        z = terms_ref[h] + terms[h]
        high = z.astype(bf16).astype(f32)
        out_ref[h, :, 1024:1152] = (high + pltpu.roll(z - high, 64, 1)).astype(bf16)
    copies = []
    for half, refs in enumerate(((cot_ref, first_ref), (third_ref, last_ref))):
        parts = rows_of(refs)
        total = products(parts, other_ref).reshape(2, 128, 512)
        for i in range(2):
            at = z_high ^ ((0, 1), (3, 2))[half][i]
            out_ref[at, :, 0:512] = done_ref[half * 2 + i]
            out_ref[at, :, 512:1024] = total[i]
            copies.append(pltpu.make_async_copy(out_ref.at[at], out_any.at[at], sems.at[half * 2 + i]))
            copies[-1].start()
    for copy in copies:
        copy.wait()


def final_kernel(
    place_ref, back_ref, scaled_ref, left_ref, keep_ref, inputs_any, grad_left_any, singular_any,
    inputs_ref, grad_left_ref, singular_ref, sems,
):
    core = place_ref[0]
    tail = jnp.sum(back_ref[:, :, 1024:].astype(f32), axis=0)
    tail = (tail + pltpu.roll(tail, 64, 1)) / n_dp
    grad_left_ref[0:8, :] = tail[:, 0:16]
    grad_left_ref[8:16, :] = pltpu.roll(tail, 112, 1)[:, 0:16]
    singular_ref[...] = adapter_scale * keep_ref[...] * pltpu.roll(tail, 96, 1)[0:1, 0:16]
    outs = [
        pltpu.make_async_copy(grad_left_ref, grad_left_any, sems.at[1]),
        pltpu.make_async_copy(singular_ref, singular_any, sems.at[2]),
    ]
    outs[0].start()
    outs[1].start()
    scaled = scaled_ref[:, 0:16]
    for h in range(4):
        for low in range(2):
            total = sum(back_ref[h * 16 + i * 2 + low, :, 0:1024].astype(f32) for i in range(8))
            own, other = total[:, :512], total[:, 512:]
            for c, part in enumerate((jnp.where(core == 0, own, other), jnp.where(core == 0, other, own))):
                for x in range(4):
                    at = h * 2048 + x * 512 + c * 256 + low * 128
                    term = jnp.dot(scaled, left_ref[:, at : at + 128], preferred_element_type=f32)
                    inputs_ref[:, at : at + 128] = (part[:, x * 128 : x * 128 + 128] + term).astype(bf16)
    outs.append(pltpu.make_async_copy(inputs_ref, inputs_any, sems.at[3]))
    outs[2].start()
    for copy in outs:
        copy.wait()


def body(inputs, cotangent, weight, left_factor, right_factor, singular, keep_mask):
    core = lax.axis_index("c")
    y_low = lax.axis_index("yl")
    z_high = lax.axis_index("zh")
    place = jnp.stack([core, y_low, z_high]).astype(jnp.int32)
    shape = jax.ShapeDtypeStruct

    given = jnp.where(y_low == 0, weight[128:], weight[:128])
    mixed = jnp.concatenate([cotangent, given], axis=0)
    got = swap(mixed, "yl", 2, 1)

    own_projected = jnp.dot(inputs, left_factor, preferred_element_type=f32)
    rank_out = call(rank_kernel, shape((16, 8, 128), f32), [in_vmem] * 3, 2 << 20, 1 << 20)(
        mixed, right_factor, own_projected
    )
    rank_in = lax.all_to_all(rank_out, ("zl", "yh", "yl"), 0, 0)

    cot = call(pick_kernel, shape((2, 128, 512), bf16), [in_vmem] * 2, 1, 1 << 18)(mixed, got)
    first, third = swap(cot, "zh", 4, 1), swap(cot, "zh", 4, 3)

    x_out, scaled_back = call(
        pack_kernel,
        (shape((4, 320, 512), bf16), shape((8, 128), bf16)),
        [in_smem] * 3 + [in_vmem] * 3 + [anywhere] * 2 + [in_vmem],
        30 << 30,
        3 << 20,
        out_specs=(in_hbm, in_vmem),
        scratch=[pltpu.VMEM((4, 64, 512), bf16), dma((12,))],
    )(place, singular, keep_mask, rank_out, rank_in, cot, weight, got, inputs)
    first = after(first, scaled_back)
    held = call(copy_kernel, shape((2, 128, 512), bf16), [in_vmem], 30 << 30, 1 << 18)(first)
    last = call(stack_kernel, shape((2, 128, 512), bf16), [in_vmem] * 2 + [anywhere], 30 << 30, 1 << 20)(
        swap(first[0], "zh", 4, 3), swap(third[1], "zh", 4, 1), held
    )
    x_in = lax.all_to_all(x_out, "x", 0, 0)
    x_other = swap(x_in, "c", 2, 1)

    done, terms, own_right = call(
        own_kernel,
        (shape((4, 128, 512), bf16), shape((4, 128, 128), f32), shape((16, 512), f32)),
        [in_smem] + [in_vmem] * 5,
        1 << 29,
        3 << 20,
    )(place, x_in, cot, held, third, last)
    out, right_part = call(
        other_kernel,
        (shape((4, 128, 1152), bf16), shape((16, 512), f32)),
        [in_smem] + [in_vmem] * 8,
        1 << 29,
        5 << 20,
        out_specs=(in_hbm, in_vmem),
        scratch=[pltpu.VMEM((4, 128, 1152), bf16), dma((4,))],
    )(place, done, terms, own_right, x_other, cot, held, third, last)
    back = lax.all_to_all(out.reshape(64, 8, 1152), ("zh", "zl", "yh", "yl"), 0, 0)
    right_sent = right_part.astype(bf16)
    right_sum = right_part + sum(swap(right_sent, "zh", 4, k).astype(f32) for k in (1, 2, 3))

    grad_inputs, grad_left, grad_singular = call(
        final_kernel,
        (shape((8, 8192), bf16), shape((16, 16), f32), shape((1, 16), f32)),
        [in_smem] + [in_vmem] * 4,
        2 << 20,
        2 << 20,
        out_specs=(in_hbm, in_hbm, in_hbm),
        scratch=[
            pltpu.VMEM((8, 8192), bf16),
            pltpu.VMEM((16, 16), f32),
            pltpu.VMEM((1, 16), f32),
            dma((4,)),
        ],
    )(place, back, scaled_back, left_factor.T, keep_mask.astype(f32).reshape(1, 16))
    grad_right = right_sum / n_dp
    return (grad_inputs, grad_left, grad_right, grad_singular.reshape(16))


def solution(mesh):
    fine = Mesh(mesh.devices.reshape(4, 4, 2, 2, 4, 2), ("zh", "x", "c", "zl", "yh", "yl"))
    dp = ("zh", "x", "c")
    tensor = ("zl", "yh", "yl")
    in_specs = (
        P(dp + tensor, None),
        P(dp, tensor),
        P(dp, tensor),
        P(),
        P(None, tensor),
        P(),
        P(),
    )
    out_specs = (P(dp + tensor, None), P(dp + tensor, None), P(None, tensor), P())
    return jax.shard_map(body, mesh=fine, in_specs=in_specs, out_specs=out_specs, check_vma=False)
```

```python
import jax
import jax.numpy as jnp
from jax import lax
from jax.experimental import pallas as pl
from jax.experimental.pallas import tpu as pltpu
from jax.sharding import Mesh
from jax.sharding import PartitionSpec as P

adapter_scale = 2.0
n_dp = 32
f32 = jnp.float32
bf16 = jnp.bfloat16
in_vmem = pl.BlockSpec(memory_space=pltpu.VMEM)
in_smem = pl.BlockSpec(memory_space=pltpu.SMEM)
anywhere = pl.BlockSpec(memory_space=pl.ANY)
in_hbm = pl.BlockSpec(memory_space=pltpu.HBM)
dma = pltpu.SemaphoreType.DMA


def dot_t(a, b):
    return lax.dot_general(a, b, (((1,), (1,)), ((), ())), preferred_element_type=f32)


def t_dot(a, b):
    return lax.dot_general(a, b, (((0,), (0,)), ((), ())), preferred_element_type=f32)


def swap(a, axis, count, mask):
    return lax.ppermute(a, axis, [(i, i ^ mask) for i in range(count)])


def call(kernel, out_shape, in_specs, flops, moved, out_specs=None, scratch=()):
    return pl.pallas_call(
        kernel,
        out_shape=out_shape,
        in_specs=in_specs,
        out_specs=out_specs or jax.tree.map(lambda _: in_vmem, out_shape),
        scratch_shapes=scratch,
        compiler_params=pltpu.CompilerParams(vmem_limit_bytes=32 << 20),
        cost_estimate=pl.CostEstimate(flops=flops, bytes_accessed=moved, transcendentals=0),
    )


def after(a, *others):
    return pl.pallas_call(
        lambda *refs: None,
        out_shape=jax.ShapeDtypeStruct(a.shape, a.dtype),
        in_specs=[in_vmem] * (1 + len(others)),
        out_specs=in_vmem,
        input_output_aliases={0: 0},
        compiler_params=pltpu.CompilerParams(vmem_limit_bytes=32 << 20),
    )(a, *others)


def rank_kernel(mixed_ref, right_ref, projected_ref, out_ref):
    out_ref[...] = jnp.zeros((16, 8, 128), f32)
    out_ref[:, :, 16:32] = jnp.broadcast_to(projected_ref[...][None], (16, 8, 16))
    out_ref[:, :, 0:16] = dot_t(mixed_ref[0:128, :], right_ref[...]).reshape(16, 8, 16)


def pick_kernel(mixed_ref, got_ref, out_ref, own_ref):
    own_ref[...] = mixed_ref[0:128, :]
    out_ref[0] = mixed_ref[0:128, :]
    out_ref[1] = got_ref[0:128, :]


def copy_kernel(in_ref, out_ref):
    out_ref[...] = in_ref[...]


def stack_kernel(first_ref, second_ref, after_ref, out_ref):
    out_ref[0] = first_ref[...]
    out_ref[1] = second_ref[...]


def rows_of(*pairs):
    return [jnp.concatenate([pair[half] for pair in pairs], axis=0) for half in (0, 1)]


def pack_kernel(
    place_ref, singular_ref, keep_ref, sent_ref, rank_ref, cot_ref, weight_any, got_any, inputs_ref,
    x_any, back_ref, rest_ref, out_sems,
):
    rows = pl.ds(pl.multiple_of(place_ref[1] * 128, 128), 128)
    outs = [pltpu.make_async_copy(got_any.at[128:256], x_any.at[x, 128:256], out_sems.at[x]) for x in range(4)]
    outs += [pltpu.make_async_copy(weight_any.at[rows], x_any.at[x, 0:128], out_sems.at[8 + x]) for x in range(4)]
    for copy in outs:
        copy.start()
    lane = lax.broadcasted_iota(jnp.int32, (1, 128), 1)
    rank = rank_ref[...]
    coeff = jnp.zeros((1, 128), f32)
    for r in range(16):
        value = adapter_scale * singular_ref[r] * keep_ref[r].astype(f32)
        coeff = jnp.where((lane == r) | (lane == 16 + r), value, coeff)
    own = jnp.where(lane < 16, jnp.sum(rank, axis=0), 0.0)
    back = (own * coeff).astype(bf16)
    back_ref[...] = back
    fwd = (jnp.where((lane >= 16) & (lane < 32), rank, 0.0) * coeff).astype(bf16)
    right = t_dot(fwd.reshape(128, 128), cot_ref[0])[16:32]
    projected = pltpu.roll(sent_ref[0], 112, 1)
    singular = jnp.broadcast_to(jnp.sum(projected * own, axis=0, keepdims=True), (8, 128))
    high = singular.astype(bf16).astype(f32)
    back8 = back.astype(f32)
    none = jnp.zeros((8, 128), f32)
    small = jnp.concatenate(
        [
            jnp.concatenate([back8, pltpu.roll(back8, 16, 1), none, none], axis=1),
            jnp.concatenate([none, none, pltpu.roll(high, 32, 1), pltpu.roll(singular - high, 32, 1)], axis=1),
        ],
        axis=0,
    ).astype(bf16)
    inputs = inputs_ref[...].astype(f32)
    for x in range(4):
        parts = [inputs[:, (h * 4 + x) * 512 : (h * 4 + x + 1) * 512] for h in range(4)]
        rest_ref[x, 0:32, :] = jnp.concatenate(parts, axis=0).astype(bf16)
        rest_ref[x, 32:48, :] = small
        rest_ref[x, 48:64, :] = right.astype(bf16)
        outs.append(pltpu.make_async_copy(rest_ref.at[x], x_any.at[x, 256:320], out_sems.at[4 + x]))
        outs[-1].start()
    for copy in outs:
        copy.wait()


def products(parts, ref):
    total = dot_t(parts[0], ref[:, 0:128, :].reshape(512, 512))
    total += dot_t(parts[1], ref[:, 128:256, :].reshape(512, 512))
    return total.astype(bf16)


def adapter_terms(ref, core):
    tok, back, singular = [], [], jnp.zeros((1, 128), f32)
    for x in range(4):
        rows = ref[x, 256:288, :]
        tok.append(jnp.where(core == 0, rows[:, :256], rows[:, 256:]))
        small = ref[x, 288:304, :].astype(f32)
        back.extend([small[0:8, :256]] * 4)
        singular += small[8:9, 256:384] + small[8:9, 384:512]
    tok = jnp.concatenate(tok, axis=0)
    back = jnp.concatenate(back, axis=0)
    group = lax.rem(lax.broadcasted_iota(jnp.int32, (128, 1), 0), 32) // 8
    out = []
    for h in range(4):
        both = t_dot(tok, jnp.where(group == h, back, 0.0).astype(bf16))
        a = both[:, :128].reshape(16, 2, 8, 128)[:, 0]
        b = both[:, 128:].reshape(16, 2, 8, 128)[:, 1]
        out.append((a + b + singular).reshape(128, 128))
    right = sum(ref[x, 304:320, :].astype(f32) for x in range(4))
    return out, right


def own_kernel(
    place_ref, own_ref, cot_ref, first_ref, far_ref, third_ref, last_ref, out_ref, terms_ref, right_ref
):
    parts = rows_of(cot_ref, (first_ref[...], far_ref[...]), third_ref, last_ref)
    out_ref[...] = products(parts, own_ref).reshape(4, 128, 512)
    terms, right_ref[...] = adapter_terms(own_ref, place_ref[0])
    for h in range(4):
        terms_ref[h] = terms[h]


def other_kernel(
    place_ref, done_ref, terms_ref, own_right_ref, other_ref, cot_ref, first_ref, far_ref, third_ref, last_ref,
    out_any, right_ref, out_ref, sems,
):
    z_high = place_ref[2]
    terms, right = adapter_terms(other_ref, place_ref[0])
    right_ref[...] = own_right_ref[...] + right
    for h in range(4):
        z = terms_ref[h] + terms[h]
        high = z.astype(bf16).astype(f32)
        out_ref[h, :, 1024:1152] = (high + pltpu.roll(z - high, 64, 1)).astype(bf16)
    copies = []
    first_half = rows_of(cot_ref, (first_ref[...], far_ref[...]))
    for half, parts in enumerate((first_half, rows_of(third_ref, last_ref))):
        total = products(parts, other_ref).reshape(2, 128, 512)
        for i in range(2):
            at = z_high ^ ((0, 1), (3, 2))[half][i]
            out_ref[at, :, 0:512] = done_ref[half * 2 + i]
            out_ref[at, :, 512:1024] = total[i]
            copies.append(pltpu.make_async_copy(out_ref.at[at], out_any.at[at], sems.at[half * 2 + i]))
            copies[-1].start()
    for copy in copies:
        copy.wait()


def final_kernel(
    place_ref, back_ref, scaled_ref, left_ref, keep_ref, inputs_any, grad_left_any, singular_any,
    inputs_ref, grad_left_ref, singular_ref, sems,
):
    core = place_ref[0]
    tail = jnp.sum(back_ref[:, :, 1024:].astype(f32), axis=0)
    tail = (tail + pltpu.roll(tail, 64, 1)) / n_dp
    grad_left_ref[0:8, :] = tail[:, 0:16]
    grad_left_ref[8:16, :] = pltpu.roll(tail, 112, 1)[:, 0:16]
    singular_ref[...] = adapter_scale * keep_ref[...] * pltpu.roll(tail, 96, 1)[0:1, 0:16]
    outs = [
        pltpu.make_async_copy(grad_left_ref, grad_left_any, sems.at[1]),
        pltpu.make_async_copy(singular_ref, singular_any, sems.at[2]),
    ]
    outs[0].start()
    outs[1].start()
    scaled = scaled_ref[:, 0:16]
    for h in range(4):
        for low in range(2):
            total = sum(back_ref[h * 16 + i * 2 + low, :, 0:1024].astype(f32) for i in range(8))
            own, other = total[:, :512], total[:, 512:]
            for c, part in enumerate((jnp.where(core == 0, own, other), jnp.where(core == 0, other, own))):
                for x in range(4):
                    at = h * 2048 + x * 512 + c * 256 + low * 128
                    term = jnp.dot(scaled, left_ref[:, at : at + 128], preferred_element_type=f32)
                    inputs_ref[:, at : at + 128] = (part[:, x * 128 : x * 128 + 128] + term).astype(bf16)
    outs.append(pltpu.make_async_copy(inputs_ref, inputs_any, sems.at[3]))
    outs[2].start()
    for copy in outs:
        copy.wait()


def body(inputs, cotangent, weight, left_factor, right_factor, singular, keep_mask):
    core = lax.axis_index("c")
    y_low = lax.axis_index("yl")
    z_high = lax.axis_index("zh")
    place = jnp.stack([core, y_low, z_high]).astype(jnp.int32)
    shape = jax.ShapeDtypeStruct

    given = jnp.where(y_low == 0, weight[128:], weight[:128])
    mixed = jnp.concatenate([cotangent, given], axis=0)
    got = swap(mixed, "yl", 2, 1)

    own_projected = jnp.dot(inputs, left_factor, preferred_element_type=f32)
    rank_out = call(rank_kernel, shape((16, 8, 128), f32), [in_vmem] * 3, 2 << 20, 1 << 20)(
        mixed, right_factor, own_projected
    )
    rank_in = lax.all_to_all(rank_out, ("zl", "yh", "yl"), 0, 0)

    cot, own = call(
        pick_kernel, (shape((2, 128, 512), bf16), shape((128, 512), bf16)), [in_vmem] * 2, 1, 1 << 18
    )(mixed, got)
    first, third = swap(own, "zh", 4, 1), swap(cot, "zh", 4, 3)

    x_out, scaled_back = call(
        pack_kernel,
        (shape((4, 320, 512), bf16), shape((8, 128), bf16)),
        [in_smem] * 3 + [in_vmem] * 3 + [anywhere] * 2 + [in_vmem],
        30 << 30,
        3 << 20,
        out_specs=(in_hbm, in_vmem),
        scratch=[pltpu.VMEM((4, 64, 512), bf16), dma((12,))],
    )(place, singular, keep_mask, rank_out, rank_in, cot, weight, got, inputs)
    first = after(first, scaled_back)
    held = call(copy_kernel, shape((128, 512), bf16), [in_vmem], 30 << 30, 1 << 18)(first)
    far = call(copy_kernel, shape((128, 512), bf16), [in_vmem], 30 << 30, 1 << 18)(swap(held, "yl", 2, 1))
    last = call(stack_kernel, shape((2, 128, 512), bf16), [in_vmem] * 2 + [anywhere], 30 << 30, 1 << 20)(
        swap(first, "zh", 4, 3), swap(third[1], "zh", 4, 1), held
    )
    x_in = lax.all_to_all(x_out, "x", 0, 0)
    x_other = swap(x_in, "c", 2, 1)

    done, terms, own_right = call(
        own_kernel,
        (shape((4, 128, 512), bf16), shape((4, 128, 128), f32), shape((16, 512), f32)),
        [in_smem] + [in_vmem] * 6,
        1 << 29,
        3 << 20,
    )(place, x_in, cot, held, far, third, last)
    out, right_part = call(
        other_kernel,
        (shape((4, 128, 1152), bf16), shape((16, 512), f32)),
        [in_smem] + [in_vmem] * 9,
        1 << 29,
        5 << 20,
        out_specs=(in_hbm, in_vmem),
        scratch=[pltpu.VMEM((4, 128, 1152), bf16), dma((4,))],
    )(place, done, terms, own_right, x_other, cot, held, far, third, last)
    back = lax.all_to_all(out.reshape(64, 8, 1152), ("zh", "zl", "yh", "yl"), 0, 0)
    right_sent = right_part.astype(bf16)
    right_sum = right_part + sum(swap(right_sent, "zh", 4, k).astype(f32) for k in (1, 2, 3))

    grad_inputs, grad_left, grad_singular = call(
        final_kernel,
        (shape((8, 8192), bf16), shape((16, 16), f32), shape((1, 16), f32)),
        [in_smem] + [in_vmem] * 4,
        2 << 20,
        2 << 20,
        out_specs=(in_hbm, in_hbm, in_hbm),
        scratch=[
            pltpu.VMEM((8, 8192), bf16),
            pltpu.VMEM((16, 16), f32),
            pltpu.VMEM((1, 16), f32),
            dma((4,)),
        ],
    )(place, back, scaled_back, left_factor.T, keep_mask.astype(f32).reshape(1, 16))
    grad_right = right_sum / n_dp
    return (grad_inputs, grad_left, grad_right, grad_singular.reshape(16))


def solution(mesh):
    fine = Mesh(mesh.devices.reshape(4, 4, 2, 2, 4, 2), ("zh", "x", "c", "zl", "yh", "yl"))
    dp = ("zh", "x", "c")
    tensor = ("zl", "yh", "yl")
    in_specs = (
        P(dp + tensor, None),
        P(dp, tensor),
        P(dp, tensor),
        P(),
        P(None, tensor),
        P(),
        P(),
    )
    out_specs = (P(dp + tensor, None), P(dp + tensor, None), P(None, tensor), P())
    return jax.shard_map(body, mesh=fine, in_specs=in_specs, out_specs=out_specs, check_vma=False)
```
